32 devices in a mesh: seq: 8 (over z, x), fsdp: 4 (over y, core).
Axes of the slice: x: 2, y: 2, z: 4, core: 2. Of those that a mesh axis runs over, the one named last changes fastest.
Arguments:
- tokens: bfloat16 [3, 4, 2048, 1024], P(None, 'fsdp', 'seq'), may hold values from -6 to 6
- memory: bfloat16 [3, 4, 256, 1024], P(None, 'fsdp', 'seq'), may hold values from -6 to 6
- cotangent: bfloat16 [3, 4, 2048, 1024], P(None, 'fsdp', 'seq'), may hold values from -6 to 6
- tile_segment: int32 [3, 4, 16], P(None, 'fsdp'), may hold values from 0 to 12, as said below
- parents: int32 [3, 4, 13], P(None, 'fsdp'), may hold values from 0 to 11, as said below
- memory_lengths: int32 [3, 4], P(None, 'fsdp'), may hold values from 64 to 256, as said below
- self_qkv: bfloat16 [1024, 3072], P(('seq', 'fsdp')), may hold values from -0.1875 to 0.1875
- self_out: bfloat16 [1024, 1024], P(('seq', 'fsdp')), may hold values from -3 to 3
- cross_q: bfloat16 [1024, 1024], P(('seq', 'fsdp')), may hold values from -0.1875 to 0.1875
- cross_kv: bfloat16 [1024, 2048], P(('seq', 'fsdp')), may hold values from -0.1875 to 0.1875
- cross_out: bfloat16 [1024, 1024], P(('seq', 'fsdp')), may hold values from -3 to 3
- ffn_in: bfloat16 [1024, 4096], P(('seq', 'fsdp')), may hold values from -0.1875 to 0.1875
- ffn_out: bfloat16 [4096, 1024], P(('seq', 'fsdp')), may hold values from -0.1875 to 0.1875
- norm_gain: bfloat16 [3, 1024], P(None, ('seq', 'fsdp')), may hold values from 0.5 to 1.5
- norm_bias: bfloat16 [3, 1024], P(None, ('seq', 'fsdp')), may hold values from -1.75 to 1.75
Outputs:
- output: bfloat16 [3, 4, 2048, 1024], P(None, 'fsdp', 'seq')
- grad_tokens: bfloat16 [3, 4, 2048, 1024], P(None, 'fsdp', 'seq')
- grad_memory: bfloat16 [3, 4, 256, 1024], P(None, 'fsdp', 'seq')
- grad_self_qkv: float32 [1024, 3072], P(('seq', 'fsdp'))
- grad_self_out: float32 [1024, 1024], P(('seq', 'fsdp'))
- grad_cross_q: float32 [1024, 1024], P(('seq', 'fsdp'))
- grad_cross_kv: float32 [1024, 2048], P(('seq', 'fsdp'))
- grad_cross_out: float32 [1024, 1024], P(('seq', 'fsdp'))
- grad_ffn_in: float32 [1024, 4096], P(('seq', 'fsdp'))
- grad_ffn_out: float32 [4096, 1024], P(('seq', 'fsdp'))
- grad_norm_gain: float32 [3, 1024], P(None, ('seq', 'fsdp'))
- grad_norm_bias: float32 [3, 1024], P(None, ('seq', 'fsdp'))
The draws below stay inside these ranges and needn't reach their ends.
Inputs may be any that keep to these rules, and one draw needn't show every extreme that they name: `tile_segment`: 0 on the first 4 tiles (the trunk), 1 on tile 16 // 4, then never falling and rising by at most one from tile to tile; in some sequence every later tile starts a new segment. `parents`: the parent of segment s >= 1 is an earlier segment; the parent of segment 0 is 0. `memory_lengths`: some sequence of every draw has all 256 rows valid.
All inputs are finite; a program needn't handle non-finite values.
Results may differ from the reference program's by a relative error of at most 0.02.
Values may be sent and summed in bfloat16 or wider, within the bound.
A program may use at most 200 MiB of HBM per device.

```python
import jax
import jax.numpy as jnp
from jax import lax

D = 1024
FF = 4096
H = 16
HD = 64
LENGTH = 2048
TILE = 128
MEM = 256
MICRO = 3
TILES = 16
SEGS = 13
GROUPS = 4
N_FSDP = 4


def draw_tile_segment(key, part):
    trunk_tiles = TILES // 4
    starts = (jax.random.randint(key, (MICRO, GROUPS, TILES), 0, 3) == 0).astype(jnp.int32)
    chosen = jax.random.randint(jax.random.fold_in(key, 7), (), 0, MICRO * GROUPS)
    full_row = (jnp.arange(MICRO * GROUPS, dtype=jnp.int32).reshape(MICRO, GROUPS) == chosen)[..., None]
    tile_place = jnp.arange(TILES, dtype=jnp.int32)
    starts = jnp.where(full_row, 1, starts)
    starts = jnp.where(tile_place == trunk_tiles, 1, starts)
    starts = jnp.where(tile_place < trunk_tiles, 0, starts)
    return jnp.cumsum(starts, axis=-1).astype(jnp.int32)


def draw_parents(key, part):
    segment_ids = jnp.arange(SEGS, dtype=jnp.int32)
    limits = jnp.minimum(jnp.maximum(segment_ids, 1), 3)
    backstep = jax.random.randint(key, (MICRO, GROUPS, SEGS), 0, limits)
    chosen = jax.random.randint(jax.random.fold_in(key, 5), (), 0, MICRO * GROUPS)
    places = jnp.arange(MICRO * GROUPS, dtype=jnp.int32).reshape(MICRO, GROUPS)
    forced = jnp.logical_and((places == chosen)[..., None], (segment_ids == SEGS - 1)[None, None, :])
    backstep = jnp.where(forced, 0, backstep)
    return jnp.maximum(segment_ids - 1 - backstep, 0).astype(jnp.int32)


def draw_memory_lengths(key, part):
    drawn = jax.random.randint(key, (MICRO, GROUPS), MEM // 4, MEM + 1)
    chosen = jax.random.randint(jax.random.fold_in(key, 11), (), 0, MICRO * GROUPS)
    places = jnp.arange(MICRO * GROUPS, dtype=jnp.int32).reshape(MICRO, GROUPS)
    return jnp.where(places == chosen, MEM, drawn).astype(jnp.int32)


def block_levels(stream_key, extent, shards, least, top_value):
    def one(axis_at, blocks):
        heights = jax.random.uniform(jax.random.fold_in(jax.random.fold_in(stream_key, 6), axis_at), (blocks,), jnp.float32, least / len(shards), top_value / len(shards))
        return jnp.repeat(jnp.exp(heights), extent[axis_at] // blocks).reshape((-1,) + (1,) * (len(extent) - axis_at - 1))

    level = one(*shards[0])
    for cut in shards[1:]:
        level = level * one(*cut)
    return level


def scatter_about(rng, extent, deviation, limit, shards=(), kind=jnp.bfloat16):
    values = deviation * jax.random.normal(rng, extent, jnp.float32)
    if shards:
        values = values * block_levels(rng, extent, shards, -0.22, 0.18)
    return jnp.clip(values, -limit, limit).astype(kind)


def setup_inputs(seed: int = 0) -> dict:
    keys = jax.random.split(jax.random.key(seed), 16)
    return {
        "tokens": scatter_about(keys[0], (MICRO, GROUPS, LENGTH, D), 1.0, 6.0, ((1, 4), (2, 8))),
        "memory": scatter_about(keys[1], (MICRO, GROUPS, MEM, D), 1.0, 6.0, ((1, 4), (2, 8))),
        "cotangent": scatter_about(keys[2], (MICRO, GROUPS, LENGTH, D), 1.0, 6.0, ((1, 4), (2, 8))),
        "tile_segment": draw_tile_segment(jax.random.fold_in(keys[15], 71), 0),
        "parents": draw_parents(jax.random.fold_in(keys[15], 71), 0),
        "memory_lengths": draw_memory_lengths(jax.random.fold_in(keys[15], 71), 0),
        "self_qkv": scatter_about(keys[6], (D, 3 * D), D ** -0.5, 0.1875, ((0, 32),)),
        "self_out": scatter_about(keys[7], (D, D), (D // 256) ** -0.5, 3.0, ((0, 32),)),
        "cross_q": scatter_about(keys[8], (D, D), D ** -0.5, 0.1875, ((0, 32),)),
        "cross_kv": scatter_about(keys[9], (D, 2 * D), D ** -0.5, 0.1875, ((0, 32),)),
        "cross_out": scatter_about(keys[10], (D, D), (D // 256) ** -0.5, 3.0, ((0, 32),)),
        "ffn_in": scatter_about(keys[11], (D, FF), D ** -0.5, 0.1875, ((0, 32),)),
        "ffn_out": scatter_about(keys[12], (FF, D), (FF // 4) ** -0.5, 0.1875, ((0, 32),)),
        "norm_gain": jnp.clip(1.0 + 0.1 * jax.random.normal(keys[13], (3, D), jnp.float32), 0.5, 1.5).astype(jnp.bfloat16),
        "norm_bias": scatter_about(keys[14], (3, D), 0.3, 1.75, ((1, 32),)),
    }


scale_factor = 0.125
residual_weight = 36.0 ** 0.25
norm_epsilon = 1e-05
masked_score = -1e+30

@jax.custom_vjp
def low(v):
    return lax.optimization_barrier(v.astype(jnp.bfloat16)).astype(jnp.float32)

@jax.custom_vjp
def low_back(v):
    return v

def low_keep(v):
    return (low(v), None)

def low_pass(kept, grad):
    return (grad,)

def back_keep(v):
    return (v, None)

def back_low(kept, grad):
    return (low(grad),)
low.defvjp(low_keep, low_pass)
low_back.defvjp(back_keep, back_low)

def matmul(left_side, right_side):
    return jnp.dot(left_side, right_side, precision=lax.Precision.HIGHEST)

def layer_norm(incoming, gain_row, bias_row):
    row_mean = lax.optimization_barrier(jnp.mean(incoming, -1, keepdims=True))
    centred = incoming - row_mean
    variance = lax.optimization_barrier(jnp.mean(centred * centred, -1, keepdims=True))
    return centred * lax.rsqrt(variance + norm_epsilon) * gain_row + bias_row

def ancestors(parent_ids):
    segment_ids = jnp.arange(parent_ids.shape[0], dtype=jnp.int32)
    start_table = (segment_ids[:, None] == segment_ids[None, :]).astype(jnp.float32)

    def advance(position, loop_state):
        current, ancestry = loop_state
        current = parent_ids[current]
        found = (current[:, None] == segment_ids[None, :]).astype(jnp.float32)
        return (current, jnp.maximum(ancestry, found))
    final_state = lax.fori_loop(0, parent_ids.shape[0], advance, (segment_ids, start_table))
    return final_state[1]

def attend(queries, key_rows, value_rows, mask_maker):
    query_count = queries.shape[0]
    block_rows = min(512, query_count)
    block_count = query_count // block_rows
    query_heads = queries.reshape(block_count, block_rows, H, HD)
    key_heads = key_rows.reshape(key_rows.shape[0], H, HD)
    value_heads = value_rows.reshape(value_rows.shape[0], H, HD)
    starts = jnp.arange(block_count, dtype=jnp.int32) * block_rows

    @jax.checkpoint
    def one_block(block_items):
        query_block, start = block_items
        scores = jnp.einsum('qhd,khd->hqk', query_block, key_heads, precision=lax.Precision.HIGHEST) * scale_factor
        scores = low_back(scores)
        allowed = mask_maker(start, block_rows)[None]
        scores = jnp.where(allowed, scores, masked_score)
        row_max = lax.optimization_barrier(jnp.max(scores, -1, keepdims=True))
        exp_scores = jnp.where(allowed, jnp.exp(scores - row_max), 0.0)
        soft_max = low(exp_scores / lax.optimization_barrier(jnp.sum(exp_scores, -1, keepdims=True)))
        mixed = jnp.einsum('hqk,khd->qhd', soft_max, value_heads, precision=lax.Precision.HIGHEST)
        return mixed.reshape(block_rows, H * HD)
    joined = lax.map(one_block, (query_heads, starts)).reshape(query_count, H * HD)
    return low_back(low(joined))

def layer(params, token_rows, memory_rows, segment_tokens, ancestry, memory_length):
    joint_weight, self_output, cross_weight, pair_weight, cross_output, upward_weight, down_weight, gain_rows, bias_rows = params
    width = token_rows.shape[1]
    key_count = segment_tokens.shape[0]

    def self_mask(start, block_rows):
        query_segment = lax.dynamic_slice_in_dim(segment_tokens, start, block_rows)
        related = ancestry[query_segment][:, segment_tokens] > 0.5
        query_place = start + jnp.arange(block_rows, dtype=jnp.int32)
        key_place = jnp.arange(key_count, dtype=jnp.int32)
        return jnp.logical_and(related, key_place[None, :] <= query_place[:, None])

    def memory_mask(start, block_rows):
        valid = jnp.arange(memory_rows.shape[0], dtype=jnp.int32) < memory_length
        return jnp.broadcast_to(valid[None, :], (block_rows, memory_rows.shape[0]))
    projected = low_back(low(matmul(token_rows, joint_weight)))
    attended = attend(projected[:, :width], projected[:, width:2 * width], projected[:, 2 * width:], self_mask)
    mixed_first = residual_weight * token_rows + low_back(matmul(attended, self_output))
    hidden_first = layer_norm(mixed_first, gain_rows[0], bias_rows[0])
    cross_query = low_back(low(matmul(low(hidden_first), cross_weight)))
    memory_pairs = low_back(low(matmul(memory_rows, pair_weight)))
    cross_attended = attend(cross_query, memory_pairs[:, :width], memory_pairs[:, width:], memory_mask)
    mixed_second = residual_weight * hidden_first + low_back(matmul(cross_attended, cross_output))
    hidden_second = layer_norm(mixed_second, gain_rows[1], bias_rows[1])
    pre_active = low_back(matmul(low(hidden_second), upward_weight))
    active = low(jax.nn.gelu(pre_active, approximate=True))
    mixed_third = residual_weight * hidden_second + low_back(matmul(active, down_weight))
    return layer_norm(mixed_third, gain_rows[2], bias_rows[2])

def reference(tokens, memory, cotangent, tile_segment, parents, memory_lengths, self_qkv, self_out, cross_q, cross_kv, cross_out, ffn_in, ffn_out, norm_gain, norm_bias):
    seq_total = MICRO * N_FSDP
    weights = tuple((item.astype(jnp.float32) for item in (self_qkv, self_out, cross_q, cross_kv, cross_out, ffn_in, ffn_out, norm_gain, norm_bias)))

    def flatten(array):
        return array.reshape((seq_total,) + array.shape[2:])

    def one_sequence(totals, sequence_item):
        token_rows, memory_rows, upstream, tile_row, parent_row, memory_length = sequence_item
        segment_tokens = jnp.repeat(tile_row, TILE)
        ancestry = ancestors(parent_row)

        def forward(params, token_float, memory_float):
            return layer(params, token_float, memory_float, segment_tokens, ancestry, memory_length)
        result, back_fn = jax.vjp(forward, weights, token_rows.astype(jnp.float32), memory_rows.astype(jnp.float32))
        grad_params, grad_token_rows, grad_memory_rows = back_fn(upstream.astype(jnp.float32))
        totals = jax.tree.map(lambda total, extra: total + extra, totals, grad_params)
        return (totals, (result.astype(jnp.bfloat16), grad_token_rows.astype(jnp.bfloat16), grad_memory_rows.astype(jnp.bfloat16)))
    initial = jax.tree.map(jnp.zeros_like, weights)
    totals, results = lax.scan(one_sequence, initial, (flatten(tokens), flatten(memory), flatten(cotangent), flatten(tile_segment), flatten(parents), memory_lengths.reshape(seq_total)))
    output = results[0].reshape(tokens.shape)
    grad_tokens = results[1].reshape(tokens.shape)
    grad_memory = results[2].reshape(memory.shape)
    return (output, grad_tokens, grad_memory, totals[0], totals[1], totals[2], totals[3], totals[4], totals[5], totals[6], totals[7], totals[8])
```

```python
import functools

import jax
import jax.numpy as jnp
from jax import lax
from jax.experimental import pallas as pl
from jax.experimental.pallas import tpu as pltpu
from jax.sharding import PartitionSpec as P

H = 16
HD = 64
TILE = 128
BLOCK = 256

scale_factor = 0.125
residual_weight = 36.0**0.25
norm_epsilon = 1e-05
masked_score = -1e30
ALL = ("seq", "fsdp")
f32 = jnp.float32
bf16 = jnp.bfloat16


def dot_nn(a, b):
    return lax.dot_general(a, b, (((1,), (0,)), ((), ())), preferred_element_type=f32)


def dot_nt(a, b):
    return lax.dot_general(a, b, (((1,), (1,)), ((), ())), preferred_element_type=f32)


def dot_tn(a, b):
    return lax.dot_general(a, b, (((0,), (0,)), ((), ())), preferred_element_type=f32)


def norm_stats(incoming):
    row_mean = jnp.mean(incoming, -1, keepdims=True)
    centred = incoming - row_mean
    variance = jnp.mean(centred * centred, -1, keepdims=True)
    return centred, lax.rsqrt(variance + norm_epsilon)


def layer_norm(incoming, gain_row, bias_row):
    centred, inverse = norm_stats(incoming)
    return centred * inverse * gain_row + bias_row


def layer_norm_back(incoming, gain_row, upstream):
    centred, inverse = norm_stats(incoming)
    normal = centred * inverse
    grad_bias = jnp.sum(upstream, 0)
    grad_gain = jnp.sum(upstream * normal, 0)
    scaled = upstream * gain_row
    grad = inverse * (
        scaled
        - jnp.mean(scaled, -1, keepdims=True)
        - normal * jnp.mean(scaled * normal, -1, keepdims=True)
    )
    return grad, grad_gain, grad_bias


def ancestors(parent_ids):
    segment_ids = jnp.arange(parent_ids.shape[0], dtype=jnp.int32)
    hop = (parent_ids[:, None] == segment_ids[None, :]).astype(f32)
    reach = jnp.maximum(hop, (segment_ids[:, None] == segment_ids[None, :]).astype(f32))
    steps = 1
    while steps < parent_ids.shape[0]:
        reach = jnp.minimum(jnp.dot(reach, reach, precision=lax.Precision.HIGHEST), 1.0)
        steps *= 2
    return reach


def tree_bias(tile_segments, parent_ids, block):
    tiles = tile_segments.shape[0]
    onehot = (
        tile_segments[:, None] == jnp.arange(parent_ids.shape[0], dtype=jnp.int32)[None, :]
    ).astype(f32)
    high = lax.Precision.HIGHEST
    related = jnp.dot(
        jnp.dot(onehot, ancestors(parent_ids), precision=high), onehot.T, precision=high
    )
    bias = jnp.where(related > 0.5, 0.0, masked_score)
    per = block // TILE
    blocks = tiles // per
    bias = bias.reshape(blocks, per, blocks, per).transpose(2, 0, 3, 1)
    return jnp.repeat(bias, TILE, axis=3)


def head_masks(shape, heads):
    lane = lax.broadcasted_iota(jnp.int32, shape, 1)
    return [(lane >= h * HD) & (lane < (h + 1) * HD) for h in range(heads)]


def keep_head(value, mask, heads):
    return value if heads == 1 else jnp.where(mask, value, jnp.zeros_like(value))


def self_forward_kernel(heads, block, qkv_ref, bias_ref, out_ref, lse_ref, queries, values_t):
    length, width = qkv_ref.shape[2], qkv_ref.shape[3]
    blocks = length // block
    per = block // TILE
    masks = head_masks((block, width), heads)

    def prepare(i, carry):
        rows = pl.ds(pl.multiple_of(i * block, block), block)
        q = qkv_ref[0, 0, rows, :].astype(f32) * scale_factor
        for h in range(heads):
            queries[h, rows, :] = keep_head(q, masks[h], heads).astype(bf16)
        values_t[i] = jnp.transpose(qkv_ref[0, 2, rows, :].astype(f32)).astype(bf16)
        return carry

    lax.fori_loop(0, blocks, prepare, 0)
    key_place = lax.broadcasted_iota(jnp.int32, (block, block), 0)
    query_place = lax.broadcasted_iota(jnp.int32, (block, block), 1)
    causal = key_place <= query_place

    def scores_of(i, j, h):
        rows = pl.ds(pl.multiple_of(i * block, block), block)
        keys = qkv_ref[0, 1, pl.ds(pl.multiple_of(j * block, block), block), :]
        raw = dot_nt(keys, queries[h, rows, :])
        bias = bias_ref[0, j, i]
        return (raw.reshape(per, TILE, block) + bias[:, None, :]).reshape(block, block)

    def query_block(i, carry):
        state = []
        for h in range(heads):
            s = jnp.where(causal, scores_of(i, i, h), masked_score)
            m = jnp.max(s, 0, keepdims=True)
            p = jnp.exp(s - m)
            total = jnp.sum(p, 0, keepdims=True)
            acc = dot_nn(values_t[i][h * HD : (h + 1) * HD], p.astype(bf16))
            state += [m, total, acc]

        def key_block(j, state):
            fresh = []
            for h in range(heads):
                m, total, acc = state[3 * h : 3 * h + 3]
                s = scores_of(i, j, h)
                m_new = jnp.maximum(m, jnp.max(s, 0, keepdims=True))
                shrink = jnp.exp(m - m_new)
                p = jnp.exp(s - m_new)
                total = total * shrink + jnp.sum(p, 0, keepdims=True)
                acc = acc * shrink + dot_nn(values_t[j][h * HD : (h + 1) * HD], p.astype(bf16))
                fresh += [m_new, total, acc]
            return tuple(fresh)

        state = lax.fori_loop(0, i, key_block, tuple(state))
        out = jnp.concatenate(
            [state[3 * h + 2] * (1.0 / state[3 * h + 1]) for h in range(heads)], 0
        )
        out_ref[0, pl.ds(pl.multiple_of(i * block, block), block), :] = jnp.transpose(out).astype(
            bf16
        )
        lse_ref[0, i] = jnp.concatenate(
            [state[3 * h] + jnp.log(state[3 * h + 1]) for h in range(heads)], 0
        )
        return carry

    lax.fori_loop(0, blocks, query_block, 0)


def self_forward(qkv, bias):
    micro, _, length, width = qkv.shape
    heads = width // HD
    blocks = length // BLOCK
    return pl.pallas_call(
        functools.partial(self_forward_kernel, heads, BLOCK),
        grid=(micro,),
        in_specs=[
            pl.BlockSpec((1, 3, length, width), lambda m: (m, 0, 0, 0)),
            pl.BlockSpec((1,) + bias.shape[1:], lambda m: (m, 0, 0, 0, 0)),
        ],
        out_specs=[
            pl.BlockSpec((1, length, width), lambda m: (m, 0, 0)),
            pl.BlockSpec((1, blocks, heads, BLOCK), lambda m: (m, 0, 0, 0)),
        ],
        out_shape=[
            jax.ShapeDtypeStruct((micro, length, width), bf16),
            jax.ShapeDtypeStruct((micro, blocks, heads, BLOCK), f32),
        ],
        scratch_shapes=[
            pltpu.VMEM((heads, length, width), bf16),
            pltpu.VMEM((blocks, width, BLOCK), bf16),
        ],
        compiler_params=pltpu.CompilerParams(vmem_limit_bytes=48 << 20),
        name="self_forward",
    )(qkv, bias)


def self_backward_kernel(
    heads, block, qkv_ref, bias_ref, out_ref, lse_ref, gout_ref, grad_ref,
    queries, keys_h, gouts, delta, grad_q,
):
    length, width = qkv_ref.shape[2], qkv_ref.shape[3]
    blocks = length // block
    per = block // TILE
    masks = head_masks((block, width), heads)
    lane = lax.broadcasted_iota(jnp.int32, (8, width), 1)
    row = lax.broadcasted_iota(jnp.int32, (8, width), 0)
    pick = jnp.where(lane // HD == row, 1.0, 0.0)

    def prepare(i, carry):
        rows = pl.ds(pl.multiple_of(i * block, block), block)
        q = qkv_ref[0, 0, rows, :].astype(f32) * scale_factor
        k = qkv_ref[0, 1, rows, :].astype(f32)
        g = gout_ref[0, rows, :].astype(f32)
        for h in range(heads):
            queries[h, rows, :] = keep_head(q, masks[h], heads).astype(bf16)
            keys_h[h, rows, :] = keep_head(k, masks[h], heads).astype(bf16)
            gouts[h, rows, :] = keep_head(g, masks[h], heads).astype(bf16)
        products = g * out_ref[0, rows, :].astype(f32)
        delta[i] = lax.dot_general(
            pick,
            products,
            (((1,), (1,)), ((), ())),
            precision=lax.Precision.HIGHEST,
            preferred_element_type=f32,
        )
        grad_q[rows, :] = jnp.zeros((block, width), f32)
        return carry

    lax.fori_loop(0, blocks, prepare, 0)
    key_place = lax.broadcasted_iota(jnp.int32, (block, block), 0)
    query_place = lax.broadcasted_iota(jnp.int32, (block, block), 1)
    causal = key_place <= query_place

    def key_block(j, carry):
        krows = pl.ds(pl.multiple_of(j * block, block), block)
        keys = qkv_ref[0, 1, krows, :]
        values = qkv_ref[0, 2, krows, :]

        def pair(i, grad_k, grad_v, diagonal):
            rows = pl.ds(pl.multiple_of(i * block, block), block)
            bias = bias_ref[0, j, i]
            gq = grad_q[rows, :]
            for h in range(heads):
                raw = dot_nt(keys, queries[h, rows, :]).reshape(per, TILE, block)
                shift = bias - lse_ref[0, i, h : h + 1, :]
                s = (raw + shift[:, None, :]).reshape(block, block)
                if diagonal:
                    s = jnp.where(causal, s, masked_score)
                p = jnp.exp(s)
                gp = dot_nt(values, gouts[h, rows, :])
                gs = (p * (gp - delta[i, h : h + 1, :])).astype(bf16)
                grad_v = grad_v + dot_nn(p.astype(bf16), gouts[h, rows, :])
                grad_k = grad_k + dot_nn(gs, queries[h, rows, :])
                gq = gq + dot_tn(gs, keys_h[h, krows, :])
            grad_q[rows, :] = gq
            return grad_k, grad_v

        zero = jnp.zeros((block, width), f32)
        state = pair(j, zero, zero, True)
        state = lax.fori_loop(j + 1, blocks, lambda i, s: pair(i, s[0], s[1], False), state)
        grad_ref[0, 1, krows, :] = state[0].astype(bf16)
        grad_ref[0, 2, krows, :] = state[1].astype(bf16)
        return carry

    lax.fori_loop(0, blocks, key_block, 0)
    grad_ref[0, 0] = (grad_q[...] * scale_factor).astype(bf16)


def self_backward(qkv, bias, out, lse, gout):
    micro, _, length, width = qkv.shape
    heads = width // HD
    blocks = length // BLOCK
    return pl.pallas_call(
        functools.partial(self_backward_kernel, heads, BLOCK),
        grid=(micro,),
        in_specs=[
            pl.BlockSpec((1, 3, length, width), lambda m: (m, 0, 0, 0)),
            pl.BlockSpec((1,) + bias.shape[1:], lambda m: (m, 0, 0, 0, 0)),
            pl.BlockSpec((1, length, width), lambda m: (m, 0, 0)),
            pl.BlockSpec((1, blocks, heads, BLOCK), lambda m: (m, 0, 0, 0)),
            pl.BlockSpec((1, length, width), lambda m: (m, 0, 0)),
        ],
        out_specs=pl.BlockSpec((1, 3, length, width), lambda m: (m, 0, 0, 0)),
        out_shape=jax.ShapeDtypeStruct((micro, 3, length, width), bf16),
        scratch_shapes=[
            pltpu.VMEM((heads, length, width), bf16),
            pltpu.VMEM((heads, length, width), bf16),
            pltpu.VMEM((heads, length, width), bf16),
            pltpu.VMEM((blocks, 8, BLOCK), f32),
            pltpu.VMEM((length, width), f32),
        ],
        compiler_params=pltpu.CompilerParams(vmem_limit_bytes=48 << 20),
        name="self_backward",
    )(qkv, bias, out, lse, gout)


def cross_forward_kernel(lengths_ref, q_ref, k_ref, v_ref, out_ref, lse_ref):
    count, width = k_ref.shape[1], k_ref.shape[2]
    rows = q_ref.shape[1]
    heads = width // HD
    masks = head_masks((rows, width), heads)
    valid = (
        lax.broadcasted_iota(jnp.int32, (count, rows), 0) < lengths_ref[pl.program_id(0)]
    )
    q = q_ref[0].astype(f32) * scale_factor
    values_t = jnp.transpose(v_ref[0].astype(f32)).astype(bf16)
    outs, lses = [], []
    for h in range(heads):
        s = dot_nt(k_ref[0], keep_head(q, masks[h], heads).astype(bf16))
        s = jnp.where(valid, s, masked_score)
        m = jnp.max(s, 0, keepdims=True)
        p = jnp.exp(s - m)
        total = jnp.sum(p, 0, keepdims=True)
        out = dot_nn(values_t[h * HD : (h + 1) * HD], p.astype(bf16))
        outs.append(out * (1.0 / total))
        lses.append(m + jnp.log(total))
    out_ref[0] = jnp.transpose(jnp.concatenate(outs, 0)).astype(bf16)
    lse_ref[0, 0] = jnp.concatenate(lses, 0)


def cross_forward(lengths, queries, pairs):
    micro, rows, width = queries.shape
    count = pairs.shape[1]
    groups = width // 128
    return pl.pallas_call(
        cross_forward_kernel,
        grid=(micro, groups),
        in_specs=[
            pl.BlockSpec(memory_space=pltpu.SMEM),
            pl.BlockSpec((1, rows, 128), lambda m, g: (m, 0, g)),
            pl.BlockSpec((1, count, 128), lambda m, g: (m, 0, g)),
            pl.BlockSpec((1, count, 128), lambda m, g: (m, 0, g + groups)),
        ],
        out_specs=[
            pl.BlockSpec((1, rows, 128), lambda m, g: (m, 0, g)),
            pl.BlockSpec((1, 1, 2, rows), lambda m, g: (m, g, 0, 0)),
        ],
        out_shape=[
            jax.ShapeDtypeStruct((micro, rows, width), bf16),
            jax.ShapeDtypeStruct((micro, groups, 2, rows), f32),
        ],
        compiler_params=pltpu.CompilerParams(vmem_limit_bytes=32 << 20),
        name="cross_forward",
    )(lengths, queries, pairs, pairs)


def cross_backward_kernel(
    lengths_ref, q_ref, k_ref, v_ref, out_ref, lse_ref, gout_ref, gq_ref, gk_ref, gv_ref
):
    count, width = k_ref.shape[1], k_ref.shape[2]
    rows = q_ref.shape[1]
    heads = width // HD
    masks = head_masks((rows, width), heads)
    key_masks = head_masks((count, width), heads)
    valid = (
        lax.broadcasted_iota(jnp.int32, (count, rows), 0) < lengths_ref[pl.program_id(0)]
    )
    lane = lax.broadcasted_iota(jnp.int32, (8, width), 1)
    row = lax.broadcasted_iota(jnp.int32, (8, width), 0)
    pick = jnp.where(lane // HD == row, 1.0, 0.0)
    q = q_ref[0].astype(f32) * scale_factor
    g = gout_ref[0].astype(f32)
    k = k_ref[0].astype(f32)
    delta = lax.dot_general(
        pick,
        g * out_ref[0].astype(f32),
        (((1,), (1,)), ((), ())),
        precision=lax.Precision.HIGHEST,
        preferred_element_type=f32,
    )
    grad_q = jnp.zeros((rows, width), f32)
    grad_k = jnp.zeros((count, width), f32)
    grad_v = jnp.zeros((count, width), f32)
    for h in range(heads):
        qh = keep_head(q, masks[h], heads).astype(bf16)
        gh = keep_head(g, masks[h], heads).astype(bf16)
        kh = keep_head(k, key_masks[h], heads).astype(bf16)
        s = dot_nt(k_ref[0], qh) - lse_ref[0, 0, h : h + 1, :]
        p = jnp.exp(jnp.where(valid, s, masked_score))
        gp = dot_nt(v_ref[0], gh)
        gs = (p * (gp - delta[h : h + 1, :])).astype(bf16)
        grad_v += dot_nn(p.astype(bf16), gh)
        grad_k += dot_nn(gs, qh)
        grad_q += dot_tn(gs, kh)
    gq_ref[0] = (grad_q * scale_factor).astype(bf16)
    gk_ref[0] = grad_k.astype(bf16)
    gv_ref[0] = grad_v.astype(bf16)


def cross_backward(lengths, queries, pairs, out, lse, gout):
    micro, rows, width = queries.shape
    count = pairs.shape[1]
    groups = width // 128
    row_spec = pl.BlockSpec((1, rows, 128), lambda m, g: (m, 0, g))
    key_spec = pl.BlockSpec((1, count, 128), lambda m, g: (m, 0, g))
    value_spec = pl.BlockSpec((1, count, 128), lambda m, g: (m, 0, g + groups))
    lse_spec = pl.BlockSpec((1, 1, 2, rows), lambda m, g: (m, g, 0, 0))
    return pl.pallas_call(
        cross_backward_kernel,
        grid=(micro, groups),
        in_specs=[
            pl.BlockSpec(memory_space=pltpu.SMEM),
            row_spec,
            key_spec,
            value_spec,
            row_spec,
            lse_spec,
            row_spec,
        ],
        out_specs=[row_spec, key_spec, key_spec],
        out_shape=[
            jax.ShapeDtypeStruct((micro, rows, width), bf16),
            jax.ShapeDtypeStruct((micro, count, width), bf16),
            jax.ShapeDtypeStruct((micro, count, width), bf16),
        ],
        compiler_params=pltpu.CompilerParams(vmem_limit_bytes=32 << 20),
        name="cross_backward",
    )(lengths, queries, pairs, pairs, out, lse, gout)


def gelu_parts(v):
    inner = 0.7978845608028654 * (v + 0.044715 * (v * v * v))
    t = jnp.tanh(inner)
    value = 0.5 * v * (1.0 + t)
    slope = 0.5 * (1.0 + t) + 0.5 * v * (1.0 - t * t) * (
        0.7978845608028654 * (1.0 + 3.0 * 0.044715 * (v * v))
    )
    return value, slope


def per_device(
    tokens,
    memory,
    cotangent,
    tile_segment,
    parents,
    memory_lengths,
    self_qkv,
    self_out,
    cross_q,
    cross_kv,
    cross_out,
    ffn_in,
    ffn_out,
    norm_gain,
    norm_bias,
):
    micro, _, row_count, width = tokens.shape
    seq = lax.axis_size("seq")
    total_rows = micro * row_count
    part = width // seq
    memory_rows = memory.shape[2]

    def gather(shard, axis=0):
        return lax.all_gather(shard, ALL, axis=axis, tiled=True)

    joint_weight = gather(self_qkv)
    norms = gather(jnp.concatenate([norm_gain, norm_bias], 0), 1).astype(f32)
    gain_rows, bias_rows = norms[:3], norms[3:]
    small = gather(jnp.concatenate([self_out, cross_q, cross_kv, cross_out, ffn_in], 1))
    memory_full = lax.all_gather(memory[:, 0], "seq", axis=1, tiled=True)
    down_weight = gather(ffn_out)
    cuts = [0]
    for shard in (self_out, cross_q, cross_kv, cross_out, ffn_in):
        cuts.append(cuts[-1] + shard.shape[1])
    self_output, cross_weight, pair_weight, cross_output, upward_weight = (
        small[:, a:b] for a, b in zip(cuts[:-1], cuts[1:])
    )

    x = tokens.reshape(total_rows, width)
    x32 = x.astype(f32)
    bias = jax.vmap(lambda t, p: tree_bias(t, p, BLOCK))(tile_segment[:, 0], parents[:, 0])
    lengths = memory_lengths[:, 0]

    def to_heads(rows, parts):
        blocks = rows.reshape(micro, row_count, parts, seq, part).transpose(0, 2, 3, 1, 4)
        swapped = lax.all_to_all(blocks, "seq", split_axis=2, concat_axis=2, tiled=True)
        return swapped.reshape(micro, parts, seq * row_count, part)

    def to_rows(heads, parts):
        blocks = heads.reshape(micro, parts, seq, row_count, part)
        swapped = lax.all_to_all(blocks, "seq", split_axis=2, concat_axis=2, tiled=True)
        return swapped.transpose(0, 3, 1, 2, 4).reshape(total_rows, parts * width)

    projected = dot_nn(x, joint_weight).astype(bf16)
    qkv = to_heads(projected, 3)
    attended_heads, self_lse = self_forward(qkv, bias)
    attended = to_rows(attended_heads, 1)

    mixed_first = residual_weight * x32 + dot_nn(attended, self_output)
    hidden_first = layer_norm(mixed_first, gain_rows[0], bias_rows[0])
    hidden_first_low = hidden_first.astype(bf16)
    cross_query = dot_nn(hidden_first_low, cross_weight).astype(bf16)
    cross_query = cross_query.reshape(micro, row_count, width)
    count = memory_full.shape[1]
    pairs = dot_nn(memory_full.reshape(micro * count, width), pair_weight).astype(bf16)
    pairs = pairs.reshape(micro, count, 2 * width)
    cross_heads, cross_lse = cross_forward(lengths, cross_query, pairs)
    cross_attended = cross_heads.reshape(total_rows, width)
    mixed_second = residual_weight * hidden_first + dot_nn(cross_attended, cross_output)
    hidden_second = layer_norm(mixed_second, gain_rows[1], bias_rows[1])
    hidden_second_low = hidden_second.astype(bf16)
    pre_active = dot_nn(hidden_second_low, upward_weight)
    active = gelu_parts(pre_active)[0].astype(bf16)
    mixed_third = residual_weight * hidden_second + dot_nn(active, down_weight)
    output = layer_norm(mixed_third, gain_rows[2], bias_rows[2]).astype(bf16)

    upstream = cotangent.reshape(total_rows, width).astype(f32)
    grad_third, gain_third, bias_third = layer_norm_back(mixed_third, gain_rows[2], upstream)
    branch_third = grad_third.astype(bf16)
    grad_down = dot_tn(active, branch_third).astype(bf16)
    grad_inner = (gelu_parts(pre_active)[1] * dot_nt(branch_third, down_weight)).astype(bf16)
    grad_upward = dot_tn(hidden_second_low, grad_inner).astype(bf16)

    def scatter(full, axis=0):
        return lax.psum_scatter(full, ALL, scatter_dimension=axis, tiled=True)

    own_down = scatter(grad_down).astype(f32)
    own_upward = scatter(grad_upward).astype(f32)

    grad_hidden_second = residual_weight * grad_third + dot_nt(grad_inner, upward_weight)
    grad_second, gain_second, bias_second = layer_norm_back(
        mixed_second, gain_rows[1], grad_hidden_second
    )
    branch_second = grad_second.astype(bf16)
    grad_cross_output = dot_tn(cross_attended, branch_second).astype(bf16)
    grad_cross_attended = dot_nt(branch_second, cross_output).astype(bf16)
    grad_cross_low, grad_keys, grad_values = cross_backward(
        lengths,
        cross_query,
        pairs,
        cross_heads,
        cross_lse,
        grad_cross_attended.reshape(micro, row_count, width),
    )
    memory_partial = jnp.concatenate([grad_keys, grad_values], 2)
    own_pairs = lax.psum_scatter(memory_partial, "seq", scatter_dimension=1, tiled=True)
    grad_cross_low = grad_cross_low.reshape(total_rows, width)
    grad_cross_weight = dot_tn(hidden_first_low, grad_cross_low).astype(bf16)
    grad_hidden_first = residual_weight * grad_second + dot_nt(grad_cross_low, cross_weight)
    grad_first, gain_first, bias_first = layer_norm_back(
        mixed_first, gain_rows[0], grad_hidden_first
    )
    branch_first = grad_first.astype(bf16)
    grad_self_output = dot_tn(attended, branch_first).astype(bf16)
    grad_attended = dot_nt(branch_first, self_output).astype(bf16)
    gout = to_heads(grad_attended, 1)
    own_three = scatter(
        jnp.concatenate([grad_self_output, grad_cross_weight, grad_cross_output], 1)
    ).astype(f32)
    grad_qkv = self_backward(qkv, bias, attended_heads, self_lse, gout[:, 0])
    grad_projected = to_rows(grad_qkv, 3)
    grad_joint = dot_tn(x, grad_projected).astype(bf16)
    grad_tokens = (residual_weight * grad_first + dot_nt(grad_projected, joint_weight)).astype(bf16)
    grad_pairs_low = own_pairs.reshape(micro * memory_rows, 2 * width)
    grad_pair_weight = dot_tn(memory.reshape(micro * memory_rows, width), grad_pairs_low)
    grad_memory = dot_nt(grad_pairs_low, pair_weight).astype(bf16)
    own_last = scatter(
        jnp.concatenate([grad_joint, grad_pair_weight.astype(bf16)], 1)
    ).astype(f32)
    norm_grads = jnp.stack(
        [gain_first, gain_second, gain_third, bias_first, bias_second, bias_third]
    )
    own_norms = scatter(norm_grads, 1)
    return (
        output.reshape(tokens.shape),
        grad_tokens.reshape(tokens.shape),
        grad_memory.reshape(memory.shape),
        own_last[:, : 3 * width],
        own_three[:, :width],
        own_three[:, width : 2 * width],
        own_last[:, 3 * width :],
        own_three[:, 2 * width :],
        own_upward,
        own_down,
        own_norms[:3],
        own_norms[3:],
    )


def solution(mesh):
    rows = P(None, "fsdp", "seq", None)
    weight = P(ALL, None)
    in_specs = (
        rows,
        rows,
        rows,
        P(None, "fsdp", None),
        P(None, "fsdp", None),
        P(None, "fsdp"),
    ) + (weight,) * 7 + (P(None, ALL),) * 2
    out_specs = (rows, rows, rows) + (weight,) * 7 + (P(None, ALL),) * 2
    return jax.shard_map(
        per_device, mesh=mesh, in_specs=in_specs, out_specs=out_specs, check_vma=False
    )
```

```python
import functools

import jax
import jax.numpy as jnp
from jax import lax
from jax.experimental import pallas as pl
from jax.experimental.pallas import tpu as pltpu
from jax.sharding import PartitionSpec as P

H = 16
HD = 64
TILE = 128
BLOCK = 256

scale_factor = 0.125
residual_weight = 36.0**0.25
norm_epsilon = 1e-05
masked_score = -1e30
ALL = ("seq", "fsdp")
f32 = jnp.float32
bf16 = jnp.bfloat16
MESH = pl.DeviceIdType.MESH


def dot_nn(a, b):
    return lax.dot_general(a, b, (((1,), (0,)), ((), ())), preferred_element_type=f32)


def dot_nt(a, b):
    return lax.dot_general(a, b, (((1,), (1,)), ((), ())), preferred_element_type=f32)


def dot_tn(a, b):
    return lax.dot_general(a, b, (((0,), (0,)), ((), ())), preferred_element_type=f32)


def norm_stats(incoming):
    row_mean = jnp.mean(incoming, -1, keepdims=True)
    centred = incoming - row_mean
    variance = jnp.mean(centred * centred, -1, keepdims=True)
    return centred, lax.rsqrt(variance + norm_epsilon)


def layer_norm(incoming, gain_row, bias_row):
    centred, inverse = norm_stats(incoming)
    return centred * inverse * gain_row + bias_row


def layer_norm_back(incoming, gain_row, upstream):
    centred, inverse = norm_stats(incoming)
    normal = centred * inverse
    grad_bias = jnp.sum(upstream, 0)
    grad_gain = jnp.sum(upstream * normal, 0)
    scaled = upstream * gain_row
    grad = inverse * (
        scaled
        - jnp.mean(scaled, -1, keepdims=True)
        - normal * jnp.mean(scaled * normal, -1, keepdims=True)
    )
    return grad, grad_gain, grad_bias


def ancestors(parent_ids):
    segment_ids = jnp.arange(parent_ids.shape[0], dtype=jnp.int32)
    hop = (parent_ids[:, None] == segment_ids[None, :]).astype(f32)
    reach = jnp.maximum(hop, (segment_ids[:, None] == segment_ids[None, :]).astype(f32))
    steps = 1
    while steps < parent_ids.shape[0]:
        reach = jnp.minimum(jnp.dot(reach, reach, precision=lax.Precision.HIGHEST), 1.0)
        steps *= 2
    return reach


def tree_bias(tile_segments, parent_ids, block):
    tiles = tile_segments.shape[0]
    onehot = (
        tile_segments[:, None] == jnp.arange(parent_ids.shape[0], dtype=jnp.int32)[None, :]
    ).astype(f32)
    high = lax.Precision.HIGHEST
    related = jnp.dot(
        jnp.dot(onehot, ancestors(parent_ids), precision=high), onehot.T, precision=high
    )
    bias = jnp.where(related > 0.5, 0.0, masked_score)
    per = block // TILE
    blocks = tiles // per
    bias = bias.reshape(blocks, per, blocks, per).transpose(2, 0, 3, 1)
    return jnp.repeat(bias, TILE, axis=3)


def head_masks(shape, heads):
    lane = lax.broadcasted_iota(jnp.int32, shape, 1)
    return [(lane >= h * HD) & (lane < (h + 1) * HD) for h in range(heads)]


def keep_head(value, mask, heads):
    return value if heads == 1 else jnp.where(mask, value, jnp.zeros_like(value))


def greet(peers):
    barrier = pltpu.get_barrier_semaphore()
    for peer in peers:
        pl.semaphore_signal(barrier, inc=1, device_id=peer, device_id_type=MESH)
    pl.semaphore_wait(barrier, len(peers))


def peer_at(step):
    count = lax.axis_size("seq")
    return lax.rem(lax.axis_index("seq") + step, count)


def rows_at(i, count):
    return pl.ds(pl.multiple_of(i * count, count), count)


def cut_heads(rows_ref, m, parts, blocks_ref):
    seq, part = blocks_ref.shape[2], blocks_ref.shape[4]
    for p in range(parts):
        for s in range(seq):
            first = (p * seq + s) * part
            blocks_ref[m, p, s] = rows_ref[m, :, first : first + part]


def join_heads(blocks_ref, m, parts, rows_ref):
    seq, part = blocks_ref.shape[2], blocks_ref.shape[4]
    for p in range(parts):
        for s in range(seq):
            first = (p * seq + s) * part
            rows_ref[m, :, first : first + part] = blocks_ref[m, p, s]


def to_peer(source_ref, target_ref, send, receive, m, step):
    rows = source_ref.shape[3]
    return pltpu.make_async_remote_copy(
        src_ref=source_ref.at[m, :, peer_at(step)],
        dst_ref=target_ref.at[m, :, rows_at(lax.axis_index("seq"), rows)],
        send_sem=send.at[m, step],
        recv_sem=receive.at[m, step],
        device_id={"seq": peer_at(step)},
        device_id_type=MESH,
    )


def to_self(source_ref, target_ref, sem, m):
    rows = source_ref.shape[3]
    me = lax.axis_index("seq")
    return pltpu.make_async_copy(
        source_ref.at[m, :, me], target_ref.at[m, :, rows_at(me, rows)], sem.at[m, 0]
    )


def send_blocks(source_ref, target_ref, send, receive, m):
    for step in range(1, lax.axis_size("seq")):
        to_peer(source_ref, target_ref, send, receive, m, step).start()
    to_self(source_ref, target_ref, send, m).start()


def take_blocks(source_ref, target_ref, send, receive, m):
    for step in range(1, lax.axis_size("seq")):
        to_peer(source_ref, target_ref, send, receive, m, step).wait_recv()
    to_self(source_ref, target_ref, send, m).wait()


def home_copy(source_ref, target_ref, send, receive, m, place):
    rows = target_ref.shape[3]
    me = lax.axis_index("seq")
    count = lax.axis_size("seq")
    step = lax.rem(place - me + count, count)
    return pltpu.make_async_remote_copy(
        src_ref=source_ref.at[m, :, rows_at(place, rows)],
        dst_ref=target_ref.at[m, :, me],
        send_sem=send.at[m, step],
        recv_sem=receive.at[m, step],
        device_id={"seq": place},
        device_id_type=MESH,
    )


def home_self(source_ref, target_ref, sem, m):
    rows = target_ref.shape[3]
    me = lax.axis_index("seq")
    return pltpu.make_async_copy(
        source_ref.at[m, :, rows_at(me, rows)], target_ref.at[m, :, me], sem.at[m, 0]
    )


def send_home(source_ref, target_ref, send, receive, m, place):
    me = lax.axis_index("seq")

    @pl.when(place != me)
    def _():
        home_copy(source_ref, target_ref, send, receive, m, place).start()

    @pl.when(place == me)
    def _():
        home_self(source_ref, target_ref, send, m).start()


def take_home(source_ref, target_ref, send, receive, m):
    for step in range(1, lax.axis_size("seq")):
        home_copy(source_ref, target_ref, send, receive, m, peer_at(step)).wait()
    home_self(source_ref, target_ref, send, m).wait()


def self_forward_kernel(
    heads, block, rows_ref, bias_ref, qkv_ref, out_ref, lse_ref, attended_ref,
    cut, back, queries, values_t, send_in, take_in, send_out, take_out,
):
    micro, _, length, width = qkv_ref.shape
    seq = lax.axis_size("seq")
    blocks = length // block
    per = block // TILE
    place_rows = length // seq
    masks = head_masks((block, width), heads)
    greet([{"seq": peer_at(step)} for step in range(1, seq)])

    def launch(m, carry):
        cut_heads(rows_ref, m, 3, cut)

        @pl.when(m < 2)
        def _():
            send_blocks(cut, qkv_ref, send_in, take_in, m)

        return carry

    lax.fori_loop(0, micro, launch, 0)
    key_place = lax.broadcasted_iota(jnp.int32, (block, block), 0)
    query_place = lax.broadcasted_iota(jnp.int32, (block, block), 1)
    causal = key_place <= query_place

    def one_micro(m, carry):
        take_blocks(cut, qkv_ref, send_in, take_in, m)

        @pl.when(m + 2 < micro)
        def _():
            send_blocks(cut, qkv_ref, send_in, take_in, m + 2)

        def prepare(i, carry):
            rows = rows_at(i, block)
            q = qkv_ref[m, 0, rows, :].astype(f32) * scale_factor
            for h in range(heads):
                queries[h, rows, :] = keep_head(q, masks[h], heads).astype(bf16)
            values_t[i] = jnp.transpose(qkv_ref[m, 2, rows, :].astype(f32)).astype(bf16)
            return carry

        lax.fori_loop(0, blocks, prepare, 0)

        def scores_of(i, j, h):
            raw = dot_nt(qkv_ref[m, 1, rows_at(j, block), :], queries[h, rows_at(i, block), :])
            bias = bias_ref[m, j, i]
            return (raw.reshape(per, TILE, block) + bias[:, None, :]).reshape(block, block)

        def query_block(i, carry):
            state = []
            for h in range(heads):
                s = jnp.where(causal, scores_of(i, i, h), masked_score)
                top = jnp.max(s, 0, keepdims=True)
                p = jnp.exp(s - top)
                total = jnp.sum(p, 0, keepdims=True)
                acc = dot_nn(values_t[i][h * HD : (h + 1) * HD], p.astype(bf16))
                state += [top, total, acc]

            def key_block(j, state):
                fresh = []
                for h in range(heads):
                    top, total, acc = state[3 * h : 3 * h + 3]
                    s = scores_of(i, j, h)
                    higher = jnp.maximum(top, jnp.max(s, 0, keepdims=True))
                    shrink = jnp.exp(top - higher)
                    p = jnp.exp(s - higher)
                    total = total * shrink + jnp.sum(p, 0, keepdims=True)
                    acc = acc * shrink + dot_nn(
                        values_t[j][h * HD : (h + 1) * HD], p.astype(bf16)
                    )
                    fresh += [higher, total, acc]
                return tuple(fresh)

            state = lax.fori_loop(0, i, key_block, tuple(state))
            out = jnp.concatenate(
                [state[3 * h + 2] * (1.0 / state[3 * h + 1]) for h in range(heads)], 0
            )
            out_ref[m, 0, rows_at(i, block), :] = jnp.transpose(out).astype(bf16)
            lse_ref[m, i] = jnp.concatenate(
                [state[3 * h] + jnp.log(state[3 * h + 1]) for h in range(heads)], 0
            )
            for sub in range(block // place_rows):
                place = i * (block // place_rows) + sub
                send_home(out_ref, back, send_out, take_out, m, place)
            return carry

        lax.fori_loop(0, blocks, query_block, 0)
        return carry

    lax.fori_loop(0, micro, one_micro, 0)

    def finish(m, carry):
        for step in range(1, seq):
            to_peer(cut, qkv_ref, send_in, take_in, m, step).wait_send()
        take_home(out_ref, back, send_out, take_out, m)
        join_heads(back, m, 1, attended_ref)
        return carry

    lax.fori_loop(0, micro, finish, 0)


def self_forward(projected, bias, seq):
    micro, rows, width = projected.shape
    part = width // 3 // seq
    heads = part // HD
    length = rows * seq
    blocks = length // BLOCK
    whole = pl.BlockSpec(memory_space=pltpu.VMEM)
    sems = pltpu.SemaphoreType.DMA((micro, seq))
    return pl.pallas_call(
        functools.partial(self_forward_kernel, heads, BLOCK),
        in_specs=[whole, whole],
        out_specs=[whole] * 4,
        out_shape=[
            jax.ShapeDtypeStruct((micro, 3, length, part), bf16),
            jax.ShapeDtypeStruct((micro, 1, length, part), bf16),
            jax.ShapeDtypeStruct((micro, blocks, heads, BLOCK), f32),
            jax.ShapeDtypeStruct((micro, rows, width // 3), bf16),
        ],
        scratch_shapes=[
            pltpu.VMEM((micro, 3, seq, rows, part), bf16),
            pltpu.VMEM((micro, 1, seq, rows, part), bf16),
            pltpu.VMEM((heads, length, part), bf16),
            pltpu.VMEM((blocks, part, BLOCK), bf16),
            sems,
            sems,
            sems,
            sems,
        ],
        compiler_params=pltpu.CompilerParams(
            vmem_limit_bytes=50 << 20, collective_id=1, has_side_effects=True
        ),
        name="self_forward",
    )(projected, bias)


def self_backward_kernel(
    heads, block, rows_ref, qkv_ref, bias_ref, out_ref, lse_ref, grad_ref,
    cut, gout, grads, back, queries, keys_h, gouts, delta, grad_q,
    send_in, take_in, send_out, take_out,
):
    micro, _, length, width = qkv_ref.shape
    seq = lax.axis_size("seq")
    blocks = length // block
    per = block // TILE
    place_rows = length // seq
    masks = head_masks((block, width), heads)
    lane = lax.broadcasted_iota(jnp.int32, (8, width), 1)
    first_lane = lax.broadcasted_iota(jnp.int32, (8, width), 0) * HD
    pick = jnp.where((lane >= first_lane) & (lane < first_lane + HD), 1.0, 0.0)
    greet([{"seq": peer_at(step)} for step in range(1, seq)])

    def launch(m, carry):
        cut_heads(rows_ref, m, 1, cut)
        send_blocks(cut, gout, send_in, take_in, m)
        return carry

    lax.fori_loop(0, micro, launch, 0)
    key_place = lax.broadcasted_iota(jnp.int32, (block, block), 0)
    query_place = lax.broadcasted_iota(jnp.int32, (block, block), 1)
    causal = key_place <= query_place

    def one_micro(m, carry):
        take_blocks(cut, gout, send_in, take_in, m)

        def prepare(i, carry):
            rows = rows_at(i, block)
            q = qkv_ref[m, 0, rows, :].astype(f32) * scale_factor
            k = qkv_ref[m, 1, rows, :].astype(f32)
            g = gout[m, 0, rows, :].astype(f32)
            for h in range(heads):
                queries[h, rows, :] = keep_head(q, masks[h], heads).astype(bf16)
                keys_h[h, rows, :] = keep_head(k, masks[h], heads).astype(bf16)
                gouts[h, rows, :] = keep_head(g, masks[h], heads).astype(bf16)
            delta[i] = lax.dot_general(
                pick,
                g * out_ref[m, 0, rows, :].astype(f32),
                (((1,), (1,)), ((), ())),
                precision=lax.Precision.HIGHEST,
                preferred_element_type=f32,
            )
            grad_q[rows, :] = jnp.zeros((block, width), f32)
            return carry

        lax.fori_loop(0, blocks, prepare, 0)

        def key_block(j, carry):
            krows = rows_at(j, block)

            def pair(i, grad_k, grad_v, diagonal):
                rows = rows_at(i, block)
                bias = bias_ref[m, j, i]
                gq = grad_q[rows, :]
                for h in range(heads):
                    raw = dot_nt(qkv_ref[m, 1, krows, :], queries[h, rows, :])
                    shift = bias - lse_ref[m, i, h : h + 1, :]
                    s = (raw.reshape(per, TILE, block) + shift[:, None, :]).reshape(block, block)
                    if diagonal:
                        s = jnp.where(causal, s, masked_score)
                    p = jnp.exp(s)
                    gp = dot_nt(qkv_ref[m, 2, krows, :], gouts[h, rows, :])
                    gs = (p * (gp - delta[i, h : h + 1, :])).astype(bf16)
                    grad_v = grad_v + dot_nn(p.astype(bf16), gouts[h, rows, :])
                    grad_k = grad_k + dot_nn(gs, queries[h, rows, :])
                    gq = gq + dot_tn(gs, keys_h[h, krows, :])
                grad_q[rows, :] = gq
                return grad_k, grad_v

            zero = jnp.zeros((block, width), f32)
            state = pair(j, zero, zero, True)
            state = lax.fori_loop(
                j + 1, blocks, lambda i, s: pair(i, s[0], s[1], False), state
            )
            grads[m, 0, krows, :] = (grad_q[krows, :] * scale_factor).astype(bf16)
            grads[m, 1, krows, :] = state[0].astype(bf16)
            grads[m, 2, krows, :] = state[1].astype(bf16)
            for sub in range(block // place_rows):
                place = j * (block // place_rows) + sub
                send_home(grads, back, send_out, take_out, m, place)
            return carry

        lax.fori_loop(0, blocks, key_block, 0)
        return carry

    lax.fori_loop(0, micro, one_micro, 0)

    def finish(m, carry):
        for step in range(1, seq):
            to_peer(cut, gout, send_in, take_in, m, step).wait_send()
        take_home(grads, back, send_out, take_out, m)
        join_heads(back, m, 3, grad_ref)
        return carry

    lax.fori_loop(0, micro, finish, 0)


def self_backward(grad_attended, qkv, bias, out, lse, seq):
    micro, rows, width = grad_attended.shape
    length, part = qkv.shape[2:]
    heads = part // HD
    blocks = length // BLOCK
    whole = pl.BlockSpec(memory_space=pltpu.VMEM)
    sems = pltpu.SemaphoreType.DMA((micro, seq))
    return pl.pallas_call(
        functools.partial(self_backward_kernel, heads, BLOCK),
        in_specs=[whole] * 5,
        out_specs=whole,
        out_shape=jax.ShapeDtypeStruct((micro, rows, 3 * width), bf16),
        scratch_shapes=[
            pltpu.VMEM((micro, 1, seq, rows, part), bf16),
            pltpu.VMEM((micro, 1, length, part), bf16),
            pltpu.VMEM((micro, 3, length, part), bf16),
            pltpu.VMEM((micro, 3, seq, rows, part), bf16),
            pltpu.VMEM((heads, length, part), bf16),
            pltpu.VMEM((heads, length, part), bf16),
            pltpu.VMEM((heads, length, part), bf16),
            pltpu.VMEM((blocks, 8, BLOCK), f32),
            pltpu.VMEM((length, part), f32),
            sems,
            sems,
            sems,
            sems,
        ],
        compiler_params=pltpu.CompilerParams(
            vmem_limit_bytes=50 << 20, collective_id=2, has_side_effects=True
        ),
        name="self_backward",
    )(grad_attended, qkv, bias, out, lse)


def cross_forward_kernel(lengths_ref, q_ref, k_ref, v_ref, out_ref, lse_ref):
    count, width = k_ref.shape[1], k_ref.shape[2]
    rows = q_ref.shape[1]
    heads = width // HD
    masks = head_masks((rows, width), heads)
    valid = (
        lax.broadcasted_iota(jnp.int32, (count, rows), 0) < lengths_ref[pl.program_id(0)]
    )
    q = q_ref[0].astype(f32) * scale_factor
    values_t = jnp.transpose(v_ref[0].astype(f32)).astype(bf16)
    outs, lses = [], []
    for h in range(heads):
        s = dot_nt(k_ref[0], keep_head(q, masks[h], heads).astype(bf16))
        s = jnp.where(valid, s, masked_score)
        m = jnp.max(s, 0, keepdims=True)
        p = jnp.exp(s - m)
        total = jnp.sum(p, 0, keepdims=True)
        out = dot_nn(values_t[h * HD : (h + 1) * HD], p.astype(bf16))
        outs.append(out * (1.0 / total))
        lses.append(m + jnp.log(total))
    out_ref[0] = jnp.transpose(jnp.concatenate(outs, 0)).astype(bf16)
    lse_ref[0, 0] = jnp.concatenate(lses, 0)


def cross_forward(lengths, queries, pairs):
    micro, rows, width = queries.shape
    count = pairs.shape[1]
    groups = width // 128
    return pl.pallas_call(
        cross_forward_kernel,
        grid=(micro, groups),
        in_specs=[
            pl.BlockSpec(memory_space=pltpu.SMEM),
            pl.BlockSpec((1, rows, 128), lambda m, g: (m, 0, g)),
            pl.BlockSpec((1, count, 128), lambda m, g: (m, 0, g)),
            pl.BlockSpec((1, count, 128), lambda m, g: (m, 0, g + groups)),
        ],
        out_specs=[
            pl.BlockSpec((1, rows, 128), lambda m, g: (m, 0, g)),
            pl.BlockSpec((1, 1, 2, rows), lambda m, g: (m, g, 0, 0)),
        ],
        out_shape=[
            jax.ShapeDtypeStruct((micro, rows, width), bf16),
            jax.ShapeDtypeStruct((micro, groups, 2, rows), f32),
        ],
        compiler_params=pltpu.CompilerParams(vmem_limit_bytes=32 << 20),
        name="cross_forward",
    )(lengths, queries, pairs, pairs)


def cross_backward_kernel(
    lengths_ref, q_ref, k_ref, v_ref, out_ref, lse_ref, gout_ref, gq_ref, gk_ref, gv_ref
):
    count, width = k_ref.shape[1], k_ref.shape[2]
    rows = q_ref.shape[1]
    heads = width // HD
    masks = head_masks((rows, width), heads)
    key_masks = head_masks((count, width), heads)
    valid = (
        lax.broadcasted_iota(jnp.int32, (count, rows), 0) < lengths_ref[pl.program_id(0)]
    )
    lane = lax.broadcasted_iota(jnp.int32, (8, width), 1)
    row = lax.broadcasted_iota(jnp.int32, (8, width), 0)
    pick = jnp.where((lane >= row * HD) & (lane < (row + 1) * HD), 1.0, 0.0)
    q = q_ref[0].astype(f32) * scale_factor
    g = gout_ref[0].astype(f32)
    k = k_ref[0].astype(f32)
    delta = lax.dot_general(
        pick,
        g * out_ref[0].astype(f32),
        (((1,), (1,)), ((), ())),
        precision=lax.Precision.HIGHEST,
        preferred_element_type=f32,
    )
    grad_q = jnp.zeros((rows, width), f32)
    grad_k = jnp.zeros((count, width), f32)
    grad_v = jnp.zeros((count, width), f32)
    for h in range(heads):
        qh = keep_head(q, masks[h], heads).astype(bf16)
        gh = keep_head(g, masks[h], heads).astype(bf16)
        kh = keep_head(k, key_masks[h], heads).astype(bf16)
        s = dot_nt(k_ref[0], qh) - lse_ref[0, 0, h : h + 1, :]
        p = jnp.exp(jnp.where(valid, s, masked_score))
        gp = dot_nt(v_ref[0], gh)
        gs = (p * (gp - delta[h : h + 1, :])).astype(bf16)
        grad_v += dot_nn(p.astype(bf16), gh)
        grad_k += dot_nn(gs, qh)
        grad_q += dot_tn(gs, kh)
    gq_ref[0] = (grad_q * scale_factor).astype(bf16)
    gk_ref[0] = grad_k.astype(bf16)
    gv_ref[0] = grad_v.astype(bf16)


def cross_backward(lengths, queries, pairs, out, lse, gout):
    micro, rows, width = queries.shape
    count = pairs.shape[1]
    groups = width // 128
    row_spec = pl.BlockSpec((1, rows, 128), lambda m, g: (m, 0, g))
    key_spec = pl.BlockSpec((1, count, 128), lambda m, g: (m, 0, g))
    value_spec = pl.BlockSpec((1, count, 128), lambda m, g: (m, 0, g + groups))
    lse_spec = pl.BlockSpec((1, 1, 2, rows), lambda m, g: (m, g, 0, 0))
    return pl.pallas_call(
        cross_backward_kernel,
        grid=(micro, groups),
        in_specs=[
            pl.BlockSpec(memory_space=pltpu.SMEM),
            row_spec,
            key_spec,
            value_spec,
            row_spec,
            lse_spec,
            row_spec,
        ],
        out_specs=[row_spec, key_spec, key_spec],
        out_shape=[
            jax.ShapeDtypeStruct((micro, rows, width), bf16),
            jax.ShapeDtypeStruct((micro, count, width), bf16),
            jax.ShapeDtypeStruct((micro, count, width), bf16),
        ],
        compiler_params=pltpu.CompilerParams(vmem_limit_bytes=32 << 20),
        name="cross_backward",
    )(lengths, queries, pairs, pairs, out, lse, gout)


def gelu_parts(v):
    inner = 0.7978845608028654 * (v + 0.044715 * (v * v * v))
    t = jnp.tanh(inner)
    value = 0.5 * v * (1.0 + t)
    slope = 0.5 * (1.0 + t) + 0.5 * v * (1.0 - t * t) * (
        0.7978845608028654 * (1.0 + 3.0 * 0.044715 * (v * v))
    )
    return value, slope


def per_device(
    tokens,
    memory,
    cotangent,
    tile_segment,
    parents,
    memory_lengths,
    self_qkv,
    self_out,
    cross_q,
    cross_kv,
    cross_out,
    ffn_in,
    ffn_out,
    norm_gain,
    norm_bias,
):
    micro, _, row_count, width = tokens.shape
    seq = lax.axis_size("seq")
    total_rows = micro * row_count
    memory_rows = memory.shape[2]

    def gather(shard, axis=0):
        return lax.all_gather(shard, ALL, axis=axis, tiled=True)

    joint_weight = gather(self_qkv)
    norms = gather(jnp.concatenate([norm_gain, norm_bias], 0), 1).astype(f32)
    gain_rows, bias_rows = norms[:3], norms[3:]
    small = gather(jnp.concatenate([self_out, cross_q, cross_kv, cross_out, ffn_in], 1))
    memory_full = lax.all_gather(memory[:, 0], "seq", axis=1, tiled=True)
    down_weight = gather(ffn_out)
    cuts = [0]
    for shard in (self_out, cross_q, cross_kv, cross_out, ffn_in):
        cuts.append(cuts[-1] + shard.shape[1])
    self_output, cross_weight, pair_weight, cross_output, upward_weight = (
        small[:, a:b] for a, b in zip(cuts[:-1], cuts[1:])
    )

    x = tokens.reshape(total_rows, width)
    x32 = x.astype(f32)
    bias = jax.vmap(lambda t, p: tree_bias(t, p, BLOCK))(tile_segment[:, 0], parents[:, 0])
    lengths = memory_lengths[:, 0]

    projected = dot_nn(x, joint_weight).astype(bf16)
    qkv, attended_heads, self_lse, attended = self_forward(
        projected.reshape(micro, row_count, 3 * width), bias, seq
    )
    attended = attended.reshape(total_rows, width)

    mixed_first = residual_weight * x32 + dot_nn(attended, self_output)
    hidden_first = layer_norm(mixed_first, gain_rows[0], bias_rows[0])
    hidden_first_low = hidden_first.astype(bf16)
    cross_query = dot_nn(hidden_first_low, cross_weight).astype(bf16)
    cross_query = cross_query.reshape(micro, row_count, width)
    count = memory_full.shape[1]
    pairs = dot_nn(memory_full.reshape(micro * count, width), pair_weight).astype(bf16)
    pairs = pairs.reshape(micro, count, 2 * width)
    cross_heads, cross_lse = cross_forward(lengths, cross_query, pairs)
    cross_attended = cross_heads.reshape(total_rows, width)
    mixed_second = residual_weight * hidden_first + dot_nn(cross_attended, cross_output)
    hidden_second = layer_norm(mixed_second, gain_rows[1], bias_rows[1])
    hidden_second_low = hidden_second.astype(bf16)
    pre_active = dot_nn(hidden_second_low, upward_weight)
    active = gelu_parts(pre_active)[0].astype(bf16)
    mixed_third = residual_weight * hidden_second + dot_nn(active, down_weight)
    output = layer_norm(mixed_third, gain_rows[2], bias_rows[2]).astype(bf16)

    upstream = cotangent.reshape(total_rows, width).astype(f32)
    grad_third, gain_third, bias_third = layer_norm_back(mixed_third, gain_rows[2], upstream)
    branch_third = grad_third.astype(bf16)
    grad_down = dot_tn(active, branch_third).astype(bf16)
    grad_inner = (gelu_parts(pre_active)[1] * dot_nt(branch_third, down_weight)).astype(bf16)
    grad_upward = dot_tn(hidden_second_low, grad_inner).astype(bf16)

    def scatter(full, axis=0):
        return lax.psum_scatter(full, ALL, scatter_dimension=axis, tiled=True)

    own_down = scatter(grad_down).astype(f32)
    own_upward = scatter(grad_upward).astype(f32)

    grad_hidden_second = residual_weight * grad_third + dot_nt(grad_inner, upward_weight)
    grad_second, gain_second, bias_second = layer_norm_back(
        mixed_second, gain_rows[1], grad_hidden_second
    )
    branch_second = grad_second.astype(bf16)
    grad_cross_output = dot_tn(cross_attended, branch_second).astype(bf16)
    grad_cross_attended = dot_nt(branch_second, cross_output).astype(bf16)
    grad_cross_low, grad_keys, grad_values = cross_backward(
        lengths,
        cross_query,
        pairs,
        cross_heads,
        cross_lse,
        grad_cross_attended.reshape(micro, row_count, width),
    )
    memory_partial = jnp.concatenate([grad_keys, grad_values], 2)
    own_pairs = lax.psum_scatter(memory_partial, "seq", scatter_dimension=1, tiled=True)
    grad_cross_low = grad_cross_low.reshape(total_rows, width)
    grad_cross_weight = dot_tn(hidden_first_low, grad_cross_low).astype(bf16)
    grad_hidden_first = residual_weight * grad_second + dot_nt(grad_cross_low, cross_weight)
    grad_first, gain_first, bias_first = layer_norm_back(
        mixed_first, gain_rows[0], grad_hidden_first
    )
    branch_first = grad_first.astype(bf16)
    grad_self_output = dot_tn(attended, branch_first).astype(bf16)
    grad_attended = dot_nt(branch_first, self_output).astype(bf16)
    own_three = scatter(
        jnp.concatenate([grad_self_output, grad_cross_weight, grad_cross_output], 1)
    ).astype(f32)
    grad_projected = self_backward(
        grad_attended.reshape(micro, row_count, width), qkv, bias, attended_heads, self_lse, seq
    ).reshape(total_rows, 3 * width)
    grad_joint = dot_tn(x, grad_projected).astype(bf16)
    grad_tokens = (residual_weight * grad_first + dot_nt(grad_projected, joint_weight)).astype(bf16)
    grad_pairs_low = own_pairs.reshape(micro * memory_rows, 2 * width)
    grad_pair_weight = dot_tn(memory.reshape(micro * memory_rows, width), grad_pairs_low)
    grad_memory = dot_nt(grad_pairs_low, pair_weight).astype(bf16)
    own_last = scatter(
        jnp.concatenate([grad_joint, grad_pair_weight.astype(bf16)], 1)
    ).astype(f32)
    norm_grads = jnp.stack(
        [gain_first, gain_second, gain_third, bias_first, bias_second, bias_third]
    )
    own_norms = scatter(norm_grads, 1)
    return (
        output.reshape(tokens.shape),
        grad_tokens.reshape(tokens.shape),
        grad_memory.reshape(memory.shape),
        own_last[:, : 3 * width],
        own_three[:, :width],
        own_three[:, width : 2 * width],
        own_last[:, 3 * width :],
        own_three[:, 2 * width :],
        own_upward,
        own_down,
        own_norms[:3],
        own_norms[3:],
    )


def solution(mesh):
    rows = P(None, "fsdp", "seq", None)
    weight = P(ALL, None)
    in_specs = (
        rows,
        rows,
        rows,
        P(None, "fsdp", None),
        P(None, "fsdp", None),
        P(None, "fsdp"),
    ) + (weight,) * 7 + (P(None, ALL),) * 2
    out_specs = (rows, rows, rows) + (weight,) * 7 + (P(None, ALL),) * 2
    return jax.shard_map(
        per_device, mesh=mesh, in_specs=in_specs, out_specs=out_specs, check_vma=False
    )
```

```python
import functools

import jax
import jax.numpy as jnp
from jax import lax
from jax.experimental import pallas as pl
from jax.experimental.pallas import tpu as pltpu
from jax.sharding import PartitionSpec as P

H = 16
HD = 64
TILE = 128
BLOCK = 256

scale_factor = 0.125
residual_weight = 36.0**0.25
norm_epsilon = 1e-05
masked_score = -1e30
ALL = ("seq", "fsdp")
f32 = jnp.float32
bf16 = jnp.bfloat16
MESH = pl.DeviceIdType.MESH


def dot_nn(a, b):
    return lax.dot_general(a, b, (((1,), (0,)), ((), ())), preferred_element_type=f32)


def dot_nt(a, b):
    return lax.dot_general(a, b, (((1,), (1,)), ((), ())), preferred_element_type=f32)


def dot_tn(a, b):
    return lax.dot_general(a, b, (((0,), (0,)), ((), ())), preferred_element_type=f32)


def norm_stats(incoming):
    row_mean = jnp.mean(incoming, -1, keepdims=True)
    centred = incoming - row_mean
    variance = jnp.mean(centred * centred, -1, keepdims=True)
    return centred, lax.rsqrt(variance + norm_epsilon)


def layer_norm(incoming, gain_row, bias_row):
    centred, inverse = norm_stats(incoming)
    return centred * inverse * gain_row + bias_row


def layer_norm_back(incoming, gain_row, upstream):
    centred, inverse = norm_stats(incoming)
    normal = centred * inverse
    grad_bias = jnp.sum(upstream, 0)
    grad_gain = jnp.sum(upstream * normal, 0)
    scaled = upstream * gain_row
    grad = inverse * (
        scaled
        - jnp.mean(scaled, -1, keepdims=True)
        - normal * jnp.mean(scaled * normal, -1, keepdims=True)
    )
    return grad, grad_gain, grad_bias


def ancestors(parent_ids):
    segment_ids = jnp.arange(parent_ids.shape[0], dtype=jnp.int32)
    hop = (parent_ids[:, None] == segment_ids[None, :]).astype(f32)
    reach = jnp.maximum(hop, (segment_ids[:, None] == segment_ids[None, :]).astype(f32))
    steps = 1
    while steps < parent_ids.shape[0]:
        reach = jnp.minimum(jnp.dot(reach, reach, precision=lax.Precision.HIGHEST), 1.0)
        steps *= 2
    return reach


def tree_bias(tile_segments, parent_ids, block):
    tiles = tile_segments.shape[0]
    onehot = (
        tile_segments[:, None] == jnp.arange(parent_ids.shape[0], dtype=jnp.int32)[None, :]
    ).astype(f32)
    high = lax.Precision.HIGHEST
    related = jnp.dot(
        jnp.dot(onehot, ancestors(parent_ids), precision=high), onehot.T, precision=high
    )
    bias = jnp.where(related > 0.5, 0.0, masked_score)
    per = block // TILE
    blocks = tiles // per
    bias = bias.reshape(blocks, per, blocks, per).transpose(2, 0, 3, 1)
    return jnp.repeat(bias, TILE, axis=3)


def head_masks(shape, heads):
    lane = lax.broadcasted_iota(jnp.int32, shape, 1)
    return [(lane >= h * HD) & (lane < (h + 1) * HD) for h in range(heads)]


def keep_head(value, mask, heads):
    return value if heads == 1 else jnp.where(mask, value, jnp.zeros_like(value))


def greet(peers):
    barrier = pltpu.get_barrier_semaphore()
    for peer in peers:
        pl.semaphore_signal(barrier, inc=1, device_id=peer, device_id_type=MESH)
    pl.semaphore_wait(barrier, len(peers))


def peer_at(step):
    count = lax.axis_size("seq")
    return lax.rem(lax.axis_index("seq") + step, count)


def rows_at(i, count):
    return pl.ds(pl.multiple_of(i * count, count), count)


def cut_heads(rows_ref, m, parts, blocks_ref):
    seq, part = blocks_ref.shape[2], blocks_ref.shape[4]
    for p in range(parts):
        for s in range(seq):
            first = (p * seq + s) * part
            blocks_ref[m, p, s] = rows_ref[m, :, first : first + part]


def join_heads(blocks_ref, m, parts, rows_ref):
    seq, part = blocks_ref.shape[2], blocks_ref.shape[4]
    for p in range(parts):
        for s in range(seq):
            first = (p * seq + s) * part
            rows_ref[m, :, first : first + part] = blocks_ref[m, p, s]


def to_peer(source_ref, target_ref, send, receive, m, step):
    rows = source_ref.shape[3]
    return pltpu.make_async_remote_copy(
        src_ref=source_ref.at[m, :, peer_at(step)],
        dst_ref=target_ref.at[m, :, rows_at(lax.axis_index("seq"), rows)],
        send_sem=send.at[m, step],
        recv_sem=receive.at[m, step],
        device_id={"seq": peer_at(step)},
        device_id_type=MESH,
    )


def to_self(source_ref, target_ref, sem, m):
    rows = source_ref.shape[3]
    me = lax.axis_index("seq")
    return pltpu.make_async_copy(
        source_ref.at[m, :, me], target_ref.at[m, :, rows_at(me, rows)], sem.at[m, 0]
    )


def send_blocks(source_ref, target_ref, send, receive, m):
    for step in range(1, lax.axis_size("seq")):
        to_peer(source_ref, target_ref, send, receive, m, step).start()
    to_self(source_ref, target_ref, send, m).start()


def take_blocks(source_ref, target_ref, send, receive, m):
    for step in range(1, lax.axis_size("seq")):
        to_peer(source_ref, target_ref, send, receive, m, step).wait_recv()
    to_self(source_ref, target_ref, send, m).wait()


def home_copy(source_ref, target_ref, send, receive, m, place):
    rows = target_ref.shape[3]
    me = lax.axis_index("seq")
    count = lax.axis_size("seq")
    step = lax.rem(place - me + count, count)
    return pltpu.make_async_remote_copy(
        src_ref=source_ref.at[m, :, rows_at(place, rows)],
        dst_ref=target_ref.at[m, :, me],
        send_sem=send.at[m, step],
        recv_sem=receive.at[m, step],
        device_id={"seq": place},
        device_id_type=MESH,
    )


def home_self(source_ref, target_ref, sem, m):
    rows = target_ref.shape[3]
    me = lax.axis_index("seq")
    return pltpu.make_async_copy(
        source_ref.at[m, :, rows_at(me, rows)], target_ref.at[m, :, me], sem.at[m, 0]
    )


def send_home(source_ref, target_ref, send, receive, m, place):
    me = lax.axis_index("seq")

    @pl.when(place != me)
    def _():
        home_copy(source_ref, target_ref, send, receive, m, place).start()

    @pl.when(place == me)
    def _():
        home_self(source_ref, target_ref, send, m).start()


def take_home(source_ref, target_ref, send, receive, m):
    for step in range(1, lax.axis_size("seq")):
        home_copy(source_ref, target_ref, send, receive, m, peer_at(step)).wait()
    home_self(source_ref, target_ref, send, m).wait()


def self_forward_kernel(
    heads, block, rows_ref, bias_ref, qkv_ref, out_ref, lse_ref, attended_ref,
    cut, back, queries, values_t, send_in, take_in, send_out, take_out,
):
    micro, _, length, width = qkv_ref.shape
    seq = lax.axis_size("seq")
    blocks = length // block
    per = block // TILE
    place_rows = length // seq
    masks = head_masks((block, width), heads)
    greet([{"seq": peer_at(step)} for step in range(1, seq)])

    def launch(m, carry):
        cut_heads(rows_ref, m, 3, cut)

        @pl.when(m < 2)
        def _():
            send_blocks(cut, qkv_ref, send_in, take_in, m)

        return carry

    lax.fori_loop(0, micro, launch, 0)
    key_place = lax.broadcasted_iota(jnp.int32, (block, block), 0)
    query_place = lax.broadcasted_iota(jnp.int32, (block, block), 1)
    causal = key_place <= query_place

    def one_micro(m, carry):
        take_blocks(cut, qkv_ref, send_in, take_in, m)

        @pl.when(m + 2 < micro)
        def _():
            send_blocks(cut, qkv_ref, send_in, take_in, m + 2)

        def prepare(i, carry):
            rows = rows_at(i, block)
            q = qkv_ref[m, 0, rows, :].astype(f32) * scale_factor
            for h in range(heads):
                queries[h, rows, :] = keep_head(q, masks[h], heads).astype(bf16)
            values_t[i] = jnp.transpose(qkv_ref[m, 2, rows, :].astype(f32)).astype(bf16)
            return carry

        lax.fori_loop(0, blocks, prepare, 0)

        def scores_of(i, j, h):
            raw = dot_nt(qkv_ref[m, 1, rows_at(j, block), :], queries[h, rows_at(i, block), :])
            bias = bias_ref[m, j, i]
            return (raw.reshape(per, TILE, block) + bias[:, None, :]).reshape(block, block)

        def query_block(i, carry):
            state = []
            for h in range(heads):
                s = jnp.where(causal, scores_of(i, i, h), masked_score)
                top = jnp.max(s, 0, keepdims=True)
                p = jnp.exp(s - top)
                total = jnp.sum(p, 0, keepdims=True)
                acc = dot_nn(values_t[i][h * HD : (h + 1) * HD], p.astype(bf16))
                state += [top, total, acc]

            def key_block(j, state):
                fresh = []
                for h in range(heads):
                    top, total, acc = state[3 * h : 3 * h + 3]
                    s = scores_of(i, j, h)
                    higher = jnp.maximum(top, jnp.max(s, 0, keepdims=True))
                    shrink = jnp.exp(top - higher)
                    p = jnp.exp(s - higher)
                    total = total * shrink + jnp.sum(p, 0, keepdims=True)
                    acc = acc * shrink + dot_nn(
                        values_t[j][h * HD : (h + 1) * HD], p.astype(bf16)
                    )
                    fresh += [higher, total, acc]
                return tuple(fresh)

            state = lax.fori_loop(0, i, key_block, tuple(state))
            out = jnp.concatenate(
                [state[3 * h + 2] * (1.0 / state[3 * h + 1]) for h in range(heads)], 0
            )
            out_ref[m, 0, rows_at(i, block), :] = jnp.transpose(out).astype(bf16)
            lse_ref[m, i] = jnp.concatenate(
                [state[3 * h] + jnp.log(state[3 * h + 1]) for h in range(heads)], 0
            )
            for sub in range(block // place_rows):
                place = i * (block // place_rows) + sub
                send_home(out_ref, back, send_out, take_out, m, place)
            return carry

        lax.fori_loop(0, blocks, query_block, 0)
        return carry

    lax.fori_loop(0, micro, one_micro, 0)

    def finish(m, carry):
        for step in range(1, seq):
            to_peer(cut, qkv_ref, send_in, take_in, m, step).wait_send()
        take_home(out_ref, back, send_out, take_out, m)
        join_heads(back, m, 1, attended_ref)
        return carry

    lax.fori_loop(0, micro, finish, 0)


def self_forward(projected, bias, seq):
    micro, rows, width = projected.shape
    part = width // 3 // seq
    heads = part // HD
    length = rows * seq
    blocks = length // BLOCK
    whole = pl.BlockSpec(memory_space=pltpu.VMEM)
    sems = pltpu.SemaphoreType.DMA((micro, seq))
    return pl.pallas_call(
        functools.partial(self_forward_kernel, heads, BLOCK),
        in_specs=[whole, whole],
        out_specs=[whole] * 4,
        out_shape=[
            jax.ShapeDtypeStruct((micro, 3, length, part), bf16),
            jax.ShapeDtypeStruct((micro, 1, length, part), bf16),
            jax.ShapeDtypeStruct((micro, blocks, heads, BLOCK), f32),
            jax.ShapeDtypeStruct((micro, rows, width // 3), bf16),
        ],
        scratch_shapes=[
            pltpu.VMEM((micro, 3, seq, rows, part), bf16),
            pltpu.VMEM((micro, 1, seq, rows, part), bf16),
            pltpu.VMEM((heads, length, part), bf16),
            pltpu.VMEM((blocks, part, BLOCK), bf16),
            sems,
            sems,
            sems,
            sems,
        ],
        compiler_params=pltpu.CompilerParams(
            vmem_limit_bytes=50 << 20, collective_id=1, has_side_effects=True
        ),
        name="self_forward",
    )(projected, bias)


def self_backward_kernel(
    heads, block, rows_ref, qkv_ref, bias_ref, out_ref, lse_ref, grad_ref,
    cut, gout, grads, back, queries, keys_h, gouts, delta, grad_q,
    send_in, take_in, send_out, take_out,
):
    micro, _, length, width = qkv_ref.shape
    seq = lax.axis_size("seq")
    blocks = length // block
    per = block // TILE
    place_rows = length // seq
    masks = head_masks((block, width), heads)
    lane = lax.broadcasted_iota(jnp.int32, (8, width), 1)
    first_lane = lax.broadcasted_iota(jnp.int32, (8, width), 0) * HD
    pick = jnp.where((lane >= first_lane) & (lane < first_lane + HD), 1.0, 0.0)
    greet([{"seq": peer_at(step)} for step in range(1, seq)])

    def launch(m, carry):
        cut_heads(rows_ref, m, 1, cut)
        send_blocks(cut, gout, send_in, take_in, m)
        return carry

    lax.fori_loop(0, micro, launch, 0)
    key_place = lax.broadcasted_iota(jnp.int32, (block, block), 0)
    query_place = lax.broadcasted_iota(jnp.int32, (block, block), 1)
    causal = key_place <= query_place

    def one_micro(m, carry):
        take_blocks(cut, gout, send_in, take_in, m)

        def prepare(i, carry):
            rows = rows_at(i, block)
            q = qkv_ref[m, 0, rows, :].astype(f32) * scale_factor
            k = qkv_ref[m, 1, rows, :].astype(f32)
            g = gout[m, 0, rows, :].astype(f32)
            for h in range(heads):
                queries[h, rows, :] = keep_head(q, masks[h], heads).astype(bf16)
                keys_h[h, rows, :] = keep_head(k, masks[h], heads).astype(bf16)
                gouts[h, rows, :] = keep_head(g, masks[h], heads).astype(bf16)
            delta[i] = lax.dot_general(
                pick,
                g * out_ref[m, 0, rows, :].astype(f32),
                (((1,), (1,)), ((), ())),
                precision=lax.Precision.HIGHEST,
                preferred_element_type=f32,
            )
            grad_q[rows, :] = jnp.zeros((block, width), f32)
            return carry

        lax.fori_loop(0, blocks, prepare, 0)

        def key_block(j, carry):
            krows = rows_at(j, block)

            def pair(i, grad_k, grad_v, diagonal):
                rows = rows_at(i, block)
                bias = bias_ref[m, j, i]
                gq = grad_q[rows, :]
                for h in range(heads):
                    raw = dot_nt(qkv_ref[m, 1, krows, :], queries[h, rows, :])
                    shift = bias - lse_ref[m, i, h : h + 1, :]
                    s = (raw.reshape(per, TILE, block) + shift[:, None, :]).reshape(block, block)
                    if diagonal:
                        s = jnp.where(causal, s, masked_score)
                    p = jnp.exp(s)
                    gp = dot_nt(qkv_ref[m, 2, krows, :], gouts[h, rows, :])
                    gs = (p * (gp - delta[i, h : h + 1, :])).astype(bf16)
                    grad_v = grad_v + dot_nn(p.astype(bf16), gouts[h, rows, :])
                    grad_k = grad_k + dot_nn(gs, queries[h, rows, :])
                    gq = gq + dot_tn(gs, keys_h[h, krows, :])
                grad_q[rows, :] = gq
                return grad_k, grad_v

            zero = jnp.zeros((block, width), f32)
            state = pair(j, zero, zero, True)
            state = lax.fori_loop(
                j + 1, blocks, lambda i, s: pair(i, s[0], s[1], False), state
            )
            grads[m, 0, krows, :] = (grad_q[krows, :] * scale_factor).astype(bf16)
            grads[m, 1, krows, :] = state[0].astype(bf16)
            grads[m, 2, krows, :] = state[1].astype(bf16)
            for sub in range(block // place_rows):
                place = j * (block // place_rows) + sub
                send_home(grads, back, send_out, take_out, m, place)
            return carry

        lax.fori_loop(0, blocks, key_block, 0)
        return carry

    lax.fori_loop(0, micro, one_micro, 0)

    def finish(m, carry):
        for step in range(1, seq):
            to_peer(cut, gout, send_in, take_in, m, step).wait_send()
        take_home(grads, back, send_out, take_out, m)
        join_heads(back, m, 3, grad_ref)
        return carry

    lax.fori_loop(0, micro, finish, 0)


def self_backward(grad_attended, qkv, bias, out, lse, seq):
    micro, rows, width = grad_attended.shape
    length, part = qkv.shape[2:]
    heads = part // HD
    blocks = length // BLOCK
    whole = pl.BlockSpec(memory_space=pltpu.VMEM)
    sems = pltpu.SemaphoreType.DMA((micro, seq))
    return pl.pallas_call(
        functools.partial(self_backward_kernel, heads, BLOCK),
        in_specs=[whole] * 5,
        out_specs=whole,
        out_shape=jax.ShapeDtypeStruct((micro, rows, 3 * width), bf16),
        scratch_shapes=[
            pltpu.VMEM((micro, 1, seq, rows, part), bf16),
            pltpu.VMEM((micro, 1, length, part), bf16),
            pltpu.VMEM((micro, 3, length, part), bf16),
            pltpu.VMEM((micro, 3, seq, rows, part), bf16),
            pltpu.VMEM((heads, length, part), bf16),
            pltpu.VMEM((heads, length, part), bf16),
            pltpu.VMEM((heads, length, part), bf16),
            pltpu.VMEM((blocks, 8, BLOCK), f32),
            pltpu.VMEM((length, part), f32),
            sems,
            sems,
            sems,
            sems,
        ],
        compiler_params=pltpu.CompilerParams(
            vmem_limit_bytes=50 << 20, collective_id=2, has_side_effects=True
        ),
        name="self_backward",
    )(grad_attended, qkv, bias, out, lse)


def scatter_places():
    s, f = lax.axis_index("seq"), lax.axis_index("fsdp")
    z, y = s // 2, f // 2
    return z, s - 2 * z, y, f - 2 * y, lax.axis_size("seq") // 2, lax.axis_size("fsdp") // 2


def scatter_peers():
    z, x, y, c, z_size, y_size = scatter_places()
    peers = [{"fsdp": 2 * y + 1 - c}, {"seq": 2 * z + 1 - x}]
    peers += [{"fsdp": 2 * lax.rem(y + k, y_size) + c} for k in range(1, y_size)]
    peers += [{"seq": 2 * lax.rem(z + k, z_size) + x} for k in range(1, z_size)]
    return peers


def scatter_shapes(blocks, x_first):
    z_size, _, y_size, _, rows, columns = blocks.shape
    if x_first:
        first, second = (1, y_size), (y_size - 1,)
    else:
        first, second = (y_size - 1, 2), (1,)
    kind = blocks.dtype
    return [
        pltpu.VMEM((z_size, 2, y_size, rows, columns), kind),
        pltpu.VMEM((z_size, 2, y_size, rows, columns), kind),
        pltpu.VMEM((z_size,) + first + (rows, columns), kind),
        pltpu.VMEM((z_size,) + second + (rows, columns), kind),
        pltpu.VMEM((z_size - 1, rows, columns), kind),
    ]


def scatter_sems(count, z_size, y_size):
    pair = pltpu.SemaphoreType.DMA((count, z_size))
    triple = pltpu.SemaphoreType.DMA((count, z_size, max(1, y_size - 1)))
    return [pair, pair, pair, triple, triple, triple, triple, pair, pair]


def add_into(target, source):
    target[...] = target[...] + source[...]


def scatter_steps(kinds, sources, outs, buffers, sems):
    z, x, y, c, z_size, y_size = scatter_places()
    local, core_s, core_r, first_s, first_r, second_s, second_r, last_s, last_r = sems
    count = len(sources)

    def to_z(t):
        return lax.rem(z + 1 + t, z_size)

    def remote(source, target, send, receive, peer):
        return pltpu.make_async_remote_copy(
            src_ref=source,
            dst_ref=target,
            send_sem=send,
            recv_sem=receive,
            device_id=peer,
            device_id_type=MESH,
        )

    def own_copy(a, t):
        return pltpu.make_async_copy(
            sources[a].at[to_z(t), :, :, c], buffers[a][0].at[t], local.at[a, t]
        )

    def core_copy(a, t):
        return remote(
            sources[a].at[to_z(t), :, :, 1 - c],
            buffers[a][1].at[t],
            core_s.at[a, t],
            core_r.at[a, t],
            {"fsdp": 2 * y + 1 - c},
        )

    def x_peer():
        return {"seq": 2 * z + 1 - x}

    def y_place(k):
        return lax.rem(y + k, y_size)

    def y_peer(k):
        return {"fsdp": 2 * y_place(k) + c}

    def first_copies(a, t):
        own, _, first, _, _ = buffers[a]
        if kinds[a]:
            sends = [(own.at[t, 1 - x], x_peer())]
        else:
            sends = [(own.at[t, :, y_place(k)], y_peer(k)) for k in range(1, y_size)]
        return [
            remote(source, first.at[t, k], first_s.at[a, t, k], first_r.at[a, t, k], peer)
            for k, (source, peer) in enumerate(sends)
        ]

    def second_copies(a, t):
        own, _, _, second, _ = buffers[a]
        if kinds[a]:
            sends = [(own.at[t, x, y_place(k)], y_peer(k)) for k in range(1, y_size)]
        else:
            sends = [(own.at[t, 1 - x, y], x_peer())]
        return [
            remote(source, second.at[t, k], second_s.at[a, t, k], second_r.at[a, t, k], peer)
            for k, (source, peer) in enumerate(sends)
        ]

    def last_copy(a, t):
        own, _, _, _, last = buffers[a]
        return remote(
            own.at[t, x, y],
            last.at[t],
            last_s.at[a, t],
            last_r.at[a, t],
            {"seq": 2 * to_z(t) + x},
        )

    def start_core(t):
        for a in range(count):
            core_copy(a, t).start()
            own_copy(a, t).start()

    def core_step(t):
        for a in range(count):
            core_copy(a, t).wait_recv()
            own_copy(a, t).wait()
            own, core = buffers[a][:2]

            def add(i, carry, own=own, core=core):
                add_into(own.at[t, i // y_size, i % y_size], core.at[t, i // y_size, i % y_size])
                return carry

            lax.fori_loop(0, 2 * y_size, add, 0)
            for copy in first_copies(a, t):
                copy.start()
        if t + 2 < z_size:
            start_core(t + 2)

    def first_step(t):
        for a in range(count):
            own, _, first, _, _ = buffers[a]
            for k, copy in enumerate(first_copies(a, t)):
                copy.wait_recv()
                for i in range(y_size if kinds[a] else 2):
                    target = own.at[t, x, i] if kinds[a] else own.at[t, i, y]
                    add_into(target, first.at[t, k, i])
            for copy in second_copies(a, t):
                copy.start()

    def second_step(t):
        for a in range(count):
            own, _, _, second, _ = buffers[a]
            for k, copy in enumerate(second_copies(a, t)):
                copy.wait_recv()
                add_into(own.at[t, x, y], second.at[t, k])
            if t < z_size - 1:
                last_copy(a, t).start()

    def final_step():
        for a in range(count):
            own, _, _, _, last = buffers[a]
            total = own[z_size - 1, x, y].astype(f32)
            for t in range(z_size - 1):
                last_copy(a, t).wait()
                total = total + last[t].astype(f32)
            outs[a][...] = total
            for t in range(z_size):
                core_copy(a, t).wait_send()
                for copy in first_copies(a, t) + second_copies(a, t):
                    copy.wait_send()

    def opening():
        start_core(0)
        if z_size > 1:
            start_core(1)

    steps = [opening]
    for t in range(z_size + 2):
        if t < z_size:
            steps.append(functools.partial(core_step, t))
        if 0 <= t - 1 < z_size:
            steps.append(functools.partial(first_step, t - 1))
        if 0 <= t - 2 < z_size:
            steps.append(functools.partial(second_step, t - 2))
    steps.append(final_step)
    return steps


def scatter_kernel(kinds, *refs):
    count = len(kinds)
    sources, outs, rest = refs[:count], refs[count : 2 * count], refs[2 * count :]
    buffers = [rest[5 * a : 5 * a + 5] for a in range(count)]
    greet(scatter_peers())
    for step in scatter_steps(kinds, sources, outs, buffers, rest[5 * count :]):
        step()


def scatter_grads(arrays, kinds, z_size, y_size, collective_id):
    blocks = [
        a.reshape(z_size, 2, y_size, 2, a.shape[0] // (4 * z_size * y_size), a.shape[1])
        for a in arrays
    ]
    scratch = []
    for block, kind in zip(blocks, kinds):
        scratch += scatter_shapes(block, kind)
    return pl.pallas_call(
        functools.partial(scatter_kernel, kinds),
        in_specs=[pl.BlockSpec(memory_space=pl.ANY)] * len(arrays),
        out_specs=[pl.BlockSpec(memory_space=pltpu.VMEM)] * len(arrays),
        out_shape=[jax.ShapeDtypeStruct(b.shape[4:], f32) for b in blocks],
        scratch_shapes=scratch + scatter_sems(len(arrays), z_size, y_size),
        compiler_params=pltpu.CompilerParams(
            vmem_limit_bytes=60 << 20, collective_id=collective_id, has_side_effects=True
        ),
        name="scatter_grads",
    )(*blocks)


def cross_forward_kernel(lengths_ref, q_ref, k_ref, v_ref, out_ref, lse_ref):
    count, width = k_ref.shape[1], k_ref.shape[2]
    rows = q_ref.shape[1]
    heads = width // HD
    masks = head_masks((rows, width), heads)
    valid = (
        lax.broadcasted_iota(jnp.int32, (count, rows), 0) < lengths_ref[pl.program_id(0)]
    )
    q = q_ref[0].astype(f32) * scale_factor
    values_t = jnp.transpose(v_ref[0].astype(f32)).astype(bf16)
    outs, lses = [], []
    for h in range(heads):
        s = dot_nt(k_ref[0], keep_head(q, masks[h], heads).astype(bf16))
        s = jnp.where(valid, s, masked_score)
        m = jnp.max(s, 0, keepdims=True)
        p = jnp.exp(s - m)
        total = jnp.sum(p, 0, keepdims=True)
        out = dot_nn(values_t[h * HD : (h + 1) * HD], p.astype(bf16))
        outs.append(out * (1.0 / total))
        lses.append(m + jnp.log(total))
    out_ref[0] = jnp.transpose(jnp.concatenate(outs, 0)).astype(bf16)
    lse_ref[0, 0] = jnp.concatenate(lses, 0)


def cross_forward(lengths, queries, pairs):
    micro, rows, width = queries.shape
    count = pairs.shape[1]
    groups = width // 128
    return pl.pallas_call(
        cross_forward_kernel,
        grid=(micro, groups),
        in_specs=[
            pl.BlockSpec(memory_space=pltpu.SMEM),
            pl.BlockSpec((1, rows, 128), lambda m, g: (m, 0, g)),
            pl.BlockSpec((1, count, 128), lambda m, g: (m, 0, g)),
            pl.BlockSpec((1, count, 128), lambda m, g: (m, 0, g + groups)),
        ],
        out_specs=[
            pl.BlockSpec((1, rows, 128), lambda m, g: (m, 0, g)),
            pl.BlockSpec((1, 1, 2, rows), lambda m, g: (m, g, 0, 0)),
        ],
        out_shape=[
            jax.ShapeDtypeStruct((micro, rows, width), bf16),
            jax.ShapeDtypeStruct((micro, groups, 2, rows), f32),
        ],
        compiler_params=pltpu.CompilerParams(vmem_limit_bytes=32 << 20),
        name="cross_forward",
    )(lengths, queries, pairs, pairs)


def cross_backward_kernel(
    lengths_ref, q_ref, k_ref, v_ref, out_ref, lse_ref, gout_ref, gq_ref, gk_ref, gv_ref
):
    count, width = k_ref.shape[1], k_ref.shape[2]
    rows = q_ref.shape[1]
    heads = width // HD
    masks = head_masks((rows, width), heads)
    key_masks = head_masks((count, width), heads)
    valid = (
        lax.broadcasted_iota(jnp.int32, (count, rows), 0) < lengths_ref[pl.program_id(0)]
    )
    lane = lax.broadcasted_iota(jnp.int32, (8, width), 1)
    row = lax.broadcasted_iota(jnp.int32, (8, width), 0)
    pick = jnp.where((lane >= row * HD) & (lane < (row + 1) * HD), 1.0, 0.0)
    q = q_ref[0].astype(f32) * scale_factor
    g = gout_ref[0].astype(f32)
    k = k_ref[0].astype(f32)
    delta = lax.dot_general(
        pick,
        g * out_ref[0].astype(f32),
        (((1,), (1,)), ((), ())),
        precision=lax.Precision.HIGHEST,
        preferred_element_type=f32,
    )
    grad_q = jnp.zeros((rows, width), f32)
    grad_k = jnp.zeros((count, width), f32)
    grad_v = jnp.zeros((count, width), f32)
    for h in range(heads):
        qh = keep_head(q, masks[h], heads).astype(bf16)
        gh = keep_head(g, masks[h], heads).astype(bf16)
        kh = keep_head(k, key_masks[h], heads).astype(bf16)
        s = dot_nt(k_ref[0], qh) - lse_ref[0, 0, h : h + 1, :]
        p = jnp.exp(jnp.where(valid, s, masked_score))
        gp = dot_nt(v_ref[0], gh)
        gs = (p * (gp - delta[h : h + 1, :])).astype(bf16)
        grad_v += dot_nn(p.astype(bf16), gh)
        grad_k += dot_nn(gs, qh)
        grad_q += dot_tn(gs, kh)
    gq_ref[0] = (grad_q * scale_factor).astype(bf16)
    gk_ref[0] = grad_k.astype(bf16)
    gv_ref[0] = grad_v.astype(bf16)


def cross_backward(lengths, queries, pairs, out, lse, gout):
    micro, rows, width = queries.shape
    count = pairs.shape[1]
    groups = width // 128
    row_spec = pl.BlockSpec((1, rows, 128), lambda m, g: (m, 0, g))
    key_spec = pl.BlockSpec((1, count, 128), lambda m, g: (m, 0, g))
    value_spec = pl.BlockSpec((1, count, 128), lambda m, g: (m, 0, g + groups))
    lse_spec = pl.BlockSpec((1, 1, 2, rows), lambda m, g: (m, g, 0, 0))
    return pl.pallas_call(
        cross_backward_kernel,
        grid=(micro, groups),
        in_specs=[
            pl.BlockSpec(memory_space=pltpu.SMEM),
            row_spec,
            key_spec,
            value_spec,
            row_spec,
            lse_spec,
            row_spec,
        ],
        out_specs=[row_spec, key_spec, key_spec],
        out_shape=[
            jax.ShapeDtypeStruct((micro, rows, width), bf16),
            jax.ShapeDtypeStruct((micro, count, width), bf16),
            jax.ShapeDtypeStruct((micro, count, width), bf16),
        ],
        compiler_params=pltpu.CompilerParams(vmem_limit_bytes=32 << 20),
        name="cross_backward",
    )(lengths, queries, pairs, pairs, out, lse, gout)


def gelu_parts(v):
    inner = 0.7978845608028654 * (v + 0.044715 * (v * v * v))
    t = jnp.tanh(inner)
    value = 0.5 * v * (1.0 + t)
    slope = 0.5 * (1.0 + t) + 0.5 * v * (1.0 - t * t) * (
        0.7978845608028654 * (1.0 + 3.0 * 0.044715 * (v * v))
    )
    return value, slope


def per_device(
    tokens,
    memory,
    cotangent,
    tile_segment,
    parents,
    memory_lengths,
    self_qkv,
    self_out,
    cross_q,
    cross_kv,
    cross_out,
    ffn_in,
    ffn_out,
    norm_gain,
    norm_bias,
):
    micro, _, row_count, width = tokens.shape
    seq = lax.axis_size("seq")
    total_rows = micro * row_count
    memory_rows = memory.shape[2]

    def gather(shard, axis=0):
        return lax.all_gather(shard, ALL, axis=axis, tiled=True)

    joint_weight = gather(self_qkv)
    norms = gather(jnp.concatenate([norm_gain, norm_bias], 0), 1).astype(f32)
    gain_rows, bias_rows = norms[:3], norms[3:]
    small = gather(jnp.concatenate([self_out, cross_q, cross_kv, cross_out, ffn_in], 1))
    memory_full = lax.all_gather(memory[:, 0], "seq", axis=1, tiled=True)
    down_weight = gather(ffn_out)
    cuts = [0]
    for shard in (self_out, cross_q, cross_kv, cross_out, ffn_in):
        cuts.append(cuts[-1] + shard.shape[1])
    self_output, cross_weight, pair_weight, cross_output, upward_weight = (
        small[:, a:b] for a, b in zip(cuts[:-1], cuts[1:])
    )

    x = tokens.reshape(total_rows, width)
    x32 = x.astype(f32)
    bias = jax.vmap(lambda t, p: tree_bias(t, p, BLOCK))(tile_segment[:, 0], parents[:, 0])
    lengths = memory_lengths[:, 0]

    projected = dot_nn(x, joint_weight).astype(bf16)
    qkv, attended_heads, self_lse, attended = self_forward(
        projected.reshape(micro, row_count, 3 * width), bias, seq
    )
    attended = attended.reshape(total_rows, width)

    mixed_first = residual_weight * x32 + dot_nn(attended, self_output)
    hidden_first = layer_norm(mixed_first, gain_rows[0], bias_rows[0])
    hidden_first_low = hidden_first.astype(bf16)
    cross_query = dot_nn(hidden_first_low, cross_weight).astype(bf16)
    cross_query = cross_query.reshape(micro, row_count, width)
    count = memory_full.shape[1]
    pairs = dot_nn(memory_full.reshape(micro * count, width), pair_weight).astype(bf16)
    pairs = pairs.reshape(micro, count, 2 * width)
    cross_heads, cross_lse = cross_forward(lengths, cross_query, pairs)
    cross_attended = cross_heads.reshape(total_rows, width)
    mixed_second = residual_weight * hidden_first + dot_nn(cross_attended, cross_output)
    hidden_second = layer_norm(mixed_second, gain_rows[1], bias_rows[1])
    hidden_second_low = hidden_second.astype(bf16)
    pre_active = dot_nn(hidden_second_low, upward_weight)
    active = gelu_parts(pre_active)[0].astype(bf16)
    mixed_third = residual_weight * hidden_second + dot_nn(active, down_weight)
    output = layer_norm(mixed_third, gain_rows[2], bias_rows[2]).astype(bf16)

    upstream = cotangent.reshape(total_rows, width).astype(f32)
    grad_third, gain_third, bias_third = layer_norm_back(mixed_third, gain_rows[2], upstream)
    branch_third = grad_third.astype(bf16)
    grad_down = dot_tn(active, branch_third).astype(bf16)
    grad_inner = (gelu_parts(pre_active)[1] * dot_nt(branch_third, down_weight)).astype(bf16)
    grad_upward = dot_tn(hidden_second_low, grad_inner).astype(bf16)

    grad_hidden_second = residual_weight * grad_third + dot_nt(grad_inner, upward_weight)
    grad_second, gain_second, bias_second = layer_norm_back(
        mixed_second, gain_rows[1], grad_hidden_second
    )
    branch_second = grad_second.astype(bf16)
    grad_cross_output = dot_tn(cross_attended, branch_second).astype(bf16)
    grad_cross_attended = dot_nt(branch_second, cross_output).astype(bf16)
    grad_cross_low, grad_keys, grad_values = cross_backward(
        lengths,
        cross_query,
        pairs,
        cross_heads,
        cross_lse,
        grad_cross_attended.reshape(micro, row_count, width),
    )
    memory_partial = jnp.concatenate([grad_keys, grad_values], 2)
    own_pairs = lax.psum_scatter(memory_partial, "seq", scatter_dimension=1, tiled=True)
    grad_cross_low = grad_cross_low.reshape(total_rows, width)
    grad_cross_weight = dot_tn(hidden_first_low, grad_cross_low).astype(bf16)
    grad_hidden_first = residual_weight * grad_second + dot_nt(grad_cross_low, cross_weight)
    grad_first, gain_first, bias_first = layer_norm_back(
        mixed_first, gain_rows[0], grad_hidden_first
    )
    branch_first = grad_first.astype(bf16)
    grad_self_output = dot_tn(attended, branch_first).astype(bf16)
    grad_attended = dot_nt(branch_first, self_output).astype(bf16)
    grad_projected = self_backward(
        grad_attended.reshape(micro, row_count, width), qkv, bias, attended_heads, self_lse, seq
    ).reshape(total_rows, 3 * width)
    grad_joint = dot_tn(x, grad_projected).astype(bf16)
    grad_tokens = (residual_weight * grad_first + dot_nt(grad_projected, joint_weight)).astype(bf16)
    grad_pairs_low = own_pairs.reshape(micro * memory_rows, 2 * width)
    grad_pair_weight = dot_tn(memory.reshape(micro * memory_rows, width), grad_pairs_low)
    grad_memory = dot_nt(grad_pairs_low, pair_weight).astype(bf16)
    norm_grads = jnp.stack(
        [gain_first, gain_second, gain_third, bias_first, bias_second, bias_third]
    )
    devices = seq * lax.axis_size("fsdp")
    norm_blocks = norm_grads.reshape(6, devices, width // devices).transpose(1, 0, 2)
    owned = scatter_grads(
        [
            grad_joint,
            grad_self_output,
            grad_upward,
            grad_pair_weight.astype(bf16),
            grad_cross_weight,
            grad_cross_output,
            grad_down,
            norm_blocks.reshape(6 * devices, width // devices),
        ],
        (True, True, True, False, False, False, False, False),
        seq // 2,
        lax.axis_size("fsdp") // 2,
        3,
    )
    return (
        output.reshape(tokens.shape),
        grad_tokens.reshape(tokens.shape),
        grad_memory.reshape(memory.shape),
        owned[0],
        owned[1],
        owned[4],
        owned[3],
        owned[5],
        owned[2],
        owned[6],
        owned[7][:3],
        owned[7][3:],
    )


def solution(mesh):
    rows = P(None, "fsdp", "seq", None)
    weight = P(ALL, None)
    in_specs = (
        rows,
        rows,
        rows,
        P(None, "fsdp", None),
        P(None, "fsdp", None),
        P(None, "fsdp"),
    ) + (weight,) * 7 + (P(None, ALL),) * 2
    out_specs = (rows, rows, rows) + (weight,) * 7 + (P(None, ALL),) * 2
    return jax.shard_map(
        per_device, mesh=mesh, in_specs=in_specs, out_specs=out_specs, check_vma=False
    )
```

```python
import functools

import jax
import jax.numpy as jnp
from jax import lax
from jax.experimental import pallas as pl
from jax.experimental.pallas import tpu as pltpu
from jax.sharding import PartitionSpec as P

H = 16
HD = 64
TILE = 128
BLOCK = 256
SCATTER_END = 75

scale_factor = 0.125
residual_weight = 36.0**0.25
norm_epsilon = 1e-05
masked_score = -1e30
ALL = ("seq", "fsdp")
f32 = jnp.float32
bf16 = jnp.bfloat16
MESH = pl.DeviceIdType.MESH


def dot_nn(a, b):
    return lax.dot_general(a, b, (((1,), (0,)), ((), ())), preferred_element_type=f32)


def dot_nt(a, b):
    return lax.dot_general(a, b, (((1,), (1,)), ((), ())), preferred_element_type=f32)


def dot_tn(a, b):
    return lax.dot_general(a, b, (((0,), (0,)), ((), ())), preferred_element_type=f32)


def norm_stats(incoming):
    row_mean = jnp.mean(incoming, -1, keepdims=True)
    centred = incoming - row_mean
    variance = jnp.mean(centred * centred, -1, keepdims=True)
    return centred, lax.rsqrt(variance + norm_epsilon)


def layer_norm(incoming, gain_row, bias_row):
    centred, inverse = norm_stats(incoming)
    return centred * inverse * gain_row + bias_row


def layer_norm_back(incoming, gain_row, upstream):
    centred, inverse = norm_stats(incoming)
    normal = centred * inverse
    grad_bias = jnp.sum(upstream, 0)
    grad_gain = jnp.sum(upstream * normal, 0)
    scaled = upstream * gain_row
    grad = inverse * (
        scaled
        - jnp.mean(scaled, -1, keepdims=True)
        - normal * jnp.mean(scaled * normal, -1, keepdims=True)
    )
    return grad, grad_gain, grad_bias


def ancestors(parent_ids):
    segment_ids = jnp.arange(parent_ids.shape[0], dtype=jnp.int32)
    hop = (parent_ids[:, None] == segment_ids[None, :]).astype(f32)
    reach = jnp.maximum(hop, (segment_ids[:, None] == segment_ids[None, :]).astype(f32))
    steps = 1
    while steps < parent_ids.shape[0]:
        reach = jnp.minimum(jnp.dot(reach, reach, precision=lax.Precision.HIGHEST), 1.0)
        steps *= 2
    return reach


def tree_bias(tile_segments, parent_ids, block):
    tiles = tile_segments.shape[0]
    onehot = (
        tile_segments[:, None] == jnp.arange(parent_ids.shape[0], dtype=jnp.int32)[None, :]
    ).astype(f32)
    high = lax.Precision.HIGHEST
    related = jnp.dot(
        jnp.dot(onehot, ancestors(parent_ids), precision=high), onehot.T, precision=high
    )
    bias = jnp.where(related > 0.5, 0.0, masked_score)
    per = block // TILE
    blocks = tiles // per
    bias = bias.reshape(blocks, per, blocks, per).transpose(2, 0, 3, 1)
    return jnp.repeat(bias, TILE, axis=3)


def head_masks(shape, heads):
    lane = lax.broadcasted_iota(jnp.int32, shape, 1)
    return [(lane >= h * HD) & (lane < (h + 1) * HD) for h in range(heads)]


def keep_head(value, mask, heads):
    return value if heads == 1 else jnp.where(mask, value, jnp.zeros_like(value))


def greet(peers):
    barrier = pltpu.get_barrier_semaphore()
    for peer in peers:
        pl.semaphore_signal(barrier, inc=1, device_id=peer, device_id_type=MESH)
    pl.semaphore_wait(barrier, len(peers))


def peer_at(step):
    count = lax.axis_size("seq")
    return lax.rem(lax.axis_index("seq") + step, count)


def rows_at(i, count):
    return pl.ds(pl.multiple_of(i * count, count), count)


def cut_heads(rows_ref, m, parts, blocks_ref):
    seq, part = blocks_ref.shape[2], blocks_ref.shape[4]
    for p in range(parts):
        for s in range(seq):
            first = (p * seq + s) * part
            blocks_ref[m, p, s] = rows_ref[m, :, first : first + part]


def join_heads(blocks_ref, m, parts, rows_ref):
    seq, part = blocks_ref.shape[2], blocks_ref.shape[4]
    for p in range(parts):
        for s in range(seq):
            first = (p * seq + s) * part
            rows_ref[m, :, first : first + part] = blocks_ref[m, p, s]


def to_peer(source_ref, target_ref, send, receive, m, step):
    rows = source_ref.shape[3]
    return pltpu.make_async_remote_copy(
        src_ref=source_ref.at[m, :, peer_at(step)],
        dst_ref=target_ref.at[m, :, rows_at(lax.axis_index("seq"), rows)],
        send_sem=send.at[m, step],
        recv_sem=receive.at[m, step],
        device_id={"seq": peer_at(step)},
        device_id_type=MESH,
    )


def to_self(source_ref, target_ref, sem, m):
    rows = source_ref.shape[3]
    me = lax.axis_index("seq")
    return pltpu.make_async_copy(
        source_ref.at[m, :, me], target_ref.at[m, :, rows_at(me, rows)], sem.at[m, 0]
    )


def send_blocks(source_ref, target_ref, send, receive, m):
    for step in range(1, lax.axis_size("seq")):
        to_peer(source_ref, target_ref, send, receive, m, step).start()
    to_self(source_ref, target_ref, send, m).start()


def take_blocks(source_ref, target_ref, send, receive, m):
    for step in range(1, lax.axis_size("seq")):
        to_peer(source_ref, target_ref, send, receive, m, step).wait_recv()
    to_self(source_ref, target_ref, send, m).wait()


def home_copy(source_ref, target_ref, send, receive, m, place):
    rows = target_ref.shape[3]
    me = lax.axis_index("seq")
    count = lax.axis_size("seq")
    step = lax.rem(place - me + count, count)
    return pltpu.make_async_remote_copy(
        src_ref=source_ref.at[m, :, rows_at(place, rows)],
        dst_ref=target_ref.at[m, :, me],
        send_sem=send.at[m, step],
        recv_sem=receive.at[m, step],
        device_id={"seq": place},
        device_id_type=MESH,
    )


def home_self(source_ref, target_ref, sem, m):
    rows = target_ref.shape[3]
    me = lax.axis_index("seq")
    return pltpu.make_async_copy(
        source_ref.at[m, :, rows_at(me, rows)], target_ref.at[m, :, me], sem.at[m, 0]
    )


def send_home(source_ref, target_ref, send, receive, m, place):
    me = lax.axis_index("seq")

    @pl.when(place != me)
    def _():
        home_copy(source_ref, target_ref, send, receive, m, place).start()

    @pl.when(place == me)
    def _():
        home_self(source_ref, target_ref, send, m).start()


def take_home(source_ref, target_ref, send, receive, m):
    for step in range(1, lax.axis_size("seq")):
        home_copy(source_ref, target_ref, send, receive, m, peer_at(step)).wait()
    home_self(source_ref, target_ref, send, m).wait()


def scatter_places():
    s, f = lax.axis_index("seq"), lax.axis_index("fsdp")
    z, y = s // 2, f // 2
    return z, s - 2 * z, y, f - 2 * y, lax.axis_size("seq") // 2, lax.axis_size("fsdp") // 2


def scatter_peers():
    z, x, y, c, z_size, y_size = scatter_places()
    peers = [{"fsdp": 2 * y + 1 - c}, {"seq": 2 * z + 1 - x}]
    peers += [{"fsdp": 2 * lax.rem(y + k, y_size) + c} for k in range(1, y_size)]
    peers += [{"seq": 2 * lax.rem(z + k, z_size) + x} for k in range(1, z_size)]
    return peers


def scatter_shapes(blocks, x_first):
    z_size, _, y_size, _, rows, columns = blocks.shape
    if x_first:
        first, second = (1, y_size), (y_size - 1,)
    else:
        first, second = (y_size - 1, 2), (1,)
    kind = blocks.dtype
    return [
        pltpu.VMEM((z_size, 2, y_size, rows, columns), kind),
        pltpu.VMEM((z_size, 2, y_size, rows, columns), kind),
        pltpu.VMEM((z_size,) + first + (rows, columns), kind),
        pltpu.VMEM((z_size,) + second + (rows, columns), kind),
        pltpu.VMEM((z_size - 1, rows, columns), kind),
    ]


def scatter_sems(count, z_size, y_size):
    pair = pltpu.SemaphoreType.DMA((count, z_size))
    triple = pltpu.SemaphoreType.DMA((count, z_size, max(1, y_size - 1)))
    return [pair, pair, pair, triple, triple, triple, triple, pair, pair]


def add_into(target, source):
    target[...] = target[...] + source[...]


def scatter_steps(kinds, sources, outs, buffers, sems):
    z, x, y, c, z_size, y_size = scatter_places()
    local, core_s, core_r, first_s, first_r, second_s, second_r, last_s, last_r = sems
    count = len(sources)

    def to_z(t):
        return lax.rem(z + 1 + t, z_size)

    def remote(source, target, send, receive, peer):
        return pltpu.make_async_remote_copy(
            src_ref=source,
            dst_ref=target,
            send_sem=send,
            recv_sem=receive,
            device_id=peer,
            device_id_type=MESH,
        )

    def own_copy(a, t):
        return pltpu.make_async_copy(
            sources[a].at[to_z(t), :, :, c], buffers[a][0].at[t], local.at[a, t]
        )

    def core_copy(a, t):
        return remote(
            sources[a].at[to_z(t), :, :, 1 - c],
            buffers[a][1].at[t],
            core_s.at[a, t],
            core_r.at[a, t],
            {"fsdp": 2 * y + 1 - c},
        )

    def x_peer():
        return {"seq": 2 * z + 1 - x}

    def y_place(k):
        return lax.rem(y + k, y_size)

    def y_peer(k):
        return {"fsdp": 2 * y_place(k) + c}

    def first_copies(a, t):
        own, _, first, _, _ = buffers[a]
        if kinds[a]:
            sends = [(own.at[t, 1 - x], x_peer())]
        else:
            sends = [(own.at[t, :, y_place(k)], y_peer(k)) for k in range(1, y_size)]
        return [
            remote(source, first.at[t, k], first_s.at[a, t, k], first_r.at[a, t, k], peer)
            for k, (source, peer) in enumerate(sends)
        ]

    def second_copies(a, t):
        own, _, _, second, _ = buffers[a]
        if kinds[a]:
            sends = [(own.at[t, x, y_place(k)], y_peer(k)) for k in range(1, y_size)]
        else:
            sends = [(own.at[t, 1 - x, y], x_peer())]
        return [
            remote(source, second.at[t, k], second_s.at[a, t, k], second_r.at[a, t, k], peer)
            for k, (source, peer) in enumerate(sends)
        ]

    def last_copy(a, t):
        own, _, _, _, last = buffers[a]
        return remote(
            own.at[t, x, y],
            last.at[t],
            last_s.at[a, t],
            last_r.at[a, t],
            {"seq": 2 * to_z(t) + x},
        )

    def start_core(t):
        for a in range(count):
            core_copy(a, t).start()
            own_copy(a, t).start()

    def core_step(t):
        for a in range(count):
            core_copy(a, t).wait_recv()
            own_copy(a, t).wait()
            own, core = buffers[a][:2]

            def add(i, carry, own=own, core=core):
                add_into(own.at[t, i // y_size, i % y_size], core.at[t, i // y_size, i % y_size])
                return carry

            lax.fori_loop(0, 2 * y_size, add, 0)
            for copy in first_copies(a, t):
                copy.start()
        if t + 2 < z_size:
            start_core(t + 2)

    def first_step(t):
        for a in range(count):
            own, _, first, _, _ = buffers[a]
            for k, copy in enumerate(first_copies(a, t)):
                copy.wait_recv()
                for i in range(y_size if kinds[a] else 2):
                    target = own.at[t, x, i] if kinds[a] else own.at[t, i, y]
                    add_into(target, first.at[t, k, i])
            for copy in second_copies(a, t):
                copy.start()

    def second_step(t):
        for a in range(count):
            own, _, _, second, _ = buffers[a]
            for k, copy in enumerate(second_copies(a, t)):
                copy.wait_recv()
                add_into(own.at[t, x, y], second.at[t, k])
            if t < z_size - 1:
                last_copy(a, t).start()

    def final_step():
        for a in range(count):
            own, _, _, _, last = buffers[a]
            total = own[z_size - 1, x, y].astype(f32)
            for t in range(z_size - 1):
                last_copy(a, t).wait()
                total = total + last[t].astype(f32)
            outs[a][...] = total
            for t in range(z_size):
                core_copy(a, t).wait_send()
                for copy in first_copies(a, t) + second_copies(a, t):
                    copy.wait_send()

    def opening():
        start_core(0)
        if z_size > 1:
            start_core(1)

    steps = [opening]
    for t in range(z_size + 2):
        if t < z_size:
            steps.append(functools.partial(core_step, t))
        if 0 <= t - 1 < z_size:
            steps.append(functools.partial(first_step, t - 1))
        if 0 <= t - 2 < z_size:
            steps.append(functools.partial(second_step, t - 2))
    steps.append(final_step)
    return steps


def scatter_kernel(kinds, *refs):
    count = len(kinds)
    sources, outs, rest = refs[:count], refs[count : 2 * count], refs[2 * count :]
    buffers = [rest[5 * a : 5 * a + 5] for a in range(count)]
    greet(scatter_peers())
    for step in scatter_steps(kinds, sources, outs, buffers, rest[5 * count :]):
        step()


def scatter_blocks(arrays, z_size, y_size):
    return [
        a.reshape(z_size, 2, y_size, 2, a.shape[0] // (4 * z_size * y_size), a.shape[1])
        for a in arrays
    ]


def scatter_grads(arrays, kinds, z_size, y_size, collective_id):
    blocks = scatter_blocks(arrays, z_size, y_size)
    scratch = []
    for block, kind in zip(blocks, kinds):
        scratch += scatter_shapes(block, kind)
    return pl.pallas_call(
        functools.partial(scatter_kernel, kinds),
        in_specs=[pl.BlockSpec(memory_space=pl.ANY)] * len(arrays),
        out_specs=[pl.BlockSpec(memory_space=pltpu.VMEM)] * len(arrays),
        out_shape=[jax.ShapeDtypeStruct(b.shape[4:], f32) for b in blocks],
        scratch_shapes=scratch + scatter_sems(len(arrays), z_size, y_size),
        compiler_params=pltpu.CompilerParams(
            vmem_limit_bytes=60 << 20, collective_id=collective_id, has_side_effects=True
        ),
        name="scatter_grads",
    )(*blocks)


def self_forward_kernel(
    heads, block, rows_ref, bias_ref, qkv_ref, out_ref, lse_ref, attended_ref,
    cut, back, queries, values_t, send_in, take_in, send_out, take_out,
):
    micro, _, length, width = qkv_ref.shape
    seq = lax.axis_size("seq")
    blocks = length // block
    per = block // TILE
    place_rows = length // seq
    masks = head_masks((block, width), heads)
    greet([{"seq": peer_at(step)} for step in range(1, seq)])

    def launch(m, carry):
        cut_heads(rows_ref, m, 3, cut)

        @pl.when(m < 2)
        def _():
            send_blocks(cut, qkv_ref, send_in, take_in, m)

        return carry

    lax.fori_loop(0, micro, launch, 0)
    key_place = lax.broadcasted_iota(jnp.int32, (block, block), 0)
    query_place = lax.broadcasted_iota(jnp.int32, (block, block), 1)
    causal = key_place <= query_place

    def one_micro(m, carry):
        take_blocks(cut, qkv_ref, send_in, take_in, m)

        @pl.when(m + 2 < micro)
        def _():
            send_blocks(cut, qkv_ref, send_in, take_in, m + 2)

        def prepare(i, carry):
            rows = rows_at(i, block)
            q = qkv_ref[m, 0, rows, :].astype(f32) * scale_factor
            for h in range(heads):
                queries[h, rows, :] = keep_head(q, masks[h], heads).astype(bf16)
            values_t[i] = jnp.transpose(qkv_ref[m, 2, rows, :].astype(f32)).astype(bf16)
            return carry

        lax.fori_loop(0, blocks, prepare, 0)

        def scores_of(i, j, h):
            raw = dot_nt(qkv_ref[m, 1, rows_at(j, block), :], queries[h, rows_at(i, block), :])
            bias = bias_ref[m, j, i]
            return (raw.reshape(per, TILE, block) + bias[:, None, :]).reshape(block, block)

        def query_block(i, carry):
            state = []
            for h in range(heads):
                s = jnp.where(causal, scores_of(i, i, h), masked_score)
                top = jnp.max(s, 0, keepdims=True)
                p = jnp.exp(s - top)
                total = jnp.sum(p, 0, keepdims=True)
                acc = dot_nn(values_t[i][h * HD : (h + 1) * HD], p.astype(bf16))
                state += [top, total, acc]

            def key_block(j, state):
                fresh = []
                for h in range(heads):
                    top, total, acc = state[3 * h : 3 * h + 3]
                    s = scores_of(i, j, h)
                    higher = jnp.maximum(top, jnp.max(s, 0, keepdims=True))
                    shrink = jnp.exp(top - higher)
                    p = jnp.exp(s - higher)
                    total = total * shrink + jnp.sum(p, 0, keepdims=True)
                    acc = acc * shrink + dot_nn(
                        values_t[j][h * HD : (h + 1) * HD], p.astype(bf16)
                    )
                    fresh += [higher, total, acc]
                return tuple(fresh)

            state = lax.fori_loop(0, i, key_block, tuple(state))
            out = jnp.concatenate(
                [state[3 * h + 2] * (1.0 / state[3 * h + 1]) for h in range(heads)], 0
            )
            out_ref[m, 0, rows_at(i, block), :] = jnp.transpose(out).astype(bf16)
            lse_ref[m, i] = jnp.concatenate(
                [state[3 * h] + jnp.log(state[3 * h + 1]) for h in range(heads)], 0
            )
            for sub in range(block // place_rows):
                place = i * (block // place_rows) + sub
                send_home(out_ref, back, send_out, take_out, m, place)
            return carry

        lax.fori_loop(0, blocks, query_block, 0)
        return carry

    lax.fori_loop(0, micro, one_micro, 0)

    def finish(m, carry):
        for step in range(1, seq):
            to_peer(cut, qkv_ref, send_in, take_in, m, step).wait_send()
        take_home(out_ref, back, send_out, take_out, m)
        join_heads(back, m, 1, attended_ref)
        return carry

    lax.fori_loop(0, micro, finish, 0)


def self_forward(projected, bias, seq):
    micro, rows, width = projected.shape
    part = width // 3 // seq
    heads = part // HD
    length = rows * seq
    blocks = length // BLOCK
    whole = pl.BlockSpec(memory_space=pltpu.VMEM)
    sems = pltpu.SemaphoreType.DMA((micro, seq))
    return pl.pallas_call(
        functools.partial(self_forward_kernel, heads, BLOCK),
        in_specs=[whole, whole],
        out_specs=[whole] * 4,
        out_shape=[
            jax.ShapeDtypeStruct((micro, 3, length, part), bf16),
            jax.ShapeDtypeStruct((micro, 1, length, part), bf16),
            jax.ShapeDtypeStruct((micro, blocks, heads, BLOCK), f32),
            jax.ShapeDtypeStruct((micro, rows, width // 3), bf16),
        ],
        scratch_shapes=[
            pltpu.VMEM((micro, 3, seq, rows, part), bf16),
            pltpu.VMEM((micro, 1, seq, rows, part), bf16),
            pltpu.VMEM((heads, length, part), bf16),
            pltpu.VMEM((blocks, part, BLOCK), bf16),
            sems,
            sems,
            sems,
            sems,
        ],
        compiler_params=pltpu.CompilerParams(
            vmem_limit_bytes=50 << 20, collective_id=1, has_side_effects=True
        ),
        name="self_forward",
    )(projected, bias)


def spread(steps, first, last):
    return [(first + k * (last - first) // max(1, len(steps) - 1), s) for k, s in enumerate(steps)]


def run_slot(placed, slot):
    for at, step in placed:
        pl.when(slot == at)(step)


def both_peers():
    _, _, y, c, _, y_size = scatter_places()
    peers = [{"seq": peer_at(step)} for step in range(1, lax.axis_size("seq"))]
    peers += [{"fsdp": 2 * y + 1 - c}]
    return peers + [{"fsdp": 2 * lax.rem(y + k, y_size) + c} for k in range(1, y_size)]


def self_backward_kernel(heads, block, kinds, *refs):
    count = len(kinds)
    rows_ref, qkv_ref, bias_ref, out_ref, lse_ref = refs[:5]
    sources, refs = refs[5 : 5 + count], refs[5 + count :]
    grad_ref, owned, refs = refs[0], refs[1 : 1 + count], refs[1 + count :]
    cut, gout, grads, back, queries, keys_h, gouts, delta, grad_q = refs[:9]
    send_in, take_in, send_out, take_out = refs[9:13]
    buffers = [refs[13 + 5 * a : 18 + 5 * a] for a in range(count)]
    scatter = scatter_steps(kinds, sources, owned, buffers, refs[13 + 5 * count :])
    micro, _, length, width = qkv_ref.shape
    seq = lax.axis_size("seq")
    blocks = length // block
    per = block // TILE
    place_rows = length // seq
    masks = head_masks((block, width), heads)
    lane = lax.broadcasted_iota(jnp.int32, (8, width), 1)
    first_lane = lax.broadcasted_iota(jnp.int32, (8, width), 0) * HD
    pick = jnp.where((lane >= first_lane) & (lane < first_lane + HD), 1.0, 0.0)
    placed = spread(scatter[1:-1], 1, SCATTER_END * micro * blocks // 100)
    greet(both_peers())

    def launch(m, carry):
        cut_heads(rows_ref, m, 1, cut)
        send_blocks(cut, gout, send_in, take_in, m)
        return carry

    lax.fori_loop(0, micro, launch, 0)
    scatter[0]()
    key_place = lax.broadcasted_iota(jnp.int32, (block, block), 0)
    query_place = lax.broadcasted_iota(jnp.int32, (block, block), 1)
    causal = key_place <= query_place

    def one_micro(m, carry):
        take_blocks(cut, gout, send_in, take_in, m)

        def prepare(i, carry):
            rows = rows_at(i, block)
            q = qkv_ref[m, 0, rows, :].astype(f32) * scale_factor
            k = qkv_ref[m, 1, rows, :].astype(f32)
            g = gout[m, 0, rows, :].astype(f32)
            for h in range(heads):
                queries[h, rows, :] = keep_head(q, masks[h], heads).astype(bf16)
                keys_h[h, rows, :] = keep_head(k, masks[h], heads).astype(bf16)
                gouts[h, rows, :] = keep_head(g, masks[h], heads).astype(bf16)
            delta[i] = lax.dot_general(
                pick,
                g * out_ref[m, 0, rows, :].astype(f32),
                (((1,), (1,)), ((), ())),
                precision=lax.Precision.HIGHEST,
                preferred_element_type=f32,
            )
            grad_q[rows, :] = jnp.zeros((block, width), f32)
            return carry

        lax.fori_loop(0, blocks, prepare, 0)

        def key_block(j, carry):
            run_slot(placed, m * blocks + j)
            krows = rows_at(j, block)

            def pair(i, grad_k, grad_v, diagonal):
                rows = rows_at(i, block)
                bias = bias_ref[m, j, i]
                gq = grad_q[rows, :]
                for h in range(heads):
                    raw = dot_nt(qkv_ref[m, 1, krows, :], queries[h, rows, :])
                    shift = bias - lse_ref[m, i, h : h + 1, :]
                    s = (raw.reshape(per, TILE, block) + shift[:, None, :]).reshape(block, block)
                    if diagonal:
                        s = jnp.where(causal, s, masked_score)
                    p = jnp.exp(s)
                    gp = dot_nt(qkv_ref[m, 2, krows, :], gouts[h, rows, :])
                    gs = (p * (gp - delta[i, h : h + 1, :])).astype(bf16)
                    grad_v = grad_v + dot_nn(p.astype(bf16), gouts[h, rows, :])
                    grad_k = grad_k + dot_nn(gs, queries[h, rows, :])
                    gq = gq + dot_tn(gs, keys_h[h, krows, :])
                grad_q[rows, :] = gq
                return grad_k, grad_v

            zero = jnp.zeros((block, width), f32)
            state = pair(j, zero, zero, True)
            state = lax.fori_loop(
                j + 1, blocks, lambda i, s: pair(i, s[0], s[1], False), state
            )
            grads[m, 0, krows, :] = (grad_q[krows, :] * scale_factor).astype(bf16)
            grads[m, 1, krows, :] = state[0].astype(bf16)
            grads[m, 2, krows, :] = state[1].astype(bf16)
            for sub in range(block // place_rows):
                place = j * (block // place_rows) + sub
                send_home(grads, back, send_out, take_out, m, place)
            return carry

        lax.fori_loop(0, blocks, key_block, 0)
        return carry

    lax.fori_loop(0, micro, one_micro, 0)

    def finish(m, carry):
        for step in range(1, seq):
            to_peer(cut, gout, send_in, take_in, m, step).wait_send()
        take_home(grads, back, send_out, take_out, m)
        join_heads(back, m, 3, grad_ref)
        return carry

    scatter[-1]()
    lax.fori_loop(0, micro, finish, 0)


def self_backward(grad_attended, qkv, bias, out, lse, seq, arrays, kinds, y_size):
    micro, rows, width = grad_attended.shape
    length, part = qkv.shape[2:]
    heads = part // HD
    blocks = length // BLOCK
    whole = pl.BlockSpec(memory_space=pltpu.VMEM)
    sems = pltpu.SemaphoreType.DMA((micro, seq))
    sources = scatter_blocks(arrays, seq // 2, y_size)
    count = len(arrays)
    scratch = []
    for source, kind in zip(sources, kinds):
        scratch += scatter_shapes(source, kind)
    return pl.pallas_call(
        functools.partial(self_backward_kernel, heads, BLOCK, kinds),
        in_specs=[whole] * 5 + [pl.BlockSpec(memory_space=pl.ANY)] * count,
        out_specs=[whole] * (1 + count),
        out_shape=[jax.ShapeDtypeStruct((micro, rows, 3 * width), bf16)]
        + [jax.ShapeDtypeStruct(b.shape[4:], f32) for b in sources],
        scratch_shapes=[
            pltpu.VMEM((micro, 1, seq, rows, part), bf16),
            pltpu.VMEM((micro, 1, length, part), bf16),
            pltpu.VMEM((micro, 3, length, part), bf16),
            pltpu.VMEM((micro, 3, seq, rows, part), bf16),
            pltpu.VMEM((heads, length, part), bf16),
            pltpu.VMEM((heads, length, part), bf16),
            pltpu.VMEM((heads, length, part), bf16),
            pltpu.VMEM((blocks, 8, BLOCK), f32),
            pltpu.VMEM((length, part), f32),
            sems,
            sems,
            sems,
            sems,
        ]
        + scratch
        + scatter_sems(count, seq // 2, y_size),
        compiler_params=pltpu.CompilerParams(
            vmem_limit_bytes=60 << 20, collective_id=2, has_side_effects=True
        ),
        name="self_backward",
    )(grad_attended, qkv, bias, out, lse, *sources)


def cross_forward_kernel(lengths_ref, q_ref, k_ref, v_ref, out_ref, lse_ref):
    count, width = k_ref.shape[1], k_ref.shape[2]
    rows = q_ref.shape[1]
    heads = width // HD
    masks = head_masks((rows, width), heads)
    valid = (
        lax.broadcasted_iota(jnp.int32, (count, rows), 0) < lengths_ref[pl.program_id(0)]
    )
    q = q_ref[0].astype(f32) * scale_factor
    values_t = jnp.transpose(v_ref[0].astype(f32)).astype(bf16)
    outs, lses = [], []
    for h in range(heads):
        s = dot_nt(k_ref[0], keep_head(q, masks[h], heads).astype(bf16))
        s = jnp.where(valid, s, masked_score)
        m = jnp.max(s, 0, keepdims=True)
        p = jnp.exp(s - m)
        total = jnp.sum(p, 0, keepdims=True)
        out = dot_nn(values_t[h * HD : (h + 1) * HD], p.astype(bf16))
        outs.append(out * (1.0 / total))
        lses.append(m + jnp.log(total))
    out_ref[0] = jnp.transpose(jnp.concatenate(outs, 0)).astype(bf16)
    lse_ref[0, 0] = jnp.concatenate(lses, 0)


def cross_forward(lengths, queries, pairs):
    micro, rows, width = queries.shape
    count = pairs.shape[1]
    groups = width // 128
    return pl.pallas_call(
        cross_forward_kernel,
        grid=(micro, groups),
        in_specs=[
            pl.BlockSpec(memory_space=pltpu.SMEM),
            pl.BlockSpec((1, rows, 128), lambda m, g: (m, 0, g)),
            pl.BlockSpec((1, count, 128), lambda m, g: (m, 0, g)),
            pl.BlockSpec((1, count, 128), lambda m, g: (m, 0, g + groups)),
        ],
        out_specs=[
            pl.BlockSpec((1, rows, 128), lambda m, g: (m, 0, g)),
            pl.BlockSpec((1, 1, 2, rows), lambda m, g: (m, g, 0, 0)),
        ],
        out_shape=[
            jax.ShapeDtypeStruct((micro, rows, width), bf16),
            jax.ShapeDtypeStruct((micro, groups, 2, rows), f32),
        ],
        compiler_params=pltpu.CompilerParams(vmem_limit_bytes=32 << 20),
        name="cross_forward",
    )(lengths, queries, pairs, pairs)


def cross_backward_kernel(
    lengths_ref, q_ref, k_ref, v_ref, out_ref, lse_ref, gout_ref, gq_ref, gk_ref, gv_ref
):
    count, width = k_ref.shape[1], k_ref.shape[2]
    rows = q_ref.shape[1]
    heads = width // HD
    masks = head_masks((rows, width), heads)
    key_masks = head_masks((count, width), heads)
    valid = (
        lax.broadcasted_iota(jnp.int32, (count, rows), 0) < lengths_ref[pl.program_id(0)]
    )
    lane = lax.broadcasted_iota(jnp.int32, (8, width), 1)
    row = lax.broadcasted_iota(jnp.int32, (8, width), 0)
    pick = jnp.where((lane >= row * HD) & (lane < (row + 1) * HD), 1.0, 0.0)
    q = q_ref[0].astype(f32) * scale_factor
    g = gout_ref[0].astype(f32)
    k = k_ref[0].astype(f32)
    delta = lax.dot_general(
        pick,
        g * out_ref[0].astype(f32),
        (((1,), (1,)), ((), ())),
        precision=lax.Precision.HIGHEST,
        preferred_element_type=f32,
    )
    grad_q = jnp.zeros((rows, width), f32)
    grad_k = jnp.zeros((count, width), f32)
    grad_v = jnp.zeros((count, width), f32)
    for h in range(heads):
        qh = keep_head(q, masks[h], heads).astype(bf16)
        gh = keep_head(g, masks[h], heads).astype(bf16)
        kh = keep_head(k, key_masks[h], heads).astype(bf16)
        s = dot_nt(k_ref[0], qh) - lse_ref[0, 0, h : h + 1, :]
        p = jnp.exp(jnp.where(valid, s, masked_score))
        gp = dot_nt(v_ref[0], gh)
        gs = (p * (gp - delta[h : h + 1, :])).astype(bf16)
        grad_v += dot_nn(p.astype(bf16), gh)
        grad_k += dot_nn(gs, qh)
        grad_q += dot_tn(gs, kh)
    gq_ref[0] = (grad_q * scale_factor).astype(bf16)
    gk_ref[0] = grad_k.astype(bf16)
    gv_ref[0] = grad_v.astype(bf16)


def cross_backward(lengths, queries, pairs, out, lse, gout):
    micro, rows, width = queries.shape
    count = pairs.shape[1]
    groups = width // 128
    row_spec = pl.BlockSpec((1, rows, 128), lambda m, g: (m, 0, g))
    key_spec = pl.BlockSpec((1, count, 128), lambda m, g: (m, 0, g))
    value_spec = pl.BlockSpec((1, count, 128), lambda m, g: (m, 0, g + groups))
    lse_spec = pl.BlockSpec((1, 1, 2, rows), lambda m, g: (m, g, 0, 0))
    return pl.pallas_call(
        cross_backward_kernel,
        grid=(micro, groups),
        in_specs=[
            pl.BlockSpec(memory_space=pltpu.SMEM),
            row_spec,
            key_spec,
            value_spec,
            row_spec,
            lse_spec,
            row_spec,
        ],
        out_specs=[row_spec, key_spec, key_spec],
        out_shape=[
            jax.ShapeDtypeStruct((micro, rows, width), bf16),
            jax.ShapeDtypeStruct((micro, count, width), bf16),
            jax.ShapeDtypeStruct((micro, count, width), bf16),
        ],
        compiler_params=pltpu.CompilerParams(vmem_limit_bytes=32 << 20),
        name="cross_backward",
    )(lengths, queries, pairs, pairs, out, lse, gout)


def gelu_parts(v):
    inner = 0.7978845608028654 * (v + 0.044715 * (v * v * v))
    t = jnp.tanh(inner)
    value = 0.5 * v * (1.0 + t)
    slope = 0.5 * (1.0 + t) + 0.5 * v * (1.0 - t * t) * (
        0.7978845608028654 * (1.0 + 3.0 * 0.044715 * (v * v))
    )
    return value, slope


def per_device(
    tokens,
    memory,
    cotangent,
    tile_segment,
    parents,
    memory_lengths,
    self_qkv,
    self_out,
    cross_q,
    cross_kv,
    cross_out,
    ffn_in,
    ffn_out,
    norm_gain,
    norm_bias,
):
    micro, _, row_count, width = tokens.shape
    seq = lax.axis_size("seq")
    total_rows = micro * row_count
    memory_rows = memory.shape[2]

    def gather(shard, axis=0):
        return lax.all_gather(shard, ALL, axis=axis, tiled=True)

    joint_weight = gather(self_qkv)
    norms = gather(jnp.concatenate([norm_gain, norm_bias], 0), 1).astype(f32)
    gain_rows, bias_rows = norms[:3], norms[3:]
    small = gather(jnp.concatenate([self_out, cross_q, cross_kv, cross_out, ffn_in], 1))
    memory_full = lax.all_gather(memory[:, 0], "seq", axis=1, tiled=True)
    down_weight = gather(ffn_out)
    cuts = [0]
    for shard in (self_out, cross_q, cross_kv, cross_out, ffn_in):
        cuts.append(cuts[-1] + shard.shape[1])
    self_output, cross_weight, pair_weight, cross_output, upward_weight = (
        small[:, a:b] for a, b in zip(cuts[:-1], cuts[1:])
    )

    x = tokens.reshape(total_rows, width)
    x32 = x.astype(f32)
    bias = jax.vmap(lambda t, p: tree_bias(t, p, BLOCK))(tile_segment[:, 0], parents[:, 0])
    lengths = memory_lengths[:, 0]

    projected = dot_nn(x, joint_weight).astype(bf16)
    qkv, attended_heads, self_lse, attended = self_forward(
        projected.reshape(micro, row_count, 3 * width), bias, seq
    )
    attended = attended.reshape(total_rows, width)

    mixed_first = residual_weight * x32 + dot_nn(attended, self_output)
    hidden_first = layer_norm(mixed_first, gain_rows[0], bias_rows[0])
    hidden_first_low = hidden_first.astype(bf16)
    cross_query = dot_nn(hidden_first_low, cross_weight).astype(bf16)
    cross_query = cross_query.reshape(micro, row_count, width)
    count = memory_full.shape[1]
    pairs = dot_nn(memory_full.reshape(micro * count, width), pair_weight).astype(bf16)
    pairs = pairs.reshape(micro, count, 2 * width)
    cross_heads, cross_lse = cross_forward(lengths, cross_query, pairs)
    cross_attended = cross_heads.reshape(total_rows, width)
    mixed_second = residual_weight * hidden_first + dot_nn(cross_attended, cross_output)
    hidden_second = layer_norm(mixed_second, gain_rows[1], bias_rows[1])
    hidden_second_low = hidden_second.astype(bf16)
    pre_active = dot_nn(hidden_second_low, upward_weight)
    active = gelu_parts(pre_active)[0].astype(bf16)
    mixed_third = residual_weight * hidden_second + dot_nn(active, down_weight)
    output = layer_norm(mixed_third, gain_rows[2], bias_rows[2]).astype(bf16)

    upstream = cotangent.reshape(total_rows, width).astype(f32)
    grad_third, gain_third, bias_third = layer_norm_back(mixed_third, gain_rows[2], upstream)
    branch_third = grad_third.astype(bf16)
    grad_down = dot_tn(active, branch_third).astype(bf16)
    grad_inner = (gelu_parts(pre_active)[1] * dot_nt(branch_third, down_weight)).astype(bf16)
    grad_upward = dot_tn(hidden_second_low, grad_inner).astype(bf16)

    grad_hidden_second = residual_weight * grad_third + dot_nt(grad_inner, upward_weight)
    grad_second, gain_second, bias_second = layer_norm_back(
        mixed_second, gain_rows[1], grad_hidden_second
    )
    branch_second = grad_second.astype(bf16)
    grad_cross_output = dot_tn(cross_attended, branch_second).astype(bf16)
    grad_cross_attended = dot_nt(branch_second, cross_output).astype(bf16)
    grad_cross_low, grad_keys, grad_values = cross_backward(
        lengths,
        cross_query,
        pairs,
        cross_heads,
        cross_lse,
        grad_cross_attended.reshape(micro, row_count, width),
    )
    memory_partial = jnp.concatenate([grad_keys, grad_values], 2)
    own_pairs = lax.psum_scatter(memory_partial, "seq", scatter_dimension=1, tiled=True)
    grad_cross_low = grad_cross_low.reshape(total_rows, width)
    grad_cross_weight = dot_tn(hidden_first_low, grad_cross_low).astype(bf16)
    grad_hidden_first = residual_weight * grad_second + dot_nt(grad_cross_low, cross_weight)
    grad_first, gain_first, bias_first = layer_norm_back(
        mixed_first, gain_rows[0], grad_hidden_first
    )
    branch_first = grad_first.astype(bf16)
    grad_self_output = dot_tn(attended, branch_first).astype(bf16)
    grad_attended = dot_nt(branch_first, self_output).astype(bf16)
    grad_projected, own_upward, own_down = self_backward(
        grad_attended.reshape(micro, row_count, width),
        qkv,
        bias,
        attended_heads,
        self_lse,
        seq,
        [grad_upward, grad_down],
        (True, False),
        lax.axis_size("fsdp") // 2,
    )
    grad_projected = grad_projected.reshape(total_rows, 3 * width)
    grad_joint = dot_tn(x, grad_projected).astype(bf16)
    grad_tokens = (residual_weight * grad_first + dot_nt(grad_projected, joint_weight)).astype(bf16)
    grad_pairs_low = own_pairs.reshape(micro * memory_rows, 2 * width)
    grad_pair_weight = dot_tn(memory.reshape(micro * memory_rows, width), grad_pairs_low)
    grad_memory = dot_nt(grad_pairs_low, pair_weight).astype(bf16)
    norm_grads = jnp.stack(
        [gain_first, gain_second, gain_third, bias_first, bias_second, bias_third]
    )
    devices = seq * lax.axis_size("fsdp")
    norm_blocks = norm_grads.reshape(6, devices, width // devices).transpose(1, 0, 2)
    owned = scatter_grads(
        [
            grad_joint,
            grad_self_output,
            grad_pair_weight.astype(bf16),
            grad_cross_weight,
            grad_cross_output,
            norm_blocks.reshape(6 * devices, width // devices),
        ],
        (True, True, False, False, False, False),
        seq // 2,
        lax.axis_size("fsdp") // 2,
        3,
    )
    return (
        output.reshape(tokens.shape),
        grad_tokens.reshape(tokens.shape),
        grad_memory.reshape(memory.shape),
        owned[0],
        owned[1],
        owned[3],
        owned[2],
        owned[4],
        own_upward,
        own_down,
        owned[5][:3],
        owned[5][3:],
    )


def solution(mesh):
    rows = P(None, "fsdp", "seq", None)
    weight = P(ALL, None)
    in_specs = (
        rows,
        rows,
        rows,
        P(None, "fsdp", None),
        P(None, "fsdp", None),
        P(None, "fsdp"),
    ) + (weight,) * 7 + (P(None, ALL),) * 2
    out_specs = (rows, rows, rows) + (weight,) * 7 + (P(None, ALL),) * 2
    return jax.shard_map(
        per_device, mesh=mesh, in_specs=in_specs, out_specs=out_specs, check_vma=False
    )
```

```python
import functools

import jax
import jax.numpy as jnp
from jax import lax
from jax.experimental import pallas as pl
from jax.experimental.pallas import tpu as pltpu
from jax.sharding import PartitionSpec as P

H = 16
HD = 64
TILE = 128
BLOCK = 256
WINDOW = 4
GATHER_END = 75
SPLIT_ELEMENTS = 96 << 10
SCATTER_END = 75

scale_factor = 0.125
residual_weight = 36.0**0.25
norm_epsilon = 1e-05
masked_score = -1e30
ALL = ("seq", "fsdp")
f32 = jnp.float32
bf16 = jnp.bfloat16
MESH = pl.DeviceIdType.MESH


def dot_nn(a, b):
    return lax.dot_general(a, b, (((1,), (0,)), ((), ())), preferred_element_type=f32)


def dot_nt(a, b):
    return lax.dot_general(a, b, (((1,), (1,)), ((), ())), preferred_element_type=f32)


def dot_tn(a, b):
    return lax.dot_general(a, b, (((0,), (0,)), ((), ())), preferred_element_type=f32)


def norm_stats(incoming):
    row_mean = jnp.mean(incoming, -1, keepdims=True)
    centred = incoming - row_mean
    variance = jnp.mean(centred * centred, -1, keepdims=True)
    return centred, lax.rsqrt(variance + norm_epsilon)


def layer_norm(incoming, gain_row, bias_row):
    centred, inverse = norm_stats(incoming)
    return centred * inverse * gain_row + bias_row


def layer_norm_back(incoming, gain_row, upstream):
    centred, inverse = norm_stats(incoming)
    normal = centred * inverse
    grad_bias = jnp.sum(upstream, 0)
    grad_gain = jnp.sum(upstream * normal, 0)
    scaled = upstream * gain_row
    grad = inverse * (
        scaled
        - jnp.mean(scaled, -1, keepdims=True)
        - normal * jnp.mean(scaled * normal, -1, keepdims=True)
    )
    return grad, grad_gain, grad_bias


def ancestors(parent_ids):
    segment_ids = jnp.arange(parent_ids.shape[0], dtype=jnp.int32)
    hop = (parent_ids[:, None] == segment_ids[None, :]).astype(f32)
    reach = jnp.maximum(hop, (segment_ids[:, None] == segment_ids[None, :]).astype(f32))
    steps = 1
    while steps < parent_ids.shape[0]:
        reach = jnp.minimum(jnp.dot(reach, reach, precision=lax.Precision.HIGHEST), 1.0)
        steps *= 2
    return reach


def tree_bias(tile_segments, parent_ids, block):
    tiles = tile_segments.shape[0]
    onehot = (
        tile_segments[:, None] == jnp.arange(parent_ids.shape[0], dtype=jnp.int32)[None, :]
    ).astype(f32)
    high = lax.Precision.HIGHEST
    related = jnp.dot(
        jnp.dot(onehot, ancestors(parent_ids), precision=high), onehot.T, precision=high
    )
    bias = jnp.where(related > 0.5, 0.0, masked_score)
    per = block // TILE
    blocks = tiles // per
    bias = bias.reshape(blocks, per, blocks, per).transpose(2, 0, 3, 1)
    return jnp.repeat(bias, TILE, axis=3)


def head_masks(shape, heads):
    lane = lax.broadcasted_iota(jnp.int32, shape, 1)
    return [(lane >= h * HD) & (lane < (h + 1) * HD) for h in range(heads)]


def keep_head(value, mask, heads):
    return value if heads == 1 else jnp.where(mask, value, jnp.zeros_like(value))


def greet(peers):
    barrier = pltpu.get_barrier_semaphore()
    for peer in peers:
        pl.semaphore_signal(barrier, inc=1, device_id=peer, device_id_type=MESH)
    pl.semaphore_wait(barrier, len(peers))


def peer_at(step):
    count = lax.axis_size("seq")
    return lax.rem(lax.axis_index("seq") + step, count)


def rows_at(i, count):
    return pl.ds(pl.multiple_of(i * count, count), count)


def cut_heads(rows_ref, m, parts, blocks_ref):
    seq, part = blocks_ref.shape[2], blocks_ref.shape[4]
    for p in range(parts):
        for s in range(seq):
            first = (p * seq + s) * part
            blocks_ref[m, p, s] = rows_ref[m, :, first : first + part]


def join_heads(blocks_ref, m, parts, rows_ref):
    seq, part = blocks_ref.shape[2], blocks_ref.shape[4]
    for p in range(parts):
        for s in range(seq):
            first = (p * seq + s) * part
            rows_ref[m, :, first : first + part] = blocks_ref[m, p, s]


def to_peer(source_ref, target_ref, send, receive, m, step):
    rows = source_ref.shape[3]
    return pltpu.make_async_remote_copy(
        src_ref=source_ref.at[m, :, peer_at(step)],
        dst_ref=target_ref.at[m, :, rows_at(lax.axis_index("seq"), rows)],
        send_sem=send.at[m, step],
        recv_sem=receive.at[m, step],
        device_id={"seq": peer_at(step)},
        device_id_type=MESH,
    )


def to_self(source_ref, target_ref, sem, m):
    rows = source_ref.shape[3]
    me = lax.axis_index("seq")
    return pltpu.make_async_copy(
        source_ref.at[m, :, me], target_ref.at[m, :, rows_at(me, rows)], sem.at[m, 0]
    )


def send_blocks(source_ref, target_ref, send, receive, m):
    for step in range(1, lax.axis_size("seq")):
        to_peer(source_ref, target_ref, send, receive, m, step).start()
    to_self(source_ref, target_ref, send, m).start()


def take_blocks(source_ref, target_ref, send, receive, m, between=None):
    for step in range(1, lax.axis_size("seq")):
        to_peer(source_ref, target_ref, send, receive, m, step).wait_recv()
        if between is not None:
            between(step)
    to_self(source_ref, target_ref, send, m).wait()


def home_copy(source_ref, target_ref, send, receive, m, place):
    rows = target_ref.shape[3]
    me = lax.axis_index("seq")
    count = lax.axis_size("seq")
    step = lax.rem(place - me + count, count)
    return pltpu.make_async_remote_copy(
        src_ref=source_ref.at[m, :, rows_at(place, rows)],
        dst_ref=target_ref.at[m, :, me],
        send_sem=send.at[m, step],
        recv_sem=receive.at[m, step],
        device_id={"seq": place},
        device_id_type=MESH,
    )


def home_self(source_ref, target_ref, sem, m):
    rows = target_ref.shape[3]
    me = lax.axis_index("seq")
    return pltpu.make_async_copy(
        source_ref.at[m, :, rows_at(me, rows)], target_ref.at[m, :, me], sem.at[m, 0]
    )


def send_home(source_ref, target_ref, send, receive, m, place):
    me = lax.axis_index("seq")

    @pl.when(place != me)
    def _():
        home_copy(source_ref, target_ref, send, receive, m, place).start()

    @pl.when(place == me)
    def _():
        home_self(source_ref, target_ref, send, m).start()


def take_home(source_ref, target_ref, send, receive, m):
    for step in range(1, lax.axis_size("seq")):
        home_copy(source_ref, target_ref, send, receive, m, peer_at(step)).wait()
    home_self(source_ref, target_ref, send, m).wait()


def scatter_places():
    s, f = lax.axis_index("seq"), lax.axis_index("fsdp")
    z, y = s // 2, f // 2
    return z, s - 2 * z, y, f - 2 * y, lax.axis_size("seq") // 2, lax.axis_size("fsdp") // 2


def scatter_peers():
    z, x, y, c, z_size, y_size = scatter_places()
    peers = [{"fsdp": 2 * y + 1 - c}, {"seq": 2 * z + 1 - x}]
    peers += [{"fsdp": 2 * lax.rem(y + k, y_size) + c} for k in range(1, y_size)]
    peers += [{"seq": 2 * lax.rem(z + k, z_size) + x} for k in range(1, z_size)]
    return peers


def scatter_shapes(blocks, x_first):
    z_size, _, y_size, _, rows, columns = blocks.shape
    if x_first:
        first, second = (1, y_size), (y_size - 1,)
    else:
        first, second = (y_size - 1, 2), (1,)
    kind = blocks.dtype
    return [
        pltpu.VMEM((z_size, 2, y_size, rows, columns), kind),
        pltpu.VMEM((z_size, 2, y_size, rows, columns), kind),
        pltpu.VMEM((z_size,) + first + (rows, columns), kind),
        pltpu.VMEM((z_size,) + second + (rows, columns), kind),
        pltpu.VMEM((z_size - 1, rows, columns), kind),
    ]


def scatter_sems(count, z_size, y_size):
    pair = pltpu.SemaphoreType.DMA((count, z_size))
    triple = pltpu.SemaphoreType.DMA((count, z_size, max(1, y_size - 1)))
    return [pair, pair, pair, triple, triple, triple, triple, pair, pair]


def add_into(target, source):
    target[...] = target[...] + source[...]


def scatter_steps(kinds, sources, outs, buffers, sems):
    z, x, y, c, z_size, y_size = scatter_places()
    local, core_s, core_r, first_s, first_r, second_s, second_r, last_s, last_r = sems
    count = len(sources)

    def to_z(t):
        return lax.rem(z + 1 + t, z_size)

    def remote(source, target, send, receive, peer):
        return pltpu.make_async_remote_copy(
            src_ref=source,
            dst_ref=target,
            send_sem=send,
            recv_sem=receive,
            device_id=peer,
            device_id_type=MESH,
        )

    def own_copy(a, t):
        return pltpu.make_async_copy(
            sources[a].at[to_z(t), :, :, c], buffers[a][0].at[t], local.at[a, t]
        )

    def core_copy(a, t):
        return remote(
            sources[a].at[to_z(t), :, :, 1 - c],
            buffers[a][1].at[t],
            core_s.at[a, t],
            core_r.at[a, t],
            {"fsdp": 2 * y + 1 - c},
        )

    def x_peer():
        return {"seq": 2 * z + 1 - x}

    def y_place(k):
        return lax.rem(y + k, y_size)

    def y_peer(k):
        return {"fsdp": 2 * y_place(k) + c}

    def first_copies(a, t):
        own, _, first, _, _ = buffers[a]
        if kinds[a]:
            sends = [(own.at[t, 1 - x], x_peer())]
        else:
            sends = [(own.at[t, :, y_place(k)], y_peer(k)) for k in range(1, y_size)]
        return [
            remote(source, first.at[t, k], first_s.at[a, t, k], first_r.at[a, t, k], peer)
            for k, (source, peer) in enumerate(sends)
        ]

    def second_copies(a, t):
        own, _, _, second, _ = buffers[a]
        if kinds[a]:
            sends = [(own.at[t, x, y_place(k)], y_peer(k)) for k in range(1, y_size)]
        else:
            sends = [(own.at[t, 1 - x, y], x_peer())]
        return [
            remote(source, second.at[t, k], second_s.at[a, t, k], second_r.at[a, t, k], peer)
            for k, (source, peer) in enumerate(sends)
        ]

    def last_copy(a, t):
        own, _, _, _, last = buffers[a]
        return remote(
            own.at[t, x, y],
            last.at[t],
            last_s.at[a, t],
            last_r.at[a, t],
            {"seq": 2 * to_z(t) + x},
        )

    def start_core(t):
        for a in range(count):
            core_copy(a, t).start()
            own_copy(a, t).start()

    def core_step(t):
        for a in range(count):
            core_copy(a, t).wait_recv()
            own_copy(a, t).wait()
            own, core = buffers[a][:2]

            def add(i, carry, own=own, core=core):
                add_into(own.at[t, i // y_size, i % y_size], core.at[t, i // y_size, i % y_size])
                return carry

            lax.fori_loop(0, 2 * y_size, add, 0)
            for copy in first_copies(a, t):
                copy.start()
        if t + 2 < z_size:
            start_core(t + 2)

    def first_step(t):
        for a in range(count):
            own, _, first, _, _ = buffers[a]
            for k, copy in enumerate(first_copies(a, t)):
                copy.wait_recv()
                for i in range(y_size if kinds[a] else 2):
                    target = own.at[t, x, i] if kinds[a] else own.at[t, i, y]
                    add_into(target, first.at[t, k, i])
            for copy in second_copies(a, t):
                copy.start()

    def second_step(t):
        for a in range(count):
            own, _, _, second, _ = buffers[a]
            for k, copy in enumerate(second_copies(a, t)):
                copy.wait_recv()
                add_into(own.at[t, x, y], second.at[t, k])
            if t < z_size - 1:
                last_copy(a, t).start()

    def final_step():
        for a in range(count):
            own, _, _, _, last = buffers[a]
            total = own[z_size - 1, x, y].astype(f32)
            for t in range(z_size - 1):
                last_copy(a, t).wait()
                total = total + last[t].astype(f32)
            outs[a][...] = total
            for t in range(z_size):
                core_copy(a, t).wait_send()
                for copy in first_copies(a, t) + second_copies(a, t):
                    copy.wait_send()

    def opening():
        start_core(0)
        if z_size > 1:
            start_core(1)

    steps = [opening]
    for t in range(z_size + 2):
        if t < z_size:
            steps.append(functools.partial(core_step, t))
        if 0 <= t - 1 < z_size:
            steps.append(functools.partial(first_step, t - 1))
        if 0 <= t - 2 < z_size:
            steps.append(functools.partial(second_step, t - 2))
    steps.append(final_step)
    return steps


def scatter_kernel(kinds, *refs):
    count = len(kinds)
    sources, outs, rest = refs[:count], refs[count : 2 * count], refs[2 * count :]
    buffers = [rest[5 * a : 5 * a + 5] for a in range(count)]
    greet(scatter_peers())
    for step in scatter_steps(kinds, sources, outs, buffers, rest[5 * count :]):
        step()


def scatter_blocks(arrays, z_size, y_size):
    return [
        a.reshape(z_size, 2, y_size, 2, a.shape[0] // (4 * z_size * y_size), a.shape[1])
        for a in arrays
    ]


def scatter_grads(arrays, kinds, z_size, y_size, collective_id):
    blocks = scatter_blocks(arrays, z_size, y_size)
    scratch = []
    for block, kind in zip(blocks, kinds):
        scratch += scatter_shapes(block, kind)
    return pl.pallas_call(
        functools.partial(scatter_kernel, kinds),
        in_specs=[pl.BlockSpec(memory_space=pl.ANY)] * len(arrays),
        out_specs=[pl.BlockSpec(memory_space=pltpu.VMEM)] * len(arrays),
        out_shape=[jax.ShapeDtypeStruct(b.shape[4:], f32) for b in blocks],
        scratch_shapes=scratch + scatter_sems(len(arrays), z_size, y_size),
        compiler_params=pltpu.CompilerParams(
            vmem_limit_bytes=60 << 20, collective_id=collective_id, has_side_effects=True
        ),
        name="scatter_grads",
    )(*blocks)


def spread(steps, first, last):
    return [(first + k * (last - first) // max(1, len(steps) - 1), s) for k, s in enumerate(steps)]


def run_slot(placed, slot):
    for at, step in placed:
        pl.when(slot == at)(step)


def both_peers():
    _, _, y, c, _, y_size = scatter_places()
    peers = [{"seq": peer_at(step)} for step in range(1, lax.axis_size("seq"))]
    peers += [{"fsdp": 2 * y + 1 - c}]
    return peers + [{"fsdp": 2 * lax.rem(y + k, y_size) + c} for k in range(1, y_size)]


def gather_parts(shards, kinds, groups):
    parts, units = [], []
    for group in groups:
        pieces = []
        for a in group:
            rows, columns = shards[a].shape
            kind = kinds[a]
            split = 2 if rows % 32 == 0 and rows * columns >= SPLIT_ELEMENTS else 1
            for n in range(split):
                cut = (n * columns // split, columns // split)
                if kind == "seq" or rows % 32:
                    piece = [(a, 0, rows) + cut + ("x" if kind == "all" else kind,)]
                else:
                    half = rows // 2
                    piece = [(a, 0, half) + cut + ("x",), (a, half, half) + cut + ("y",)]
                if n == len(pieces):
                    pieces.append([])
                pieces[n] += piece
        for piece in pieces:
            units.append(range(len(parts), len(parts) + len(piece)))
            parts += piece
    return parts, units


def gather_sems(plan, z_size, y_size):
    count = len(plan[0])
    z_sem = pltpu.SemaphoreType.DMA((count, z_size))
    y_sem = pltpu.SemaphoreType.DMA((count, max(1, y_size - 1)))
    one = pltpu.SemaphoreType.DMA((count, 1))
    return [z_sem, z_sem, y_sem, y_sem, y_sem, y_sem, one, one]


def gather_steps(plan, shards, outs, sems):
    z, x, y, c, z_size, y_size = scatter_places()
    z_s, z_r, first_s, first_r, second_s, second_r, core_s, core_r = sems
    parts, units = plan

    def remote(view, peer, send, receive):
        return pltpu.make_async_remote_copy(
            src_ref=view,
            dst_ref=view,
            send_sem=send,
            recv_sem=receive,
            device_id=peer,
            device_id_type=MESH,
        )

    def shard_of(p):
        a, start, rows, left, columns, _ = parts[p]
        return shards[a].at[pl.ds(start, rows), pl.ds(left, columns)]

    def place(p, *lead):
        a, start, rows, left, columns, _ = parts[p]
        return outs[a].at[lead + (pl.ds(start, rows), pl.ds(left, columns))]

    def own(p):
        return place(p, z, x) if parts[p][-1] == "seq" else place(p, z, x, y, c)

    def own_copy(p):
        return pltpu.make_async_copy(shard_of(p), own(p), z_s.at[p, 0])

    def z_copies(p):
        return [
            pltpu.make_async_remote_copy(
                src_ref=shard_of(p),
                dst_ref=own(p),
                send_sem=z_s.at[p, k],
                recv_sem=z_r.at[p, k],
                device_id={"seq": 2 * lax.rem(z + k, z_size) + x},
                device_id_type=MESH,
            )
            for k in range(1, z_size)
        ]

    def x_peer():
        return {"seq": 2 * z + 1 - x}

    def y_peers():
        return [{"fsdp": 2 * lax.rem(y + k, y_size) + c} for k in range(1, y_size)]

    whole = slice(None)

    def first_copies(p):
        kind = parts[p][-1]
        view = place(p, whole, x) if kind == "seq" else place(p, whole, x, y, c)
        peers = y_peers() if kind == "y" else [x_peer()]
        return [
            remote(view, peer, first_s.at[p, k], first_r.at[p, k]) for k, peer in enumerate(peers)
        ]

    def second_copies(p):
        kind = parts[p][-1]
        if kind == "seq":
            return []
        view = place(p, whole, whole, y, c) if kind == "x" else place(p, whole, x, whole, c)
        peers = y_peers() if kind == "x" else [x_peer()]
        return [
            remote(view, peer, second_s.at[p, k], second_r.at[p, k]) for k, peer in enumerate(peers)
        ]

    def core_copies(p):
        if parts[p][-1] == "seq":
            return []
        view = place(p, whole, whole, whole, c)
        return [remote(view, {"fsdp": 2 * y + 1 - c}, core_s.at[p, 0], core_r.at[p, 0])]

    def step(t):
        def unit(at):
            return units[at] if 0 <= at < len(units) else ()

        for p in unit(t - 3):
            for copy in second_copies(p):
                copy.wait_recv()
            for copy in core_copies(p):
                copy.start()
        for p in unit(t - 2):
            for copy in first_copies(p):
                copy.wait_recv()
            for copy in second_copies(p):
                copy.start()
        for p in unit(t - 1):
            for copy in z_copies(p):
                copy.wait_recv()
            own_copy(p).wait()
            for copy in first_copies(p):
                copy.start()
        for p in unit(t):
            for copy in z_copies(p):
                copy.start()
            own_copy(p).start()

    def final_step():
        for p in range(len(parts)):
            for copy in core_copies(p):
                copy.wait()
            for copy in z_copies(p) + first_copies(p) + second_copies(p):
                copy.wait_send()

    return [functools.partial(step, t) for t in range(len(units) + 3)] + [final_step]


def gather_out(shard, kind, z_size, y_size):
    lead = (z_size, 2) if kind == "seq" else (z_size, 2, y_size, 2)
    return jax.ShapeDtypeStruct(lead + shard.shape, shard.dtype)


def gather_kernel(plan, count, *refs):
    shards, outs, sems = refs[:count], refs[count : 2 * count], refs[2 * count :]
    greet(scatter_peers())
    for step in gather_steps(plan, shards, outs, sems):
        step()


def gather_first(shards, kinds, groups, z_size, y_size, collective_id):
    plan = gather_parts(shards, kinds, groups)
    return pl.pallas_call(
        functools.partial(gather_kernel, plan, len(shards)),
        in_specs=[pl.BlockSpec(memory_space=pl.ANY)] * len(shards),
        out_specs=[pl.BlockSpec(memory_space=pl.ANY)] * len(shards),
        out_shape=[gather_out(s, k, z_size, y_size) for s, k in zip(shards, kinds)],
        scratch_shapes=gather_sems(plan, z_size, y_size),
        compiler_params=pltpu.CompilerParams(collective_id=collective_id, has_side_effects=True),
        name="gather_first",
    )(*shards)


def self_forward_kernel(heads, block, plan, count, *refs):
    rows_ref, bias_ref = refs[:2]
    shards, refs = refs[2 : 2 + count], refs[2 + count :]
    qkv_ref, out_ref, lse_ref, attended_ref = refs[:4]
    whole, refs = refs[4 : 4 + count], refs[4 + count :]
    cut, back, queries, values_t, send_in, take_in, send_out, take_out = refs[:8]
    gather = gather_steps(plan, shards, whole, refs[8:])
    micro, _, length, width = qkv_ref.shape
    seq = lax.axis_size("seq")
    blocks = length // block
    per = block // TILE
    place_rows = length // seq
    masks = head_masks((block, width), heads)
    per_micro = blocks + seq - 1
    window = min(WINDOW, seq - 1)
    placed = spread(gather[1:-1], 0, GATHER_END * micro * per_micro // 100)
    greet(both_peers())

    def launch(m, carry):
        cut_heads(rows_ref, m, 3, cut)

        @pl.when(m < 1)
        def _():
            for step in range(1, window + 1):
                to_peer(cut, qkv_ref, send_in, take_in, m, step).start()

        to_self(cut, qkv_ref, send_in, m).start()
        return carry

    lax.fori_loop(0, micro, launch, 0)
    gather[0]()
    key_place = lax.broadcasted_iota(jnp.int32, (block, block), 0)
    query_place = lax.broadcasted_iota(jnp.int32, (block, block), 1)
    causal = key_place <= query_place

    def one_micro(m, carry):
        def between(step):
            run_slot(placed, m * per_micro + step - 1)
            if step + window < seq:
                to_peer(cut, qkv_ref, send_in, take_in, m, step + window).start()
            else:

                @pl.when(m + 1 < micro)
                def _():
                    following = step + window + 1 - seq
                    to_peer(cut, qkv_ref, send_in, take_in, m + 1, following).start()

        take_blocks(cut, qkv_ref, send_in, take_in, m, between)

        def prepare(i, carry):
            rows = rows_at(i, block)
            q = qkv_ref[m, 0, rows, :].astype(f32) * scale_factor
            for h in range(heads):
                queries[h, rows, :] = keep_head(q, masks[h], heads).astype(bf16)
            values_t[i] = jnp.transpose(qkv_ref[m, 2, rows, :].astype(f32)).astype(bf16)
            return carry

        lax.fori_loop(0, blocks, prepare, 0)

        def scores_of(i, j, h):
            raw = dot_nt(qkv_ref[m, 1, rows_at(j, block), :], queries[h, rows_at(i, block), :])
            bias = bias_ref[m, j, i]
            return (raw.reshape(per, TILE, block) + bias[:, None, :]).reshape(block, block)

        def query_block(i, carry):
            run_slot(placed, m * per_micro + seq - 1 + i)
            state = []
            for h in range(heads):
                s = jnp.where(causal, scores_of(i, i, h), masked_score)
                top = jnp.max(s, 0, keepdims=True)
                p = jnp.exp(s - top)
                total = jnp.sum(p, 0, keepdims=True)
                acc = dot_nn(values_t[i][h * HD : (h + 1) * HD], p.astype(bf16))
                state += [top, total, acc]

            def key_block(j, state):
                fresh = []
                for h in range(heads):
                    top, total, acc = state[3 * h : 3 * h + 3]
                    s = scores_of(i, j, h)
                    higher = jnp.maximum(top, jnp.max(s, 0, keepdims=True))
                    shrink = jnp.exp(top - higher)
                    p = jnp.exp(s - higher)
                    total = total * shrink + jnp.sum(p, 0, keepdims=True)
                    acc = acc * shrink + dot_nn(
                        values_t[j][h * HD : (h + 1) * HD], p.astype(bf16)
                    )
                    fresh += [higher, total, acc]
                return tuple(fresh)

            state = lax.fori_loop(0, i, key_block, tuple(state))
            out = jnp.concatenate(
                [state[3 * h + 2] * (1.0 / state[3 * h + 1]) for h in range(heads)], 0
            )
            out_ref[m, 0, rows_at(i, block), :] = jnp.transpose(out).astype(bf16)
            lse_ref[m, i] = jnp.concatenate(
                [state[3 * h] + jnp.log(state[3 * h + 1]) for h in range(heads)], 0
            )
            for sub in range(block // place_rows):
                place = i * (block // place_rows) + sub
                send_home(out_ref, back, send_out, take_out, m, place)
            return carry

        lax.fori_loop(0, blocks, query_block, 0)
        return carry

    lax.fori_loop(0, micro, one_micro, 0)

    def finish(m, carry):
        for step in range(1, seq):
            to_peer(cut, qkv_ref, send_in, take_in, m, step).wait_send()
        take_home(out_ref, back, send_out, take_out, m)
        join_heads(back, m, 1, attended_ref)
        return carry

    lax.fori_loop(0, micro, finish, 0)
    gather[-1]()


def self_forward(projected, bias, seq, shards, kinds, groups, y_size):
    micro, rows, width = projected.shape
    part = width // 3 // seq
    heads = part // HD
    length = rows * seq
    blocks = length // BLOCK
    whole = pl.BlockSpec(memory_space=pltpu.VMEM)
    sems = pltpu.SemaphoreType.DMA((micro, seq))
    count = len(shards)
    any_place = [pl.BlockSpec(memory_space=pl.ANY)] * count
    plan = gather_parts(shards, kinds, groups)
    return pl.pallas_call(
        functools.partial(self_forward_kernel, heads, BLOCK, plan, count),
        in_specs=[whole, whole] + any_place,
        out_specs=[whole] * 4 + any_place,
        out_shape=[
            jax.ShapeDtypeStruct((micro, 3, length, part), bf16),
            jax.ShapeDtypeStruct((micro, 1, length, part), bf16),
            jax.ShapeDtypeStruct((micro, blocks, heads, BLOCK), f32),
            jax.ShapeDtypeStruct((micro, rows, width // 3), bf16),
        ]
        + [gather_out(s, k, seq // 2, y_size) for s, k in zip(shards, kinds)],
        scratch_shapes=[
            pltpu.VMEM((micro, 3, seq, rows, part), bf16),
            pltpu.VMEM((micro, 1, seq, rows, part), bf16),
            pltpu.VMEM((heads, length, part), bf16),
            pltpu.VMEM((blocks, part, BLOCK), bf16),
            sems,
            sems,
            sems,
            sems,
        ]
        + gather_sems(plan, seq // 2, y_size),
        compiler_params=pltpu.CompilerParams(
            vmem_limit_bytes=50 << 20, collective_id=1, has_side_effects=True
        ),
        name="self_forward",
    )(projected, bias, *shards)


def self_backward_kernel(heads, block, kinds, *refs):
    count = len(kinds)
    rows_ref, qkv_ref, bias_ref, out_ref, lse_ref = refs[:5]
    sources, refs = refs[5 : 5 + count], refs[5 + count :]
    grad_ref, owned, refs = refs[0], refs[1 : 1 + count], refs[1 + count :]
    cut, gout, grads, back, queries, keys_h, gouts, delta, grad_q = refs[:9]
    send_in, take_in, send_out, take_out = refs[9:13]
    buffers = [refs[13 + 5 * a : 18 + 5 * a] for a in range(count)]
    scatter = scatter_steps(kinds, sources, owned, buffers, refs[13 + 5 * count :])
    micro, _, length, width = qkv_ref.shape
    seq = lax.axis_size("seq")
    blocks = length // block
    per = block // TILE
    place_rows = length // seq
    masks = head_masks((block, width), heads)
    lane = lax.broadcasted_iota(jnp.int32, (8, width), 1)
    first_lane = lax.broadcasted_iota(jnp.int32, (8, width), 0) * HD
    pick = jnp.where((lane >= first_lane) & (lane < first_lane + HD), 1.0, 0.0)
    placed = spread(scatter[1:-1], 1, SCATTER_END * micro * blocks // 100)
    greet(both_peers())

    def launch(m, carry):
        cut_heads(rows_ref, m, 1, cut)
        send_blocks(cut, gout, send_in, take_in, m)
        return carry

    lax.fori_loop(0, micro, launch, 0)
    scatter[0]()
    key_place = lax.broadcasted_iota(jnp.int32, (block, block), 0)
    query_place = lax.broadcasted_iota(jnp.int32, (block, block), 1)
    causal = key_place <= query_place

    def one_micro(m, carry):
        take_blocks(cut, gout, send_in, take_in, m)

        def prepare(i, carry):
            rows = rows_at(i, block)
            q = qkv_ref[m, 0, rows, :].astype(f32) * scale_factor
            k = qkv_ref[m, 1, rows, :].astype(f32)
            g = gout[m, 0, rows, :].astype(f32)
            for h in range(heads):
                queries[h, rows, :] = keep_head(q, masks[h], heads).astype(bf16)
                keys_h[h, rows, :] = keep_head(k, masks[h], heads).astype(bf16)
                gouts[h, rows, :] = keep_head(g, masks[h], heads).astype(bf16)
            delta[i] = lax.dot_general(
                pick,
                g * out_ref[m, 0, rows, :].astype(f32),
                (((1,), (1,)), ((), ())),
                precision=lax.Precision.HIGHEST,
                preferred_element_type=f32,
            )
            grad_q[rows, :] = jnp.zeros((block, width), f32)
            return carry

        lax.fori_loop(0, blocks, prepare, 0)

        def key_block(j, carry):
            run_slot(placed, m * blocks + j)
            krows = rows_at(j, block)

            def pair(i, grad_k, grad_v, diagonal):
                rows = rows_at(i, block)
                bias = bias_ref[m, j, i]
                gq = grad_q[rows, :]
                for h in range(heads):
                    raw = dot_nt(qkv_ref[m, 1, krows, :], queries[h, rows, :])
                    shift = bias - lse_ref[m, i, h : h + 1, :]
                    s = (raw.reshape(per, TILE, block) + shift[:, None, :]).reshape(block, block)
                    if diagonal:
                        s = jnp.where(causal, s, masked_score)
                    p = jnp.exp(s)
                    gp = dot_nt(qkv_ref[m, 2, krows, :], gouts[h, rows, :])
                    gs = (p * (gp - delta[i, h : h + 1, :])).astype(bf16)
                    grad_v = grad_v + dot_nn(p.astype(bf16), gouts[h, rows, :])
                    grad_k = grad_k + dot_nn(gs, queries[h, rows, :])
                    gq = gq + dot_tn(gs, keys_h[h, krows, :])
                grad_q[rows, :] = gq
                return grad_k, grad_v

            zero = jnp.zeros((block, width), f32)
            state = pair(j, zero, zero, True)
            state = lax.fori_loop(
                j + 1, blocks, lambda i, s: pair(i, s[0], s[1], False), state
            )
            grads[m, 0, krows, :] = (grad_q[krows, :] * scale_factor).astype(bf16)
            grads[m, 1, krows, :] = state[0].astype(bf16)
            grads[m, 2, krows, :] = state[1].astype(bf16)
            for sub in range(block // place_rows):
                place = j * (block // place_rows) + sub
                send_home(grads, back, send_out, take_out, m, place)
            return carry

        lax.fori_loop(0, blocks, key_block, 0)
        return carry

    lax.fori_loop(0, micro, one_micro, 0)

    def finish(m, carry):
        for step in range(1, seq):
            to_peer(cut, gout, send_in, take_in, m, step).wait_send()
        take_home(grads, back, send_out, take_out, m)
        join_heads(back, m, 3, grad_ref)
        return carry

    scatter[-1]()
    lax.fori_loop(0, micro, finish, 0)


def self_backward(grad_attended, qkv, bias, out, lse, seq, arrays, kinds, y_size):
    micro, rows, width = grad_attended.shape
    length, part = qkv.shape[2:]
    heads = part // HD
    blocks = length // BLOCK
    whole = pl.BlockSpec(memory_space=pltpu.VMEM)
    sems = pltpu.SemaphoreType.DMA((micro, seq))
    sources = scatter_blocks(arrays, seq // 2, y_size)
    count = len(arrays)
    scratch = []
    for source, kind in zip(sources, kinds):
        scratch += scatter_shapes(source, kind)
    return pl.pallas_call(
        functools.partial(self_backward_kernel, heads, BLOCK, kinds),
        in_specs=[whole] * 5 + [pl.BlockSpec(memory_space=pl.ANY)] * count,
        out_specs=[whole] * (1 + count),
        out_shape=[jax.ShapeDtypeStruct((micro, rows, 3 * width), bf16)]
        + [jax.ShapeDtypeStruct(b.shape[4:], f32) for b in sources],
        scratch_shapes=[
            pltpu.VMEM((micro, 1, seq, rows, part), bf16),
            pltpu.VMEM((micro, 1, length, part), bf16),
            pltpu.VMEM((micro, 3, length, part), bf16),
            pltpu.VMEM((micro, 3, seq, rows, part), bf16),
            pltpu.VMEM((heads, length, part), bf16),
            pltpu.VMEM((heads, length, part), bf16),
            pltpu.VMEM((heads, length, part), bf16),
            pltpu.VMEM((blocks, 8, BLOCK), f32),
            pltpu.VMEM((length, part), f32),
            sems,
            sems,
            sems,
            sems,
        ]
        + scratch
        + scatter_sems(count, seq // 2, y_size),
        compiler_params=pltpu.CompilerParams(
            vmem_limit_bytes=60 << 20, collective_id=2, has_side_effects=True
        ),
        name="self_backward",
    )(grad_attended, qkv, bias, out, lse, *sources)


def cross_forward_kernel(lengths_ref, q_ref, k_ref, v_ref, out_ref, lse_ref):
    count, width = k_ref.shape[1], k_ref.shape[2]
    rows = q_ref.shape[1]
    heads = width // HD
    masks = head_masks((rows, width), heads)
    valid = (
        lax.broadcasted_iota(jnp.int32, (count, rows), 0) < lengths_ref[pl.program_id(0)]
    )
    q = q_ref[0].astype(f32) * scale_factor
    values_t = jnp.transpose(v_ref[0].astype(f32)).astype(bf16)
    outs, lses = [], []
    for h in range(heads):
        s = dot_nt(k_ref[0], keep_head(q, masks[h], heads).astype(bf16))
        s = jnp.where(valid, s, masked_score)
        m = jnp.max(s, 0, keepdims=True)
        p = jnp.exp(s - m)
        total = jnp.sum(p, 0, keepdims=True)
        out = dot_nn(values_t[h * HD : (h + 1) * HD], p.astype(bf16))
        outs.append(out * (1.0 / total))
        lses.append(m + jnp.log(total))
    out_ref[0] = jnp.transpose(jnp.concatenate(outs, 0)).astype(bf16)
    lse_ref[0, 0] = jnp.concatenate(lses, 0)


def cross_forward(lengths, queries, pairs):
    micro, rows, width = queries.shape
    count = pairs.shape[1]
    groups = width // 128
    return pl.pallas_call(
        cross_forward_kernel,
        grid=(micro, groups),
        in_specs=[
            pl.BlockSpec(memory_space=pltpu.SMEM),
            pl.BlockSpec((1, rows, 128), lambda m, g: (m, 0, g)),
            pl.BlockSpec((1, count, 128), lambda m, g: (m, 0, g)),
            pl.BlockSpec((1, count, 128), lambda m, g: (m, 0, g + groups)),
        ],
        out_specs=[
            pl.BlockSpec((1, rows, 128), lambda m, g: (m, 0, g)),
            pl.BlockSpec((1, 1, 2, rows), lambda m, g: (m, g, 0, 0)),
        ],
        out_shape=[
            jax.ShapeDtypeStruct((micro, rows, width), bf16),
            jax.ShapeDtypeStruct((micro, groups, 2, rows), f32),
        ],
        compiler_params=pltpu.CompilerParams(vmem_limit_bytes=32 << 20),
        name="cross_forward",
    )(lengths, queries, pairs, pairs)


def cross_backward_kernel(
    lengths_ref, q_ref, k_ref, v_ref, out_ref, lse_ref, gout_ref, gq_ref, gk_ref, gv_ref
):
    count, width = k_ref.shape[1], k_ref.shape[2]
    rows = q_ref.shape[1]
    heads = width // HD
    masks = head_masks((rows, width), heads)
    key_masks = head_masks((count, width), heads)
    valid = (
        lax.broadcasted_iota(jnp.int32, (count, rows), 0) < lengths_ref[pl.program_id(0)]
    )
    lane = lax.broadcasted_iota(jnp.int32, (8, width), 1)
    row = lax.broadcasted_iota(jnp.int32, (8, width), 0)
    pick = jnp.where((lane >= row * HD) & (lane < (row + 1) * HD), 1.0, 0.0)
    q = q_ref[0].astype(f32) * scale_factor
    g = gout_ref[0].astype(f32)
    k = k_ref[0].astype(f32)
    delta = lax.dot_general(
        pick,
        g * out_ref[0].astype(f32),
        (((1,), (1,)), ((), ())),
        precision=lax.Precision.HIGHEST,
        preferred_element_type=f32,
    )
    grad_q = jnp.zeros((rows, width), f32)
    grad_k = jnp.zeros((count, width), f32)
    grad_v = jnp.zeros((count, width), f32)
    for h in range(heads):
        qh = keep_head(q, masks[h], heads).astype(bf16)
        gh = keep_head(g, masks[h], heads).astype(bf16)
        kh = keep_head(k, key_masks[h], heads).astype(bf16)
        s = dot_nt(k_ref[0], qh) - lse_ref[0, 0, h : h + 1, :]
        p = jnp.exp(jnp.where(valid, s, masked_score))
        gp = dot_nt(v_ref[0], gh)
        gs = (p * (gp - delta[h : h + 1, :])).astype(bf16)
        grad_v += dot_nn(p.astype(bf16), gh)
        grad_k += dot_nn(gs, qh)
        grad_q += dot_tn(gs, kh)
    gq_ref[0] = (grad_q * scale_factor).astype(bf16)
    gk_ref[0] = grad_k.astype(bf16)
    gv_ref[0] = grad_v.astype(bf16)


def cross_backward(lengths, queries, pairs, out, lse, gout):
    micro, rows, width = queries.shape
    count = pairs.shape[1]
    groups = width // 128
    row_spec = pl.BlockSpec((1, rows, 128), lambda m, g: (m, 0, g))
    key_spec = pl.BlockSpec((1, count, 128), lambda m, g: (m, 0, g))
    value_spec = pl.BlockSpec((1, count, 128), lambda m, g: (m, 0, g + groups))
    lse_spec = pl.BlockSpec((1, 1, 2, rows), lambda m, g: (m, g, 0, 0))
    return pl.pallas_call(
        cross_backward_kernel,
        grid=(micro, groups),
        in_specs=[
            pl.BlockSpec(memory_space=pltpu.SMEM),
            row_spec,
            key_spec,
            value_spec,
            row_spec,
            lse_spec,
            row_spec,
        ],
        out_specs=[row_spec, key_spec, key_spec],
        out_shape=[
            jax.ShapeDtypeStruct((micro, rows, width), bf16),
            jax.ShapeDtypeStruct((micro, count, width), bf16),
            jax.ShapeDtypeStruct((micro, count, width), bf16),
        ],
        compiler_params=pltpu.CompilerParams(vmem_limit_bytes=32 << 20),
        name="cross_backward",
    )(lengths, queries, pairs, pairs, out, lse, gout)


def gelu_parts(v):
    inner = 0.7978845608028654 * (v + 0.044715 * (v * v * v))
    t = jnp.tanh(inner)
    value = 0.5 * v * (1.0 + t)
    slope = 0.5 * (1.0 + t) + 0.5 * v * (1.0 - t * t) * (
        0.7978845608028654 * (1.0 + 3.0 * 0.044715 * (v * v))
    )
    return value, slope


def per_device(
    tokens,
    memory,
    cotangent,
    tile_segment,
    parents,
    memory_lengths,
    self_qkv,
    self_out,
    cross_q,
    cross_kv,
    cross_out,
    ffn_in,
    ffn_out,
    norm_gain,
    norm_bias,
):
    micro, _, row_count, width = tokens.shape
    seq = lax.axis_size("seq")
    total_rows = micro * row_count
    memory_rows = memory.shape[2]

    devices = seq * lax.axis_size("fsdp")
    z_size, y_size = seq // 2, lax.axis_size("fsdp") // 2

    def flat(blocks):
        return blocks.reshape(-1, blocks.shape[-1])

    joint_weight = flat(gather_first([self_qkv], ("all",), ((0,),), z_size, y_size, 4)[0])

    x = tokens.reshape(total_rows, width)
    x32 = x.astype(f32)
    bias = jax.vmap(lambda t, p: tree_bias(t, p, BLOCK))(tile_segment[:, 0], parents[:, 0])
    lengths = memory_lengths[:, 0]

    projected = dot_nn(x, joint_weight).astype(bf16)
    gathered = self_forward(
        projected.reshape(micro, row_count, 3 * width),
        bias,
        seq,
        [
            self_out,
            jnp.concatenate([norm_gain, norm_bias], 0).astype(f32),
            cross_q,
            cross_kv,
            memory.reshape(micro * memory_rows, width),
            cross_out,
            ffn_in,
            ffn_out,
        ],
        ("all", "all", "all", "all", "seq", "all", "all", "all"),
        ((0, 1), (2, 4), (3,), (5,), (6,), (7,)),
        y_size,
    )
    qkv, attended_heads, self_lse, attended = gathered[:4]
    self_output, cross_weight, pair_weight = (flat(gathered[i]) for i in (4, 6, 7))
    cross_output, upward_weight, down_weight = (flat(gathered[i]) for i in (9, 10, 11))
    norms = gathered[5].reshape(devices, 6, width // devices).transpose(1, 0, 2).reshape(6, width)
    gain_rows, bias_rows = norms[:3], norms[3:]
    memory_full = gathered[8].reshape(seq, micro, memory_rows, width).transpose(1, 0, 2, 3)
    memory_full = memory_full.reshape(micro, seq * memory_rows, width)
    attended = attended.reshape(total_rows, width)

    mixed_first = residual_weight * x32 + dot_nn(attended, self_output)
    hidden_first = layer_norm(mixed_first, gain_rows[0], bias_rows[0])
    hidden_first_low = hidden_first.astype(bf16)
    cross_query = dot_nn(hidden_first_low, cross_weight).astype(bf16)
    cross_query = cross_query.reshape(micro, row_count, width)
    count = memory_full.shape[1]
    pairs = dot_nn(memory_full.reshape(micro * count, width), pair_weight).astype(bf16)
    pairs = pairs.reshape(micro, count, 2 * width)
    cross_heads, cross_lse = cross_forward(lengths, cross_query, pairs)
    cross_attended = cross_heads.reshape(total_rows, width)
    mixed_second = residual_weight * hidden_first + dot_nn(cross_attended, cross_output)
    hidden_second = layer_norm(mixed_second, gain_rows[1], bias_rows[1])
    hidden_second_low = hidden_second.astype(bf16)
    pre_active = dot_nn(hidden_second_low, upward_weight)
    active = gelu_parts(pre_active)[0].astype(bf16)
    mixed_third = residual_weight * hidden_second + dot_nn(active, down_weight)
    output = layer_norm(mixed_third, gain_rows[2], bias_rows[2]).astype(bf16)

    upstream = cotangent.reshape(total_rows, width).astype(f32)
    grad_third, gain_third, bias_third = layer_norm_back(mixed_third, gain_rows[2], upstream)
    branch_third = grad_third.astype(bf16)
    grad_down = dot_tn(active, branch_third).astype(bf16)
    grad_inner = (gelu_parts(pre_active)[1] * dot_nt(branch_third, down_weight)).astype(bf16)
    grad_upward = dot_tn(hidden_second_low, grad_inner).astype(bf16)

    grad_hidden_second = residual_weight * grad_third + dot_nt(grad_inner, upward_weight)
    grad_second, gain_second, bias_second = layer_norm_back(
        mixed_second, gain_rows[1], grad_hidden_second
    )
    branch_second = grad_second.astype(bf16)
    grad_cross_output = dot_tn(cross_attended, branch_second).astype(bf16)
    grad_cross_attended = dot_nt(branch_second, cross_output).astype(bf16)
    grad_cross_low, grad_keys, grad_values = cross_backward(
        lengths,
        cross_query,
        pairs,
        cross_heads,
        cross_lse,
        grad_cross_attended.reshape(micro, row_count, width),
    )
    memory_partial = jnp.concatenate([grad_keys, grad_values], 2)
    own_pairs = lax.psum_scatter(memory_partial, "seq", scatter_dimension=1, tiled=True)
    grad_cross_low = grad_cross_low.reshape(total_rows, width)
    grad_cross_weight = dot_tn(hidden_first_low, grad_cross_low).astype(bf16)
    grad_hidden_first = residual_weight * grad_second + dot_nt(grad_cross_low, cross_weight)
    grad_first, gain_first, bias_first = layer_norm_back(
        mixed_first, gain_rows[0], grad_hidden_first
    )
    branch_first = grad_first.astype(bf16)
    grad_self_output = dot_tn(attended, branch_first).astype(bf16)
    grad_attended = dot_nt(branch_first, self_output).astype(bf16)
    grad_projected, own_upward, own_down = self_backward(
        grad_attended.reshape(micro, row_count, width),
        qkv,
        bias,
        attended_heads,
        self_lse,
        seq,
        [grad_upward, grad_down],
        (True, False),
        y_size,
    )
    grad_projected = grad_projected.reshape(total_rows, 3 * width)
    grad_joint = dot_tn(x, grad_projected).astype(bf16)
    grad_tokens = (residual_weight * grad_first + dot_nt(grad_projected, joint_weight)).astype(bf16)
    grad_pairs_low = own_pairs.reshape(micro * memory_rows, 2 * width)
    grad_pair_weight = dot_tn(memory.reshape(micro * memory_rows, width), grad_pairs_low)
    grad_memory = dot_nt(grad_pairs_low, pair_weight).astype(bf16)
    norm_grads = jnp.stack(
        [gain_first, gain_second, gain_third, bias_first, bias_second, bias_third]
    )
    norm_blocks = norm_grads.reshape(6, devices, width // devices).transpose(1, 0, 2)
    owned = scatter_grads(
        [
            grad_joint,
            grad_self_output,
            grad_pair_weight.astype(bf16),
            grad_cross_weight,
            grad_cross_output,
            norm_blocks.reshape(6 * devices, width // devices),
        ],
        (True, True, False, False, False, False),
        z_size,
        y_size,
        3,
    )
    return (
        output.reshape(tokens.shape),
        grad_tokens.reshape(tokens.shape),
        grad_memory.reshape(memory.shape),
        owned[0],
        owned[1],
        owned[3],
        owned[2],
        owned[4],
        own_upward,
        own_down,
        owned[5][:3],
        owned[5][3:],
    )


def solution(mesh):
    rows = P(None, "fsdp", "seq", None)
    weight = P(ALL, None)
    in_specs = (
        rows,
        rows,
        rows,
        P(None, "fsdp", None),
        P(None, "fsdp", None),
        P(None, "fsdp"),
    ) + (weight,) * 7 + (P(None, ALL),) * 2
    out_specs = (rows, rows, rows) + (weight,) * 7 + (P(None, ALL),) * 2
    return jax.shard_map(
        per_device, mesh=mesh, in_specs=in_specs, out_specs=out_specs, check_vma=False
    )
```

```python
import functools

import jax
import jax.numpy as jnp
from jax import lax
from jax.experimental import pallas as pl
from jax.experimental.pallas import tpu as pltpu
from jax.sharding import PartitionSpec as P

H = 16
HD = 64
TILE = 128
BLOCK = 256
WINDOW = 4
GATHER_END = 75
SPLIT_ELEMENTS = 96 << 10
SCATTER_END = 75

scale_factor = 0.125
residual_weight = 36.0**0.25
norm_epsilon = 1e-05
masked_score = -1e30
ALL = ("seq", "fsdp")
f32 = jnp.float32
bf16 = jnp.bfloat16
MESH = pl.DeviceIdType.MESH


def dot_nn(a, b):
    return lax.dot_general(a, b, (((1,), (0,)), ((), ())), preferred_element_type=f32)


def dot_nt(a, b):
    return lax.dot_general(a, b, (((1,), (1,)), ((), ())), preferred_element_type=f32)


def dot_tn(a, b):
    return lax.dot_general(a, b, (((0,), (0,)), ((), ())), preferred_element_type=f32)


def norm_stats(incoming):
    row_mean = jnp.mean(incoming, -1, keepdims=True)
    centred = incoming - row_mean
    variance = jnp.mean(centred * centred, -1, keepdims=True)
    return centred, lax.rsqrt(variance + norm_epsilon)


def layer_norm(incoming, gain_row, bias_row):
    centred, inverse = norm_stats(incoming)
    return centred * inverse * gain_row + bias_row


def layer_norm_back(incoming, gain_row, upstream):
    centred, inverse = norm_stats(incoming)
    normal = centred * inverse
    grad_bias = jnp.sum(upstream, 0)
    grad_gain = jnp.sum(upstream * normal, 0)
    scaled = upstream * gain_row
    grad = inverse * (
        scaled
        - jnp.mean(scaled, -1, keepdims=True)
        - normal * jnp.mean(scaled * normal, -1, keepdims=True)
    )
    return grad, grad_gain, grad_bias


def ancestors(parent_ids):
    segment_ids = jnp.arange(parent_ids.shape[0], dtype=jnp.int32)
    hop = (parent_ids[:, None] == segment_ids[None, :]).astype(f32)
    reach = jnp.maximum(hop, (segment_ids[:, None] == segment_ids[None, :]).astype(f32))
    steps = 1
    while steps < parent_ids.shape[0]:
        reach = jnp.minimum(jnp.dot(reach, reach, precision=lax.Precision.HIGHEST), 1.0)
        steps *= 2
    return reach


def tree_bias(tile_segments, parent_ids, block):
    tiles = tile_segments.shape[0]
    onehot = (
        tile_segments[:, None] == jnp.arange(parent_ids.shape[0], dtype=jnp.int32)[None, :]
    ).astype(f32)
    high = lax.Precision.HIGHEST
    related = jnp.dot(
        jnp.dot(onehot, ancestors(parent_ids), precision=high), onehot.T, precision=high
    )
    bias = jnp.where(related > 0.5, 0.0, masked_score)
    per = block // TILE
    blocks = tiles // per
    bias = bias.reshape(blocks, per, blocks, per).transpose(2, 0, 3, 1)
    return jnp.repeat(bias, TILE, axis=3)


def head_masks(shape, heads):
    lane = lax.broadcasted_iota(jnp.int32, shape, 1)
    return [(lane >= h * HD) & (lane < (h + 1) * HD) for h in range(heads)]


def keep_head(value, mask, heads):
    return value if heads == 1 else jnp.where(mask, value, jnp.zeros_like(value))


def greet(peers):
    barrier = pltpu.get_barrier_semaphore()
    for peer in peers:
        pl.semaphore_signal(barrier, inc=1, device_id=peer, device_id_type=MESH)
    pl.semaphore_wait(barrier, len(peers))


def peer_at(step):
    count = lax.axis_size("seq")
    return lax.rem(lax.axis_index("seq") + step, count)


def rows_at(i, count):
    return pl.ds(pl.multiple_of(i * count, count), count)


def cut_heads(rows_ref, m, parts, blocks_ref):
    seq, part = blocks_ref.shape[2], blocks_ref.shape[4]
    for p in range(parts):
        for s in range(seq):
            first = (p * seq + s) * part
            blocks_ref[m, p, s] = rows_ref[m, :, first : first + part]


def join_heads(blocks_ref, m, parts, rows_ref):
    seq, part = blocks_ref.shape[2], blocks_ref.shape[4]
    for p in range(parts):
        for s in range(seq):
            first = (p * seq + s) * part
            rows_ref[m, :, first : first + part] = blocks_ref[m, p, s]


def to_peer(source_ref, target_ref, send, receive, m, step):
    rows = source_ref.shape[3]
    return pltpu.make_async_remote_copy(
        src_ref=source_ref.at[m, :, peer_at(step)],
        dst_ref=target_ref.at[m, :, rows_at(lax.axis_index("seq"), rows)],
        send_sem=send.at[m, step],
        recv_sem=receive.at[m, step],
        device_id={"seq": peer_at(step)},
        device_id_type=MESH,
    )


def to_self(source_ref, target_ref, sem, m):
    rows = source_ref.shape[3]
    me = lax.axis_index("seq")
    return pltpu.make_async_copy(
        source_ref.at[m, :, me], target_ref.at[m, :, rows_at(me, rows)], sem.at[m, 0]
    )


def send_blocks(source_ref, target_ref, send, receive, m):
    for step in range(1, lax.axis_size("seq")):
        to_peer(source_ref, target_ref, send, receive, m, step).start()
    to_self(source_ref, target_ref, send, m).start()


def take_blocks(source_ref, target_ref, send, receive, m, between=None):
    for step in range(1, lax.axis_size("seq")):
        to_peer(source_ref, target_ref, send, receive, m, step).wait_recv()
        if between is not None:
            between(step)
    to_self(source_ref, target_ref, send, m).wait()


def home_copy(source_ref, target_ref, send, receive, m, place):
    rows = target_ref.shape[3]
    me = lax.axis_index("seq")
    count = lax.axis_size("seq")
    step = lax.rem(place - me + count, count)
    return pltpu.make_async_remote_copy(
        src_ref=source_ref.at[m, :, rows_at(place, rows)],
        dst_ref=target_ref.at[m, :, me],
        send_sem=send.at[m, step],
        recv_sem=receive.at[m, step],
        device_id={"seq": place},
        device_id_type=MESH,
    )


def home_self(source_ref, target_ref, sem, m):
    rows = target_ref.shape[3]
    me = lax.axis_index("seq")
    return pltpu.make_async_copy(
        source_ref.at[m, :, rows_at(me, rows)], target_ref.at[m, :, me], sem.at[m, 0]
    )


def send_home(source_ref, target_ref, send, receive, m, place):
    me = lax.axis_index("seq")

    @pl.when(place != me)
    def _():
        home_copy(source_ref, target_ref, send, receive, m, place).start()

    @pl.when(place == me)
    def _():
        home_self(source_ref, target_ref, send, m).start()


def take_home(source_ref, target_ref, send, receive, m):
    for step in range(1, lax.axis_size("seq")):
        home_copy(source_ref, target_ref, send, receive, m, peer_at(step)).wait()
    home_self(source_ref, target_ref, send, m).wait()


def scatter_places():
    s, f = lax.axis_index("seq"), lax.axis_index("fsdp")
    z, y = s // 2, f // 2
    return z, s - 2 * z, y, f - 2 * y, lax.axis_size("seq") // 2, lax.axis_size("fsdp") // 2


def scatter_peers():
    z, x, y, c, z_size, y_size = scatter_places()
    peers = [{"fsdp": 2 * y + 1 - c}, {"seq": 2 * z + 1 - x}]
    peers += [{"fsdp": 2 * lax.rem(y + k, y_size) + c} for k in range(1, y_size)]
    peers += [{"seq": 2 * lax.rem(z + k, z_size) + x} for k in range(1, z_size)]
    return peers


def scatter_shapes(blocks, x_first):
    if x_first == "seq":
        z_size, _, rows, columns = blocks.shape
        shape = (z_size, rows, columns)
        return [pltpu.VMEM(shape, blocks.dtype)] * 2 + [
            pltpu.VMEM((z_size - 1, rows, columns), blocks.dtype)
        ]
    z_size, _, y_size, _, rows, columns = blocks.shape
    if x_first:
        first, second = (1, y_size), (y_size - 1,)
    else:
        first, second = (y_size - 1, 2), (1,)
    kind = blocks.dtype
    return [
        pltpu.VMEM((z_size, 2, y_size, rows, columns), kind),
        pltpu.VMEM((z_size, 2, y_size, rows, columns), kind),
        pltpu.VMEM((z_size,) + first + (rows, columns), kind),
        pltpu.VMEM((z_size,) + second + (rows, columns), kind),
        pltpu.VMEM((z_size - 1, rows, columns), kind),
    ]


def scatter_sems(count, z_size, y_size):
    pair = pltpu.SemaphoreType.DMA((count, z_size))
    triple = pltpu.SemaphoreType.DMA((count, z_size, max(1, y_size - 1)))
    return [pair, pair, pair, triple, triple, triple, triple, pair, pair]


def add_into(target, source):
    target[...] = target[...] + source[...]


def scatter_steps(kinds, sources, outs, buffers, sems):
    z, x, y, c, z_size, y_size = scatter_places()
    local, core_s, core_r, first_s, first_r, second_s, second_r, last_s, last_r = sems
    count = len(sources)

    def to_z(t):
        return lax.rem(z + 1 + t, z_size)

    def remote(source, target, send, receive, peer):
        return pltpu.make_async_remote_copy(
            src_ref=source,
            dst_ref=target,
            send_sem=send,
            recv_sem=receive,
            device_id=peer,
            device_id_type=MESH,
        )

    across = [a for a in range(count) if kinds[a] != "seq"]
    along = [a for a in range(count) if kinds[a] == "seq"]

    def own_copy(a, t):
        if kinds[a] == "seq":
            source = sources[a].at[to_z(t), x]
        else:
            source = sources[a].at[to_z(t), :, :, c]
        return pltpu.make_async_copy(source, buffers[a][0].at[t], local.at[a, t])

    def seq_first(a, t):
        return remote(
            sources[a].at[to_z(t), 1 - x],
            buffers[a][1].at[t],
            core_s.at[a, t],
            core_r.at[a, t],
            x_peer(),
        )

    def seq_last(a, t):
        return remote(
            buffers[a][0].at[t],
            buffers[a][2].at[t],
            last_s.at[a, t],
            last_r.at[a, t],
            {"seq": 2 * to_z(t) + x},
        )

    def core_copy(a, t):
        return remote(
            sources[a].at[to_z(t), :, :, 1 - c],
            buffers[a][1].at[t],
            core_s.at[a, t],
            core_r.at[a, t],
            {"fsdp": 2 * y + 1 - c},
        )

    def x_peer():
        return {"seq": 2 * z + 1 - x}

    def y_place(k):
        return lax.rem(y + k, y_size)

    def y_peer(k):
        return {"fsdp": 2 * y_place(k) + c}

    def first_copies(a, t):
        own, _, first, _, _ = buffers[a]
        if kinds[a]:
            sends = [(own.at[t, 1 - x], x_peer())]
        else:
            sends = [(own.at[t, :, y_place(k)], y_peer(k)) for k in range(1, y_size)]
        return [
            remote(source, first.at[t, k], first_s.at[a, t, k], first_r.at[a, t, k], peer)
            for k, (source, peer) in enumerate(sends)
        ]

    def second_copies(a, t):
        own, _, _, second, _ = buffers[a]
        if kinds[a]:
            sends = [(own.at[t, x, y_place(k)], y_peer(k)) for k in range(1, y_size)]
        else:
            sends = [(own.at[t, 1 - x, y], x_peer())]
        return [
            remote(source, second.at[t, k], second_s.at[a, t, k], second_r.at[a, t, k], peer)
            for k, (source, peer) in enumerate(sends)
        ]

    def last_copy(a, t):
        own, _, _, _, last = buffers[a]
        return remote(
            own.at[t, x, y],
            last.at[t],
            last_s.at[a, t],
            last_r.at[a, t],
            {"seq": 2 * to_z(t) + x},
        )

    def start_core(t):
        for a in range(count):
            (core_copy if a in across else seq_first)(a, t).start()
            own_copy(a, t).start()

    def core_step(t):
        for a in across:
            core_copy(a, t).wait_recv()
            own_copy(a, t).wait()
            own, core = buffers[a][:2]

            def add(i, carry, own=own, core=core):
                add_into(own.at[t, i // y_size, i % y_size], core.at[t, i // y_size, i % y_size])
                return carry

            lax.fori_loop(0, 2 * y_size, add, 0)
            for copy in first_copies(a, t):
                copy.start()
        if t + 2 < z_size:
            start_core(t + 2)

    def first_step(t):
        for a in across:
            own, _, first, _, _ = buffers[a]
            for k, copy in enumerate(first_copies(a, t)):
                copy.wait_recv()
                for i in range(y_size if kinds[a] else 2):
                    target = own.at[t, x, i] if kinds[a] else own.at[t, i, y]
                    add_into(target, first.at[t, k, i])
            for copy in second_copies(a, t):
                copy.start()

    def second_step(t):
        for a in along:
            seq_first(a, t).wait_recv()
            own_copy(a, t).wait()
            add_into(buffers[a][0].at[t], buffers[a][1].at[t])
            if t < z_size - 1:
                seq_last(a, t).start()
        for a in across:
            own, _, _, second, _ = buffers[a]
            for k, copy in enumerate(second_copies(a, t)):
                copy.wait_recv()
                add_into(own.at[t, x, y], second.at[t, k])
            if t < z_size - 1:
                last_copy(a, t).start()

    def final_step():
        for a in along:
            own, _, last = buffers[a]
            total = own[z_size - 1].astype(f32)
            for t in range(z_size - 1):
                seq_last(a, t).wait()
                total = total + last[t].astype(f32)
            outs[a][...] = total
            for t in range(z_size):
                seq_first(a, t).wait_send()
        for a in across:
            own, _, _, _, last = buffers[a]
            total = own[z_size - 1, x, y].astype(f32)
            for t in range(z_size - 1):
                last_copy(a, t).wait()
                total = total + last[t].astype(f32)
            outs[a][...] = total
            for t in range(z_size):
                core_copy(a, t).wait_send()
                for copy in first_copies(a, t) + second_copies(a, t):
                    copy.wait_send()

    def opening():
        start_core(0)
        if z_size > 1:
            start_core(1)

    steps = [opening]
    for t in range(z_size + 2):
        if t < z_size:
            steps.append(functools.partial(core_step, t))
        if 0 <= t - 1 < z_size:
            steps.append(functools.partial(first_step, t - 1))
        if 0 <= t - 2 < z_size:
            steps.append(functools.partial(second_step, t - 2))
    steps.append(final_step)
    return steps


def scatter_buffers(kinds, refs):
    buffers = []
    for kind in kinds:
        size = 3 if kind == "seq" else 5
        buffers.append(refs[:size])
        refs = refs[size:]
    return buffers, refs


def scatter_kernel(kinds, *refs):
    count = len(kinds)
    sources, outs, rest = refs[:count], refs[count : 2 * count], refs[2 * count :]
    buffers, rest = scatter_buffers(kinds, rest)
    greet(scatter_peers())
    for step in scatter_steps(kinds, sources, outs, buffers, rest):
        step()


def scatter_blocks(arrays, kinds, z_size, y_size):
    blocks = []
    for a, kind in zip(arrays, kinds):
        lead = (z_size, 2) if kind == "seq" else (z_size, 2, y_size, 2)
        blocks.append(a.reshape(lead + (-1, a.shape[1])))
    return blocks


def scatter_grads(arrays, kinds, z_size, y_size, collective_id):
    blocks = scatter_blocks(arrays, kinds, z_size, y_size)
    scratch = []
    for block, kind in zip(blocks, kinds):
        scratch += scatter_shapes(block, kind)
    return pl.pallas_call(
        functools.partial(scatter_kernel, kinds),
        in_specs=[pl.BlockSpec(memory_space=pl.ANY)] * len(arrays),
        out_specs=[pl.BlockSpec(memory_space=pltpu.VMEM)] * len(arrays),
        out_shape=[jax.ShapeDtypeStruct(b.shape[-2:], f32) for b in blocks],
        scratch_shapes=scratch + scatter_sems(len(arrays), z_size, y_size),
        compiler_params=pltpu.CompilerParams(
            vmem_limit_bytes=60 << 20, collective_id=collective_id, has_side_effects=True
        ),
        name="scatter_grads",
    )(*blocks)


def spread(steps, first, last):
    return [(first + k * (last - first) // max(1, len(steps) - 1), s) for k, s in enumerate(steps)]


def run_slot(placed, slot):
    for at, step in placed:
        pl.when(slot == at)(step)


def both_peers():
    _, _, y, c, _, y_size = scatter_places()
    peers = [{"seq": peer_at(step)} for step in range(1, lax.axis_size("seq"))]
    peers += [{"fsdp": 2 * y + 1 - c}]
    return peers + [{"fsdp": 2 * lax.rem(y + k, y_size) + c} for k in range(1, y_size)]


def gather_parts(shards, kinds, groups):
    parts, units = [], []
    for group in groups:
        pieces = []
        for a in group:
            rows, columns = shards[a].shape
            kind = kinds[a]
            split = 2 if rows % 32 == 0 and rows * columns >= SPLIT_ELEMENTS else 1
            for n in range(split):
                cut = (n * columns // split, columns // split)
                if kind == "seq" or rows % 32:
                    piece = [(a, 0, rows) + cut + ("x" if kind == "all" else kind,)]
                else:
                    half = rows // 2
                    piece = [(a, 0, half) + cut + ("x",), (a, half, half) + cut + ("y",)]
                if n == len(pieces):
                    pieces.append([])
                pieces[n] += piece
        for piece in pieces:
            units.append(range(len(parts), len(parts) + len(piece)))
            parts += piece
    return parts, units


def gather_sems(plan, z_size, y_size):
    count = len(plan[0])
    z_sem = pltpu.SemaphoreType.DMA((count, z_size))
    y_sem = pltpu.SemaphoreType.DMA((count, max(1, y_size - 1)))
    one = pltpu.SemaphoreType.DMA((count, 1))
    return [z_sem, z_sem, y_sem, y_sem, y_sem, y_sem, one, one]


def gather_steps(plan, shards, outs, sems):
    z, x, y, c, z_size, y_size = scatter_places()
    z_s, z_r, first_s, first_r, second_s, second_r, core_s, core_r = sems
    parts, units = plan

    def remote(view, peer, send, receive):
        return pltpu.make_async_remote_copy(
            src_ref=view,
            dst_ref=view,
            send_sem=send,
            recv_sem=receive,
            device_id=peer,
            device_id_type=MESH,
        )

    def shard_of(p):
        a, start, rows, left, columns, _ = parts[p]
        return shards[a].at[pl.ds(start, rows), pl.ds(left, columns)]

    def place(p, *lead):
        a, start, rows, left, columns, _ = parts[p]
        return outs[a].at[lead + (pl.ds(start, rows), pl.ds(left, columns))]

    def own(p):
        return place(p, z, x) if parts[p][-1] == "seq" else place(p, z, x, y, c)

    def own_copy(p):
        return pltpu.make_async_copy(shard_of(p), own(p), z_s.at[p, 0])

    def z_copies(p):
        return [
            pltpu.make_async_remote_copy(
                src_ref=shard_of(p),
                dst_ref=own(p),
                send_sem=z_s.at[p, k],
                recv_sem=z_r.at[p, k],
                device_id={"seq": 2 * lax.rem(z + k, z_size) + x},
                device_id_type=MESH,
            )
            for k in range(1, z_size)
        ]

    def x_peer():
        return {"seq": 2 * z + 1 - x}

    def y_peers():
        return [{"fsdp": 2 * lax.rem(y + k, y_size) + c} for k in range(1, y_size)]

    whole = slice(None)

    def first_copies(p):
        kind = parts[p][-1]
        view = place(p, whole, x) if kind == "seq" else place(p, whole, x, y, c)
        peers = y_peers() if kind == "y" else [x_peer()]
        return [
            remote(view, peer, first_s.at[p, k], first_r.at[p, k]) for k, peer in enumerate(peers)
        ]

    def second_copies(p):
        kind = parts[p][-1]
        if kind == "seq":
            return []
        view = place(p, whole, whole, y, c) if kind == "x" else place(p, whole, x, whole, c)
        peers = y_peers() if kind == "x" else [x_peer()]
        return [
            remote(view, peer, second_s.at[p, k], second_r.at[p, k]) for k, peer in enumerate(peers)
        ]

    def core_copies(p):
        if parts[p][-1] == "seq":
            return []
        view = place(p, whole, whole, whole, c)
        return [remote(view, {"fsdp": 2 * y + 1 - c}, core_s.at[p, 0], core_r.at[p, 0])]

    def step(t):
        def unit(at):
            return units[at] if 0 <= at < len(units) else ()

        for p in unit(t - 3):
            for copy in second_copies(p):
                copy.wait_recv()
            for copy in core_copies(p):
                copy.start()
        for p in unit(t - 2):
            for copy in first_copies(p):
                copy.wait_recv()
            for copy in second_copies(p):
                copy.start()
        for p in unit(t - 1):
            for copy in z_copies(p):
                copy.wait_recv()
            own_copy(p).wait()
            for copy in first_copies(p):
                copy.start()
        for p in unit(t):
            for copy in z_copies(p):
                copy.start()
            own_copy(p).start()

    def final_step():
        for p in range(len(parts)):
            for copy in core_copies(p):
                copy.wait()
            for copy in z_copies(p) + first_copies(p) + second_copies(p):
                copy.wait_send()

    return [functools.partial(step, t) for t in range(len(units) + 3)] + [final_step]


def gather_out(shard, kind, z_size, y_size):
    lead = (z_size, 2) if kind == "seq" else (z_size, 2, y_size, 2)
    return jax.ShapeDtypeStruct(lead + shard.shape, shard.dtype)


def gather_kernel(plan, count, *refs):
    shards, outs, sems = refs[:count], refs[count : 2 * count], refs[2 * count :]
    greet(scatter_peers())
    for step in gather_steps(plan, shards, outs, sems):
        step()


def gather_first(shards, kinds, groups, z_size, y_size, collective_id):
    plan = gather_parts(shards, kinds, groups)
    return pl.pallas_call(
        functools.partial(gather_kernel, plan, len(shards)),
        in_specs=[pl.BlockSpec(memory_space=pl.ANY)] * len(shards),
        out_specs=[pl.BlockSpec(memory_space=pl.ANY)] * len(shards),
        out_shape=[gather_out(s, k, z_size, y_size) for s, k in zip(shards, kinds)],
        scratch_shapes=gather_sems(plan, z_size, y_size),
        compiler_params=pltpu.CompilerParams(collective_id=collective_id, has_side_effects=True),
        name="gather_first",
    )(*shards)


def self_forward_kernel(heads, block, plan, count, *refs):
    rows_ref, bias_ref = refs[:2]
    shards, refs = refs[2 : 2 + count], refs[2 + count :]
    qkv_ref, out_ref, lse_ref, attended_ref = refs[:4]
    whole, refs = refs[4 : 4 + count], refs[4 + count :]
    cut, back, queries, values_t, send_in, take_in, send_out, take_out = refs[:8]
    gather = gather_steps(plan, shards, whole, refs[8:])
    micro, _, length, width = qkv_ref.shape
    seq = lax.axis_size("seq")
    blocks = length // block
    per = block // TILE
    place_rows = length // seq
    masks = head_masks((block, width), heads)
    per_micro = blocks + seq - 1
    window = min(WINDOW, seq - 1)
    placed = spread(gather[1:-1], 0, GATHER_END * micro * per_micro // 100)
    greet(both_peers())

    def launch(m, carry):
        cut_heads(rows_ref, m, 3, cut)

        @pl.when(m < 1)
        def _():
            for step in range(1, window + 1):
                to_peer(cut, qkv_ref, send_in, take_in, m, step).start()

        to_self(cut, qkv_ref, send_in, m).start()
        return carry

    lax.fori_loop(0, micro, launch, 0)
    gather[0]()
    key_place = lax.broadcasted_iota(jnp.int32, (block, block), 0)
    query_place = lax.broadcasted_iota(jnp.int32, (block, block), 1)
    causal = key_place <= query_place

    def one_micro(m, carry):
        def between(step):
            run_slot(placed, m * per_micro + step - 1)
            if step + window < seq:
                to_peer(cut, qkv_ref, send_in, take_in, m, step + window).start()
            else:

                @pl.when(m + 1 < micro)
                def _():
                    following = step + window + 1 - seq
                    to_peer(cut, qkv_ref, send_in, take_in, m + 1, following).start()

        take_blocks(cut, qkv_ref, send_in, take_in, m, between)

        def prepare(i, carry):
            rows = rows_at(i, block)
            q = qkv_ref[m, 0, rows, :].astype(f32) * scale_factor
            for h in range(heads):
                queries[h, rows, :] = keep_head(q, masks[h], heads).astype(bf16)
            values_t[i] = jnp.transpose(qkv_ref[m, 2, rows, :].astype(f32)).astype(bf16)
            return carry

        lax.fori_loop(0, blocks, prepare, 0)

        def scores_of(i, j, h):
            raw = dot_nt(qkv_ref[m, 1, rows_at(j, block), :], queries[h, rows_at(i, block), :])
            bias = bias_ref[m, j, i]
            return (raw.reshape(per, TILE, block) + bias[:, None, :]).reshape(block, block)

        def query_block(i, carry):
            run_slot(placed, m * per_micro + seq - 1 + i)
            state = []
            for h in range(heads):
                s = jnp.where(causal, scores_of(i, i, h), masked_score)
                top = jnp.max(s, 0, keepdims=True)
                p = jnp.exp(s - top)
                total = jnp.sum(p, 0, keepdims=True)
                acc = dot_nn(values_t[i][h * HD : (h + 1) * HD], p.astype(bf16))
                state += [top, total, acc]

            def key_block(j, state):
                fresh = []
                for h in range(heads):
                    top, total, acc = state[3 * h : 3 * h + 3]
                    s = scores_of(i, j, h)
                    higher = jnp.maximum(top, jnp.max(s, 0, keepdims=True))
                    shrink = jnp.exp(top - higher)
                    p = jnp.exp(s - higher)
                    total = total * shrink + jnp.sum(p, 0, keepdims=True)
                    acc = acc * shrink + dot_nn(
                        values_t[j][h * HD : (h + 1) * HD], p.astype(bf16)
                    )
                    fresh += [higher, total, acc]
                return tuple(fresh)

            state = lax.fori_loop(0, i, key_block, tuple(state))
            out = jnp.concatenate(
                [state[3 * h + 2] * (1.0 / state[3 * h + 1]) for h in range(heads)], 0
            )
            out_ref[m, 0, rows_at(i, block), :] = jnp.transpose(out).astype(bf16)
            lse_ref[m, i] = jnp.concatenate(
                [state[3 * h] + jnp.log(state[3 * h + 1]) for h in range(heads)], 0
            )
            for sub in range(block // place_rows):
                place = i * (block // place_rows) + sub
                send_home(out_ref, back, send_out, take_out, m, place)
            return carry

        lax.fori_loop(0, blocks, query_block, 0)
        return carry

    lax.fori_loop(0, micro, one_micro, 0)

    def finish(m, carry):
        for step in range(1, seq):
            to_peer(cut, qkv_ref, send_in, take_in, m, step).wait_send()
        take_home(out_ref, back, send_out, take_out, m)
        join_heads(back, m, 1, attended_ref)
        return carry

    lax.fori_loop(0, micro, finish, 0)
    gather[-1]()


def self_forward(projected, bias, seq, shards, kinds, groups, y_size):
    micro, rows, width = projected.shape
    part = width // 3 // seq
    heads = part // HD
    length = rows * seq
    blocks = length // BLOCK
    whole = pl.BlockSpec(memory_space=pltpu.VMEM)
    sems = pltpu.SemaphoreType.DMA((micro, seq))
    count = len(shards)
    any_place = [pl.BlockSpec(memory_space=pl.ANY)] * count
    plan = gather_parts(shards, kinds, groups)
    return pl.pallas_call(
        functools.partial(self_forward_kernel, heads, BLOCK, plan, count),
        in_specs=[whole, whole] + any_place,
        out_specs=[whole] * 4 + any_place,
        out_shape=[
            jax.ShapeDtypeStruct((micro, 3, length, part), bf16),
            jax.ShapeDtypeStruct((micro, 1, length, part), bf16),
            jax.ShapeDtypeStruct((micro, blocks, heads, BLOCK), f32),
            jax.ShapeDtypeStruct((micro, rows, width // 3), bf16),
        ]
        + [gather_out(s, k, seq // 2, y_size) for s, k in zip(shards, kinds)],
        scratch_shapes=[
            pltpu.VMEM((micro, 3, seq, rows, part), bf16),
            pltpu.VMEM((micro, 1, seq, rows, part), bf16),
            pltpu.VMEM((heads, length, part), bf16),
            pltpu.VMEM((blocks, part, BLOCK), bf16),
            sems,
            sems,
            sems,
            sems,
        ]
        + gather_sems(plan, seq // 2, y_size),
        compiler_params=pltpu.CompilerParams(
            vmem_limit_bytes=50 << 20, collective_id=1, has_side_effects=True
        ),
        name="self_forward",
    )(projected, bias, *shards)


def self_backward_kernel(heads, block, kinds, *refs):
    count = len(kinds)
    rows_ref, qkv_ref, bias_ref, out_ref, lse_ref = refs[:5]
    sources, refs = refs[5 : 5 + count], refs[5 + count :]
    grad_ref, owned, refs = refs[0], refs[1 : 1 + count], refs[1 + count :]
    cut, gout, grads, back, queries, keys_h, gouts, delta, grad_q = refs[:9]
    send_in, take_in, send_out, take_out = refs[9:13]
    buffers, refs = scatter_buffers(kinds, refs[13:])
    scatter = scatter_steps(kinds, sources, owned, buffers, refs)
    micro, _, length, width = qkv_ref.shape
    seq = lax.axis_size("seq")
    blocks = length // block
    per = block // TILE
    place_rows = length // seq
    masks = head_masks((block, width), heads)
    lane = lax.broadcasted_iota(jnp.int32, (8, width), 1)
    first_lane = lax.broadcasted_iota(jnp.int32, (8, width), 0) * HD
    pick = jnp.where((lane >= first_lane) & (lane < first_lane + HD), 1.0, 0.0)
    placed = spread(scatter[1:-1], 1, SCATTER_END * micro * blocks // 100)
    greet(both_peers())

    def launch(m, carry):
        cut_heads(rows_ref, m, 1, cut)
        send_blocks(cut, gout, send_in, take_in, m)
        return carry

    lax.fori_loop(0, micro, launch, 0)
    scatter[0]()
    key_place = lax.broadcasted_iota(jnp.int32, (block, block), 0)
    query_place = lax.broadcasted_iota(jnp.int32, (block, block), 1)
    causal = key_place <= query_place

    def one_micro(m, carry):
        take_blocks(cut, gout, send_in, take_in, m)

        def prepare(i, carry):
            rows = rows_at(i, block)
            q = qkv_ref[m, 0, rows, :].astype(f32) * scale_factor
            k = qkv_ref[m, 1, rows, :].astype(f32)
            g = gout[m, 0, rows, :].astype(f32)
            for h in range(heads):
                queries[h, rows, :] = keep_head(q, masks[h], heads).astype(bf16)
                keys_h[h, rows, :] = keep_head(k, masks[h], heads).astype(bf16)
                gouts[h, rows, :] = keep_head(g, masks[h], heads).astype(bf16)
            delta[i] = lax.dot_general(
                pick,
                g * out_ref[m, 0, rows, :].astype(f32),
                (((1,), (1,)), ((), ())),
                precision=lax.Precision.HIGHEST,
                preferred_element_type=f32,
            )
            grad_q[rows, :] = jnp.zeros((block, width), f32)
            return carry

        lax.fori_loop(0, blocks, prepare, 0)

        def key_block(j, carry):
            run_slot(placed, m * blocks + j)
            krows = rows_at(j, block)

            def pair(i, grad_k, grad_v, diagonal):
                rows = rows_at(i, block)
                bias = bias_ref[m, j, i]
                gq = grad_q[rows, :]
                for h in range(heads):
                    raw = dot_nt(qkv_ref[m, 1, krows, :], queries[h, rows, :])
                    shift = bias - lse_ref[m, i, h : h + 1, :]
                    s = (raw.reshape(per, TILE, block) + shift[:, None, :]).reshape(block, block)
                    if diagonal:
                        s = jnp.where(causal, s, masked_score)
                    p = jnp.exp(s)
                    gp = dot_nt(qkv_ref[m, 2, krows, :], gouts[h, rows, :])
                    gs = (p * (gp - delta[i, h : h + 1, :])).astype(bf16)
                    grad_v = grad_v + dot_nn(p.astype(bf16), gouts[h, rows, :])
                    grad_k = grad_k + dot_nn(gs, queries[h, rows, :])
                    gq = gq + dot_tn(gs, keys_h[h, krows, :])
                grad_q[rows, :] = gq
                return grad_k, grad_v

            zero = jnp.zeros((block, width), f32)
            state = pair(j, zero, zero, True)
            state = lax.fori_loop(
                j + 1, blocks, lambda i, s: pair(i, s[0], s[1], False), state
            )
            grads[m, 0, krows, :] = (grad_q[krows, :] * scale_factor).astype(bf16)
            grads[m, 1, krows, :] = state[0].astype(bf16)
            grads[m, 2, krows, :] = state[1].astype(bf16)
            for sub in range(block // place_rows):
                place = j * (block // place_rows) + sub
                send_home(grads, back, send_out, take_out, m, place)
            return carry

        lax.fori_loop(0, blocks, key_block, 0)
        return carry

    lax.fori_loop(0, micro, one_micro, 0)

    def finish(m, carry):
        for step in range(1, seq):
            to_peer(cut, gout, send_in, take_in, m, step).wait_send()
        take_home(grads, back, send_out, take_out, m)
        join_heads(back, m, 3, grad_ref)
        return carry

    scatter[-1]()
    lax.fori_loop(0, micro, finish, 0)


def self_backward(grad_attended, qkv, bias, out, lse, seq, arrays, kinds, y_size):
    micro, rows, width = grad_attended.shape
    length, part = qkv.shape[2:]
    heads = part // HD
    blocks = length // BLOCK
    whole = pl.BlockSpec(memory_space=pltpu.VMEM)
    sems = pltpu.SemaphoreType.DMA((micro, seq))
    sources = scatter_blocks(arrays, kinds, seq // 2, y_size)
    count = len(arrays)
    scratch = []
    for source, kind in zip(sources, kinds):
        scratch += scatter_shapes(source, kind)
    return pl.pallas_call(
        functools.partial(self_backward_kernel, heads, BLOCK, kinds),
        in_specs=[whole] * 5 + [pl.BlockSpec(memory_space=pl.ANY)] * count,
        out_specs=[whole] * (1 + count),
        out_shape=[jax.ShapeDtypeStruct((micro, rows, 3 * width), bf16)]
        + [jax.ShapeDtypeStruct(b.shape[-2:], f32) for b in sources],
        scratch_shapes=[
            pltpu.VMEM((micro, 1, seq, rows, part), bf16),
            pltpu.VMEM((micro, 1, length, part), bf16),
            pltpu.VMEM((micro, 3, length, part), bf16),
            pltpu.VMEM((micro, 3, seq, rows, part), bf16),
            pltpu.VMEM((heads, length, part), bf16),
            pltpu.VMEM((heads, length, part), bf16),
            pltpu.VMEM((heads, length, part), bf16),
            pltpu.VMEM((blocks, 8, BLOCK), f32),
            pltpu.VMEM((length, part), f32),
            sems,
            sems,
            sems,
            sems,
        ]
        + scratch
        + scatter_sems(count, seq // 2, y_size),
        compiler_params=pltpu.CompilerParams(
            vmem_limit_bytes=60 << 20, collective_id=2, has_side_effects=True
        ),
        name="self_backward",
    )(grad_attended, qkv, bias, out, lse, *sources)


def cross_forward_kernel(lengths_ref, q_ref, pairs_ref, out_ref, lse_ref):
    count, width, rows = pairs_ref.shape[1], q_ref.shape[2], q_ref.shape[1]
    masks = head_masks((rows, 128), 2)
    valid = (
        lax.broadcasted_iota(jnp.int32, (count, rows), 0) < lengths_ref[pl.program_id(0)]
    )
    for g in range(width // 128):
        cut = slice(g * 128, g * 128 + 128)
        q = q_ref[0, :, cut].astype(f32) * scale_factor
        values = pairs_ref[0, :, width + g * 128 : width + g * 128 + 128]
        values_t = jnp.transpose(values.astype(f32)).astype(bf16)
        outs, lses = [], []
        for h in range(2):
            s = dot_nt(pairs_ref[0, :, cut], keep_head(q, masks[h], 2).astype(bf16))
            s = jnp.where(valid, s, masked_score)
            m = jnp.max(s, 0, keepdims=True)
            p = jnp.exp(s - m)
            total = jnp.sum(p, 0, keepdims=True)
            out = dot_nn(values_t[h * HD : (h + 1) * HD], p.astype(bf16))
            outs.append(out * (1.0 / total))
            lses.append(m + jnp.log(total))
        out_ref[0, :, cut] = jnp.transpose(jnp.concatenate(outs, 0)).astype(bf16)
        lse_ref[0, g] = jnp.concatenate(lses, 0)


def cross_forward(lengths, queries, pairs):
    micro, rows, width = queries.shape
    count = pairs.shape[1]
    groups = width // 128
    return pl.pallas_call(
        cross_forward_kernel,
        grid=(micro,),
        in_specs=[
            pl.BlockSpec(memory_space=pltpu.SMEM),
            pl.BlockSpec((1, rows, width), lambda m: (m, 0, 0)),
            pl.BlockSpec((1, count, 2 * width), lambda m: (m, 0, 0)),
        ],
        out_specs=[
            pl.BlockSpec((1, rows, width), lambda m: (m, 0, 0)),
            pl.BlockSpec((1, groups, 2, rows), lambda m: (m, 0, 0, 0)),
        ],
        out_shape=[
            jax.ShapeDtypeStruct((micro, rows, width), bf16),
            jax.ShapeDtypeStruct((micro, groups, 2, rows), f32),
        ],
        compiler_params=pltpu.CompilerParams(vmem_limit_bytes=32 << 20),
        name="cross_forward",
    )(lengths, queries, pairs)


def cross_backward_kernel(
    lengths_ref, q_ref, pairs_ref, out_ref, lse_ref, gout_ref, gq_ref, gpairs_ref
):
    count, width, rows = pairs_ref.shape[1], q_ref.shape[2], q_ref.shape[1]
    masks = head_masks((rows, 128), 2)
    key_masks = head_masks((count, 128), 2)
    valid = (
        lax.broadcasted_iota(jnp.int32, (count, rows), 0) < lengths_ref[pl.program_id(0)]
    )
    lane = lax.broadcasted_iota(jnp.int32, (8, 128), 1)
    row = lax.broadcasted_iota(jnp.int32, (8, 128), 0)
    pick = jnp.where((lane >= row * HD) & (lane < (row + 1) * HD), 1.0, 0.0)
    for group in range(width // 128):
        cut = slice(group * 128, group * 128 + 128)
        value_cut = slice(width + group * 128, width + group * 128 + 128)
        q = q_ref[0, :, cut].astype(f32) * scale_factor
        g = gout_ref[0, :, cut].astype(f32)
        k = pairs_ref[0, :, cut].astype(f32)
        delta = lax.dot_general(
            pick,
            g * out_ref[0, :, cut].astype(f32),
            (((1,), (1,)), ((), ())),
            precision=lax.Precision.HIGHEST,
            preferred_element_type=f32,
        )
        grad_q = jnp.zeros((rows, 128), f32)
        grad_k = jnp.zeros((count, 128), f32)
        grad_v = jnp.zeros((count, 128), f32)
        for h in range(2):
            qh = keep_head(q, masks[h], 2).astype(bf16)
            gh = keep_head(g, masks[h], 2).astype(bf16)
            kh = keep_head(k, key_masks[h], 2).astype(bf16)
            s = dot_nt(pairs_ref[0, :, cut], qh) - lse_ref[0, group, h : h + 1, :]
            p = jnp.exp(jnp.where(valid, s, masked_score))
            gp = dot_nt(pairs_ref[0, :, value_cut], gh)
            gs = (p * (gp - delta[h : h + 1, :])).astype(bf16)
            grad_v += dot_nn(p.astype(bf16), gh)
            grad_k += dot_nn(gs, qh)
            grad_q += dot_tn(gs, kh)
        gq_ref[0, :, cut] = (grad_q * scale_factor).astype(bf16)
        gpairs_ref[0, :, cut] = grad_k.astype(bf16)
        gpairs_ref[0, :, value_cut] = grad_v.astype(bf16)


def cross_backward(lengths, queries, pairs, out, lse, gout):
    micro, rows, width = queries.shape
    count = pairs.shape[1]
    groups = width // 128
    row_spec = pl.BlockSpec((1, rows, width), lambda m: (m, 0, 0))
    pair_spec = pl.BlockSpec((1, count, 2 * width), lambda m: (m, 0, 0))
    return pl.pallas_call(
        cross_backward_kernel,
        grid=(micro,),
        in_specs=[
            pl.BlockSpec(memory_space=pltpu.SMEM),
            row_spec,
            pair_spec,
            row_spec,
            pl.BlockSpec((1, groups, 2, rows), lambda m: (m, 0, 0, 0)),
            row_spec,
        ],
        out_specs=[row_spec, pair_spec],
        out_shape=[
            jax.ShapeDtypeStruct((micro, rows, width), bf16),
            jax.ShapeDtypeStruct((micro, count, 2 * width), bf16),
        ],
        compiler_params=pltpu.CompilerParams(vmem_limit_bytes=32 << 20),
        name="cross_backward",
    )(lengths, queries, pairs, out, lse, gout)


def ffn_backward_kernel(
    branch_ref, hidden_ref, active_ref, slope_ref, down_ref, up_ref,
    grad_down_ref, grad_up_ref, grad_hidden_ref, hidden_t,
):
    @pl.when(pl.program_id(0) == 0)
    def _():
        hidden_t[...] = jnp.transpose(hidden_ref[...].astype(f32)).astype(bf16)
        grad_hidden_ref[...] = jnp.zeros_like(grad_hidden_ref)

    branch = branch_ref[...]
    grad_active = dot_nt(branch, down_ref[...])
    grad_inner = (slope_ref[...].astype(f32) * grad_active).astype(bf16)
    grad_down_ref[...] = dot_tn(active_ref[...], branch).astype(bf16)
    grad_up_ref[...] = dot_nn(hidden_t[...], grad_inner).astype(bf16)
    grad_hidden_ref[...] += dot_nt(grad_inner, up_ref[...])


def ffn_backward(branch, hidden, active, slope, down_weight, upward_weight):
    rows, width = branch.shape
    inner = active.shape[1]
    piece = 512
    whole = pl.BlockSpec((rows, width), lambda i: (0, 0))
    across = pl.BlockSpec((rows, piece), lambda i: (0, i))
    down = pl.BlockSpec((piece, width), lambda i: (i, 0))
    up = pl.BlockSpec((width, piece), lambda i: (0, i))
    return pl.pallas_call(
        ffn_backward_kernel,
        grid=(inner // piece,),
        in_specs=[whole, whole, across, across, down, up],
        out_specs=[down, up, whole],
        out_shape=[
            jax.ShapeDtypeStruct((inner, width), bf16),
            jax.ShapeDtypeStruct((width, inner), bf16),
            jax.ShapeDtypeStruct((rows, width), f32),
        ],
        scratch_shapes=[pltpu.VMEM((width, rows), bf16)],
        compiler_params=pltpu.CompilerParams(vmem_limit_bytes=48 << 20),
        name="ffn_backward",
    )(branch, hidden, active, slope, down_weight, upward_weight)


def gelu_parts(v):
    inner = 0.7978845608028654 * (v + 0.044715 * (v * v * v))
    t = jnp.tanh(inner)
    value = 0.5 * v * (1.0 + t)
    slope = 0.5 * (1.0 + t) + 0.5 * v * (1.0 - t * t) * (
        0.7978845608028654 * (1.0 + 3.0 * 0.044715 * (v * v))
    )
    return value, slope


def per_device(
    tokens,
    memory,
    cotangent,
    tile_segment,
    parents,
    memory_lengths,
    self_qkv,
    self_out,
    cross_q,
    cross_kv,
    cross_out,
    ffn_in,
    ffn_out,
    norm_gain,
    norm_bias,
):
    micro, _, row_count, width = tokens.shape
    seq = lax.axis_size("seq")
    total_rows = micro * row_count
    memory_rows = memory.shape[2]

    devices = seq * lax.axis_size("fsdp")
    z_size, y_size = seq // 2, lax.axis_size("fsdp") // 2

    def flat(blocks):
        return blocks.reshape(-1, blocks.shape[-1])

    joint_weight = flat(gather_first([self_qkv], ("all",), ((0,),), z_size, y_size, 4)[0])

    x = tokens.reshape(total_rows, width)
    x32 = x.astype(f32)
    bias = jax.vmap(lambda t, p: tree_bias(t, p, BLOCK))(tile_segment[:, 0], parents[:, 0])
    lengths = memory_lengths[:, 0]

    projected = dot_nn(x, joint_weight).astype(bf16)
    gathered = self_forward(
        projected.reshape(micro, row_count, 3 * width),
        bias,
        seq,
        [
            self_out,
            jnp.concatenate([norm_gain, norm_bias], 0).astype(f32),
            cross_q,
            cross_kv,
            memory.reshape(micro * memory_rows, width),
            cross_out,
            ffn_in,
            ffn_out,
        ],
        ("all", "all", "all", "all", "seq", "all", "all", "all"),
        ((0, 1), (2, 4), (3,), (5,), (6,), (7,)),
        y_size,
    )
    qkv, attended_heads, self_lse, attended = gathered[:4]
    self_output, cross_weight, pair_weight = (flat(gathered[i]) for i in (4, 6, 7))
    cross_output, upward_weight, down_weight = (flat(gathered[i]) for i in (9, 10, 11))
    norms = gathered[5].reshape(devices, 6, width // devices).transpose(1, 0, 2).reshape(6, width)
    gain_rows, bias_rows = norms[:3], norms[3:]
    memory_full = gathered[8].reshape(seq, micro, memory_rows, width).transpose(1, 0, 2, 3)
    memory_full = memory_full.reshape(micro, seq * memory_rows, width)
    attended = attended.reshape(total_rows, width)

    mixed_first = residual_weight * x32 + dot_nn(attended, self_output)
    hidden_first = layer_norm(mixed_first, gain_rows[0], bias_rows[0])
    hidden_first_low = hidden_first.astype(bf16)
    cross_query = dot_nn(hidden_first_low, cross_weight).astype(bf16)
    cross_query = cross_query.reshape(micro, row_count, width)
    count = memory_full.shape[1]
    pairs = dot_nn(memory_full.reshape(micro * count, width), pair_weight).astype(bf16)
    pairs = pairs.reshape(micro, count, 2 * width)
    cross_heads, cross_lse = cross_forward(lengths, cross_query, pairs)
    cross_attended = cross_heads.reshape(total_rows, width)
    mixed_second = residual_weight * hidden_first + dot_nn(cross_attended, cross_output)
    hidden_second = layer_norm(mixed_second, gain_rows[1], bias_rows[1])
    hidden_second_low = hidden_second.astype(bf16)
    pre_active = dot_nn(hidden_second_low, upward_weight)
    active, slope = gelu_parts(pre_active)
    active, slope = lax.optimization_barrier((active.astype(bf16), slope.astype(bf16)))
    mixed_third = residual_weight * hidden_second + dot_nn(active, down_weight)
    output = layer_norm(mixed_third, gain_rows[2], bias_rows[2]).astype(bf16)

    upstream = cotangent.reshape(total_rows, width).astype(f32)
    grad_third, gain_third, bias_third = layer_norm_back(mixed_third, gain_rows[2], upstream)
    branch_third = grad_third.astype(bf16)
    grad_down, grad_upward, grad_hidden = ffn_backward(
        branch_third, hidden_second_low, active, slope, down_weight, upward_weight
    )
    grad_hidden_second = residual_weight * grad_third + grad_hidden
    grad_second, gain_second, bias_second = layer_norm_back(
        mixed_second, gain_rows[1], grad_hidden_second
    )
    branch_second = grad_second.astype(bf16)
    grad_cross_output = dot_tn(cross_attended, branch_second).astype(bf16)
    grad_cross_attended = dot_nt(branch_second, cross_output).astype(bf16)
    grad_cross_low, memory_partial = cross_backward(
        lengths,
        cross_query,
        pairs,
        cross_heads,
        cross_lse,
        grad_cross_attended.reshape(micro, row_count, width),
    )
    memory_partial = memory_partial.reshape(micro * count, 2 * width)
    memory_share = dot_nt(memory_partial, pair_weight).astype(bf16)
    memory_share = memory_share.reshape(micro, seq, memory_rows, width).transpose(1, 0, 2, 3)
    grad_pair_weight = dot_tn(memory_full.reshape(micro * count, width), memory_partial)
    grad_cross_low = grad_cross_low.reshape(total_rows, width)
    grad_cross_weight = dot_tn(hidden_first_low, grad_cross_low).astype(bf16)
    grad_hidden_first = residual_weight * grad_second + dot_nt(grad_cross_low, cross_weight)
    grad_first, gain_first, bias_first = layer_norm_back(
        mixed_first, gain_rows[0], grad_hidden_first
    )
    branch_first = grad_first.astype(bf16)
    grad_self_output = dot_tn(attended, branch_first).astype(bf16)
    grad_attended = dot_nt(branch_first, self_output).astype(bf16)
    grad_projected, own_upward, own_down, grad_memory = self_backward(
        grad_attended.reshape(micro, row_count, width),
        qkv,
        bias,
        attended_heads,
        self_lse,
        seq,
        [grad_upward, grad_down, memory_share.reshape(seq * micro * memory_rows, width)],
        (True, False, "seq"),
        y_size,
    )
    grad_projected = grad_projected.reshape(total_rows, 3 * width)
    grad_joint = dot_tn(x, grad_projected).astype(bf16)
    grad_tokens = (residual_weight * grad_first + dot_nt(grad_projected, joint_weight)).astype(bf16)
    norm_grads = jnp.stack(
        [gain_first, gain_second, gain_third, bias_first, bias_second, bias_third]
    )
    norm_blocks = norm_grads.reshape(6, devices, width // devices).transpose(1, 0, 2)
    owned = scatter_grads(
        [
            grad_joint,
            grad_self_output,
            grad_pair_weight.astype(bf16),
            grad_cross_weight,
            grad_cross_output,
            norm_blocks.reshape(6 * devices, width // devices),
        ],
        (True, True, False, False, False, False),
        z_size,
        y_size,
        3,
    )
    return (
        output.reshape(tokens.shape),
        grad_tokens.reshape(tokens.shape),
        grad_memory.astype(bf16).reshape(memory.shape),
        owned[0],
        owned[1],
        owned[3],
        owned[2],
        owned[4],
        own_upward,
        own_down,
        owned[5][:3],
        owned[5][3:],
    )


def solution(mesh):
    rows = P(None, "fsdp", "seq", None)
    weight = P(ALL, None)
    in_specs = (
        rows,
        rows,
        rows,
        P(None, "fsdp", None),
        P(None, "fsdp", None),
        P(None, "fsdp"),
    ) + (weight,) * 7 + (P(None, ALL),) * 2
    out_specs = (rows, rows, rows) + (weight,) * 7 + (P(None, ALL),) * 2
    return jax.shard_map(
        per_device, mesh=mesh, in_specs=in_specs, out_specs=out_specs, check_vma=False
    )
```

```python
import functools

import jax
import jax.numpy as jnp
from jax import lax
from jax.experimental import pallas as pl
from jax.experimental.pallas import tpu as pltpu
from jax.sharding import PartitionSpec as P

H = 16
HD = 64
TILE = 128
BLOCK = 256
FIRST_SPLIT = 3
WINDOW = 4
GATHER_END = 85
SPLIT_ELEMENTS = 96 << 10
SCATTER_END = 95

scale_factor = 0.125
residual_weight = 36.0**0.25
norm_epsilon = 1e-05
masked_score = -1e30
ALL = ("seq", "fsdp")
f32 = jnp.float32
bf16 = jnp.bfloat16
MESH = pl.DeviceIdType.MESH


def dot_nn(a, b):
    return lax.dot_general(a, b, (((1,), (0,)), ((), ())), preferred_element_type=f32)


def dot_nt(a, b):
    return lax.dot_general(a, b, (((1,), (1,)), ((), ())), preferred_element_type=f32)


def dot_tn(a, b):
    return lax.dot_general(a, b, (((0,), (0,)), ((), ())), preferred_element_type=f32)


def norm_stats(incoming):
    row_mean = jnp.mean(incoming, -1, keepdims=True)
    centred = incoming - row_mean
    variance = jnp.mean(centred * centred, -1, keepdims=True)
    return centred, lax.rsqrt(variance + norm_epsilon)


def layer_norm(incoming, gain_row, bias_row):
    centred, inverse = norm_stats(incoming)
    return centred * inverse * gain_row + bias_row


def layer_norm_back(incoming, gain_row, upstream):
    centred, inverse = norm_stats(incoming)
    normal = centred * inverse
    grad_bias = jnp.sum(upstream, 0)
    grad_gain = jnp.sum(upstream * normal, 0)
    scaled = upstream * gain_row
    grad = inverse * (
        scaled
        - jnp.mean(scaled, -1, keepdims=True)
        - normal * jnp.mean(scaled * normal, -1, keepdims=True)
    )
    return grad, grad_gain, grad_bias


def ancestors(parent_ids):
    segment_ids = jnp.arange(parent_ids.shape[0], dtype=jnp.int32)
    hop = (parent_ids[:, None] == segment_ids[None, :]).astype(f32)
    reach = jnp.maximum(hop, (segment_ids[:, None] == segment_ids[None, :]).astype(f32))
    steps = 1
    while steps < parent_ids.shape[0]:
        reach = jnp.minimum(jnp.dot(reach, reach, precision=lax.Precision.HIGHEST), 1.0)
        steps *= 2
    return reach


def tree_bias(tile_segments, parent_ids, block):
    tiles = tile_segments.shape[0]
    onehot = (
        tile_segments[:, None] == jnp.arange(parent_ids.shape[0], dtype=jnp.int32)[None, :]
    ).astype(f32)
    high = lax.Precision.HIGHEST
    related = jnp.dot(
        jnp.dot(onehot, ancestors(parent_ids), precision=high), onehot.T, precision=high
    )
    bias = jnp.where(related > 0.5, 0.0, masked_score)
    per = block // TILE
    blocks = tiles // per
    bias = bias.reshape(blocks, per, blocks, per).transpose(2, 0, 3, 1)
    return jnp.repeat(bias, TILE, axis=3)


def head_masks(shape, heads):
    lane = lax.broadcasted_iota(jnp.int32, shape, 1)
    return [(lane >= h * HD) & (lane < (h + 1) * HD) for h in range(heads)]


def keep_head(value, mask, heads):
    return value if heads == 1 else jnp.where(mask, value, jnp.zeros_like(value))


def greet(peers):
    barrier = pltpu.get_barrier_semaphore()
    for peer in peers:
        pl.semaphore_signal(barrier, inc=1, device_id=peer, device_id_type=MESH)
    pl.semaphore_wait(barrier, len(peers))


def peer_at(step):
    count = lax.axis_size("seq")
    return lax.rem(lax.axis_index("seq") + step, count)


def rows_at(i, count):
    return pl.ds(pl.multiple_of(i * count, count), count)


def cut_heads(rows_ref, m, parts, blocks_ref):
    seq, part = blocks_ref.shape[2], blocks_ref.shape[4]
    for p in range(parts):
        for s in range(seq):
            first = (p * seq + s) * part
            blocks_ref[m, p, s] = rows_ref[m, :, first : first + part]


def join_heads(blocks_ref, m, parts, rows_ref):
    seq, part = blocks_ref.shape[2], blocks_ref.shape[4]
    for p in range(parts):
        for s in range(seq):
            first = (p * seq + s) * part
            rows_ref[m, :, first : first + part] = blocks_ref[m, p, s]


def to_peer(source_ref, target_ref, send, receive, m, step):
    rows = source_ref.shape[3]
    return pltpu.make_async_remote_copy(
        src_ref=source_ref.at[m, :, peer_at(step)],
        dst_ref=target_ref.at[m, :, rows_at(lax.axis_index("seq"), rows)],
        send_sem=send.at[m, step],
        recv_sem=receive.at[m, step],
        device_id={"seq": peer_at(step)},
        device_id_type=MESH,
    )


def to_self(source_ref, target_ref, sem, m):
    rows = source_ref.shape[3]
    me = lax.axis_index("seq")
    return pltpu.make_async_copy(
        source_ref.at[m, :, me], target_ref.at[m, :, rows_at(me, rows)], sem.at[m, 0]
    )


def send_blocks(source_ref, target_ref, send, receive, m):
    for step in range(1, lax.axis_size("seq")):
        to_peer(source_ref, target_ref, send, receive, m, step).start()
    to_self(source_ref, target_ref, send, m).start()


def take_blocks(source_ref, target_ref, send, receive, m, between=None):
    for step in range(1, lax.axis_size("seq")):
        to_peer(source_ref, target_ref, send, receive, m, step).wait_recv()
        if between is not None:
            between(step)
    to_self(source_ref, target_ref, send, m).wait()


def home_copy(source_ref, target_ref, send, receive, m, place):
    rows = target_ref.shape[3]
    me = lax.axis_index("seq")
    count = lax.axis_size("seq")
    step = lax.rem(place - me + count, count)
    return pltpu.make_async_remote_copy(
        src_ref=source_ref.at[m, :, rows_at(place, rows)],
        dst_ref=target_ref.at[m, :, me],
        send_sem=send.at[m, step],
        recv_sem=receive.at[m, step],
        device_id={"seq": place},
        device_id_type=MESH,
    )


def home_self(source_ref, target_ref, sem, m):
    rows = target_ref.shape[3]
    me = lax.axis_index("seq")
    return pltpu.make_async_copy(
        source_ref.at[m, :, rows_at(me, rows)], target_ref.at[m, :, me], sem.at[m, 0]
    )


def send_home(source_ref, target_ref, send, receive, m, place):
    me = lax.axis_index("seq")

    @pl.when(place != me)
    def _():
        home_copy(source_ref, target_ref, send, receive, m, place).start()

    @pl.when(place == me)
    def _():
        home_self(source_ref, target_ref, send, m).start()


def take_home(source_ref, target_ref, send, receive, m):
    for step in range(1, lax.axis_size("seq")):
        home_copy(source_ref, target_ref, send, receive, m, peer_at(step)).wait()
    home_self(source_ref, target_ref, send, m).wait()


def scatter_places():
    s, f = lax.axis_index("seq"), lax.axis_index("fsdp")
    z, y = s // 2, f // 2
    return z, s - 2 * z, y, f - 2 * y, lax.axis_size("seq") // 2, lax.axis_size("fsdp") // 2


def scatter_peers():
    z, x, y, c, z_size, y_size = scatter_places()
    peers = [{"fsdp": 2 * y + 1 - c}, {"seq": 2 * z + 1 - x}]
    peers += [{"fsdp": 2 * lax.rem(y + k, y_size) + c} for k in range(1, y_size)]
    peers += [{"seq": 2 * lax.rem(z + k, z_size) + x} for k in range(1, z_size)]
    return peers


def scatter_shapes(blocks, x_first):
    if x_first == "seq":
        z_size, _, rows, columns = blocks.shape
        shape = (z_size, rows, columns)
        return [pltpu.VMEM(shape, blocks.dtype)] * 2 + [
            pltpu.VMEM((z_size - 1, rows, columns), blocks.dtype)
        ]
    z_size, _, y_size, _, rows, columns = blocks.shape
    if x_first:
        first, second = (1, y_size), (y_size - 1,)
    else:
        first, second = (y_size - 1, 2), (1,)
    kind = blocks.dtype
    return [
        pltpu.VMEM((z_size, 2, y_size, rows, columns), kind),
        pltpu.VMEM((z_size, 2, y_size, rows, columns), kind),
        pltpu.VMEM((z_size,) + first + (rows, columns), kind),
        pltpu.VMEM((z_size,) + second + (rows, columns), kind),
        pltpu.VMEM((z_size - 1, rows, columns), kind),
    ]


def scatter_sems(count, z_size, y_size):
    pair = pltpu.SemaphoreType.DMA((count, z_size))
    triple = pltpu.SemaphoreType.DMA((count, z_size, max(1, y_size - 1)))
    return [pair, pair, pair, triple, triple, triple, triple, pair, pair]


def add_into(target, source):
    target[...] = target[...] + source[...]


def scatter_steps(kinds, sources, outs, buffers, sems):
    z, x, y, c, z_size, y_size = scatter_places()
    local, core_s, core_r, first_s, first_r, second_s, second_r, last_s, last_r = sems
    count = len(sources)

    def to_z(t):
        return lax.rem(z + 1 + t, z_size)

    def remote(source, target, send, receive, peer):
        return pltpu.make_async_remote_copy(
            src_ref=source,
            dst_ref=target,
            send_sem=send,
            recv_sem=receive,
            device_id=peer,
            device_id_type=MESH,
        )

    across = [a for a in range(count) if kinds[a] != "seq"]
    along = [a for a in range(count) if kinds[a] == "seq"]

    def own_copy(a, t):
        if kinds[a] == "seq":
            source = sources[a].at[to_z(t), x]
        else:
            source = sources[a].at[to_z(t), :, :, c]
        return pltpu.make_async_copy(source, buffers[a][0].at[t], local.at[a, t])

    def seq_first(a, t):
        return remote(
            sources[a].at[to_z(t), 1 - x],
            buffers[a][1].at[t],
            core_s.at[a, t],
            core_r.at[a, t],
            x_peer(),
        )

    def seq_last(a, t):
        return remote(
            buffers[a][0].at[t],
            buffers[a][2].at[t],
            last_s.at[a, t],
            last_r.at[a, t],
            {"seq": 2 * to_z(t) + x},
        )

    def core_copy(a, t):
        return remote(
            sources[a].at[to_z(t), :, :, 1 - c],
            buffers[a][1].at[t],
            core_s.at[a, t],
            core_r.at[a, t],
            {"fsdp": 2 * y + 1 - c},
        )

    def x_peer():
        return {"seq": 2 * z + 1 - x}

    def y_place(k):
        return lax.rem(y + k, y_size)

    def y_peer(k):
        return {"fsdp": 2 * y_place(k) + c}

    def first_copies(a, t):
        own, _, first, _, _ = buffers[a]
        if kinds[a]:
            sends = [(own.at[t, 1 - x], x_peer())]
        else:
            sends = [(own.at[t, :, y_place(k)], y_peer(k)) for k in range(1, y_size)]
        return [
            remote(source, first.at[t, k], first_s.at[a, t, k], first_r.at[a, t, k], peer)
            for k, (source, peer) in enumerate(sends)
        ]

    def second_copies(a, t):
        own, _, _, second, _ = buffers[a]
        if kinds[a]:
            sends = [(own.at[t, x, y_place(k)], y_peer(k)) for k in range(1, y_size)]
        else:
            sends = [(own.at[t, 1 - x, y], x_peer())]
        return [
            remote(source, second.at[t, k], second_s.at[a, t, k], second_r.at[a, t, k], peer)
            for k, (source, peer) in enumerate(sends)
        ]

    def last_copy(a, t):
        own, _, _, _, last = buffers[a]
        return remote(
            own.at[t, x, y],
            last.at[t],
            last_s.at[a, t],
            last_r.at[a, t],
            {"seq": 2 * to_z(t) + x},
        )

    def start_core(t):
        for a in range(count):
            (core_copy if a in across else seq_first)(a, t).start()
            own_copy(a, t).start()

    def core_step(t):
        for a in across:
            core_copy(a, t).wait_recv()
            own_copy(a, t).wait()
            own, core = buffers[a][:2]

            def add(i, carry, own=own, core=core):
                add_into(own.at[t, i // y_size, i % y_size], core.at[t, i // y_size, i % y_size])
                return carry

            lax.fori_loop(0, 2 * y_size, add, 0)
            for copy in first_copies(a, t):
                copy.start()
        if t + 2 < z_size:
            start_core(t + 2)

    def first_step(t):
        for a in across:
            own, _, first, _, _ = buffers[a]
            for k, copy in enumerate(first_copies(a, t)):
                copy.wait_recv()
                for i in range(y_size if kinds[a] else 2):
                    target = own.at[t, x, i] if kinds[a] else own.at[t, i, y]
                    add_into(target, first.at[t, k, i])
            for copy in second_copies(a, t):
                copy.start()

    def second_step(t):
        for a in along:
            seq_first(a, t).wait_recv()
            own_copy(a, t).wait()
            add_into(buffers[a][0].at[t], buffers[a][1].at[t])
            if t < z_size - 1:
                seq_last(a, t).start()
        for a in across:
            own, _, _, second, _ = buffers[a]
            for k, copy in enumerate(second_copies(a, t)):
                copy.wait_recv()
                add_into(own.at[t, x, y], second.at[t, k])
            if t < z_size - 1:
                last_copy(a, t).start()

    def final_step():
        for a in along:
            own, _, last = buffers[a]
            total = own[z_size - 1].astype(f32)
            for t in range(z_size - 1):
                seq_last(a, t).wait()
                total = total + last[t].astype(f32)
            outs[a][...] = total
            for t in range(z_size):
                seq_first(a, t).wait_send()
        for a in across:
            own, _, _, _, last = buffers[a]
            total = own[z_size - 1, x, y].astype(f32)
            for t in range(z_size - 1):
                last_copy(a, t).wait()
                total = total + last[t].astype(f32)
            outs[a][...] = total
            for t in range(z_size):
                core_copy(a, t).wait_send()
                for copy in first_copies(a, t) + second_copies(a, t):
                    copy.wait_send()

    def opening():
        start_core(0)
        if z_size > 1:
            start_core(1)

    steps = [opening]
    for t in range(z_size + 2):
        if t < z_size:
            steps.append(functools.partial(core_step, t))
        if 0 <= t - 1 < z_size:
            steps.append(functools.partial(first_step, t - 1))
        if 0 <= t - 2 < z_size:
            steps.append(functools.partial(second_step, t - 2))
    steps.append(final_step)
    return steps


def scatter_buffers(kinds, refs):
    buffers = []
    for kind in kinds:
        size = 3 if kind == "seq" else 5
        buffers.append(refs[:size])
        refs = refs[size:]
    return buffers, refs


def scatter_kernel(kinds, *refs):
    count = len(kinds)
    sources, outs, rest = refs[:count], refs[count : 2 * count], refs[2 * count :]
    buffers, rest = scatter_buffers(kinds, rest)
    greet(scatter_peers())
    for step in scatter_steps(kinds, sources, outs, buffers, rest):
        step()


def scatter_blocks(arrays, kinds, z_size, y_size):
    blocks = []
    for a, kind in zip(arrays, kinds):
        lead = (z_size, 2) if kind == "seq" else (z_size, 2, y_size, 2)
        blocks.append(a.reshape(lead + (-1, a.shape[1])))
    return blocks


def scatter_grads(arrays, kinds, z_size, y_size, collective_id):
    blocks = scatter_blocks(arrays, kinds, z_size, y_size)
    scratch = []
    for block, kind in zip(blocks, kinds):
        scratch += scatter_shapes(block, kind)
    return pl.pallas_call(
        functools.partial(scatter_kernel, kinds),
        in_specs=[pl.BlockSpec(memory_space=pl.ANY)] * len(arrays),
        out_specs=[pl.BlockSpec(memory_space=pltpu.VMEM)] * len(arrays),
        out_shape=[jax.ShapeDtypeStruct(b.shape[-2:], f32) for b in blocks],
        scratch_shapes=scratch + scatter_sems(len(arrays), z_size, y_size),
        compiler_params=pltpu.CompilerParams(
            vmem_limit_bytes=60 << 20, collective_id=collective_id, has_side_effects=True
        ),
        name="scatter_grads",
    )(*blocks)


def spread(steps, first, last):
    return [(first + k * (last - first) // max(1, len(steps) - 1), s) for k, s in enumerate(steps)]


def run_slot(placed, slot):
    for at, step in placed:
        pl.when(slot == at)(step)


def both_peers():
    _, _, y, c, _, y_size = scatter_places()
    peers = [{"seq": peer_at(step)} for step in range(1, lax.axis_size("seq"))]
    peers += [{"fsdp": 2 * y + 1 - c}]
    return peers + [{"fsdp": 2 * lax.rem(y + k, y_size) + c} for k in range(1, y_size)]


def gather_parts(shards, kinds, groups, most=2):
    parts, units = [], []
    for group in groups:
        pieces = []
        for a in group:
            rows, columns = shards[a].shape
            kind = kinds[a]
            split = most if rows % 32 == 0 and rows * columns >= SPLIT_ELEMENTS else 1
            for n in range(split):
                cut = (n * columns // split, columns // split)
                if kind == "seq" or rows % 32:
                    piece = [(a, 0, rows) + cut + ("x" if kind == "all" else kind,)]
                else:
                    half = rows // 2
                    piece = [(a, 0, half) + cut + ("x",), (a, half, half) + cut + ("y",)]
                if n == len(pieces):
                    pieces.append([])
                pieces[n] += piece
        for piece in pieces:
            units.append(range(len(parts), len(parts) + len(piece)))
            parts += piece
    return parts, units


def gather_sems(plan, z_size, y_size):
    count = len(plan[0])
    z_sem = pltpu.SemaphoreType.DMA((count, z_size))
    y_sem = pltpu.SemaphoreType.DMA((count, max(1, y_size - 1)))
    one = pltpu.SemaphoreType.DMA((count, 1))
    return [z_sem, z_sem, y_sem, y_sem, y_sem, y_sem, one, one]


def gather_steps(plan, shards, outs, sems):
    z, x, y, c, z_size, y_size = scatter_places()
    z_s, z_r, first_s, first_r, second_s, second_r, core_s, core_r = sems
    parts, units = plan

    def remote(view, peer, send, receive):
        return pltpu.make_async_remote_copy(
            src_ref=view,
            dst_ref=view,
            send_sem=send,
            recv_sem=receive,
            device_id=peer,
            device_id_type=MESH,
        )

    def shard_of(p):
        a, start, rows, left, columns, _ = parts[p]
        return shards[a].at[pl.ds(start, rows), pl.ds(left, columns)]

    def place(p, *lead):
        a, start, rows, left, columns, _ = parts[p]
        return outs[a].at[lead + (pl.ds(start, rows), pl.ds(left, columns))]

    def own(p):
        return place(p, z, x) if parts[p][-1] == "seq" else place(p, z, x, y, c)

    def own_copy(p):
        return pltpu.make_async_copy(shard_of(p), own(p), z_s.at[p, 0])

    def z_copies(p):
        return [
            pltpu.make_async_remote_copy(
                src_ref=shard_of(p),
                dst_ref=own(p),
                send_sem=z_s.at[p, k],
                recv_sem=z_r.at[p, k],
                device_id={"seq": 2 * lax.rem(z + k, z_size) + x},
                device_id_type=MESH,
            )
            for k in range(1, z_size)
        ]

    def x_peer():
        return {"seq": 2 * z + 1 - x}

    def y_peers():
        return [{"fsdp": 2 * lax.rem(y + k, y_size) + c} for k in range(1, y_size)]

    whole = slice(None)

    def first_copies(p):
        kind = parts[p][-1]
        view = place(p, whole, x) if kind == "seq" else place(p, whole, x, y, c)
        peers = y_peers() if kind == "y" else [x_peer()]
        return [
            remote(view, peer, first_s.at[p, k], first_r.at[p, k]) for k, peer in enumerate(peers)
        ]

    def second_copies(p):
        kind = parts[p][-1]
        if kind == "seq":
            return []
        view = place(p, whole, whole, y, c) if kind == "x" else place(p, whole, x, whole, c)
        peers = y_peers() if kind == "x" else [x_peer()]
        return [
            remote(view, peer, second_s.at[p, k], second_r.at[p, k]) for k, peer in enumerate(peers)
        ]

    def core_copies(p):
        if parts[p][-1] == "seq":
            return []
        view = place(p, whole, whole, whole, c)
        return [remote(view, {"fsdp": 2 * y + 1 - c}, core_s.at[p, 0], core_r.at[p, 0])]

    def step(t):
        def unit(at):
            return units[at] if 0 <= at < len(units) else ()

        for p in unit(t - 3):
            for copy in second_copies(p):
                copy.wait_recv()
            for copy in core_copies(p):
                copy.start()
        for p in unit(t - 2):
            for copy in first_copies(p):
                copy.wait_recv()
            for copy in second_copies(p):
                copy.start()
        for p in unit(t - 1):
            for copy in z_copies(p):
                copy.wait_recv()
            own_copy(p).wait()
            for copy in first_copies(p):
                copy.start()
        for p in unit(t):
            for copy in z_copies(p):
                copy.start()
            own_copy(p).start()

    def final_step():
        for p in range(len(parts)):
            for copy in core_copies(p):
                copy.wait()
            for copy in z_copies(p) + first_copies(p) + second_copies(p):
                copy.wait_send()

    return [functools.partial(step, t) for t in range(len(units) + 3)] + [final_step]


def gather_out(shard, kind, z_size, y_size):
    lead = (z_size, 2) if kind == "seq" else (z_size, 2, y_size, 2)
    return jax.ShapeDtypeStruct(lead + shard.shape, shard.dtype)


def gather_kernel(plan, count, *refs):
    shards, outs, sems = refs[:count], refs[count : 2 * count], refs[2 * count :]
    greet(scatter_peers())
    for step in gather_steps(plan, shards, outs, sems):
        step()


def gather_first(shards, kinds, groups, z_size, y_size, collective_id):
    plan = gather_parts(shards, kinds, groups, FIRST_SPLIT)
    return pl.pallas_call(
        functools.partial(gather_kernel, plan, len(shards)),
        in_specs=[pl.BlockSpec(memory_space=pl.ANY)] * len(shards),
        out_specs=[pl.BlockSpec(memory_space=pl.ANY)] * len(shards),
        out_shape=[gather_out(s, k, z_size, y_size) for s, k in zip(shards, kinds)],
        scratch_shapes=gather_sems(plan, z_size, y_size),
        compiler_params=pltpu.CompilerParams(collective_id=collective_id, has_side_effects=True),
        name="gather_first",
    )(*shards)


def self_forward_kernel(heads, block, plan, count, *refs):
    rows_ref, bias_ref = refs[:2]
    shards, refs = refs[2 : 2 + count], refs[2 + count :]
    qkv_ref, out_ref, lse_ref, attended_ref = refs[:4]
    whole, refs = refs[4 : 4 + count], refs[4 + count :]
    cut, back, queries, values_t, send_in, take_in, send_out, take_out = refs[:8]
    gather = gather_steps(plan, shards, whole, refs[8:])
    micro, _, length, width = qkv_ref.shape
    seq = lax.axis_size("seq")
    blocks = length // block
    per = block // TILE
    place_rows = length // seq
    masks = head_masks((block, width), heads)
    per_micro = blocks + seq - 1
    window = min(WINDOW, seq - 1)
    placed = spread(gather[1:-1], 0, GATHER_END * micro * per_micro // 100)
    greet(both_peers())

    def launch(m, carry):
        cut_heads(rows_ref, m, 3, cut)

        @pl.when(m < 1)
        def _():
            for step in range(1, window + 1):
                to_peer(cut, qkv_ref, send_in, take_in, m, step).start()

        to_self(cut, qkv_ref, send_in, m).start()
        return carry

    lax.fori_loop(0, micro, launch, 0)
    gather[0]()
    key_place = lax.broadcasted_iota(jnp.int32, (block, block), 0)
    query_place = lax.broadcasted_iota(jnp.int32, (block, block), 1)
    causal = key_place <= query_place

    def one_micro(m, carry):
        def between(step):
            run_slot(placed, m * per_micro + step - 1)
            if step + window < seq:
                to_peer(cut, qkv_ref, send_in, take_in, m, step + window).start()
            else:

                @pl.when(m + 1 < micro)
                def _():
                    following = step + window + 1 - seq
                    to_peer(cut, qkv_ref, send_in, take_in, m + 1, following).start()

        take_blocks(cut, qkv_ref, send_in, take_in, m, between)

        def prepare(i, carry):
            rows = rows_at(i, block)
            q = qkv_ref[m, 0, rows, :].astype(f32) * scale_factor
            for h in range(heads):
                queries[h, rows, :] = keep_head(q, masks[h], heads).astype(bf16)
            values_t[i] = jnp.transpose(qkv_ref[m, 2, rows, :].astype(f32)).astype(bf16)
            return carry

        lax.fori_loop(0, blocks, prepare, 0)

        def scores_of(i, j, count, h):
            keys = pl.ds(pl.multiple_of(j * block, block), count * block)
            raw = dot_nt(qkv_ref[m, 1, keys, :], queries[h, rows_at(i, block), :])
            bias = jnp.concatenate([bias_ref[m, j + k, i] for k in range(count)], 0)
            raw = raw.reshape(count * per, TILE, block) + bias[:, None, :]
            return raw.reshape(count * block, block)

        def values_by(j, count, h, p):
            p = p.astype(bf16)
            return sum(
                dot_nn(values_t[j + k][h * HD : (h + 1) * HD], p[k * block : (k + 1) * block])
                for k in range(count)
            )

        def query_block(i, carry):
            run_slot(placed, m * per_micro + seq - 1 + i)
            state = []
            for h in range(heads):
                s = jnp.where(causal, scores_of(i, i, 1, h), masked_score)
                top = jnp.max(s, 0, keepdims=True)
                p = jnp.exp(s - top)
                state += [top, jnp.sum(p, 0, keepdims=True), values_by(i, 1, h, p)]

            def key_blocks(j, count, state):
                fresh = []
                for h in range(heads):
                    top, total, acc = state[3 * h : 3 * h + 3]
                    s = scores_of(i, j, count, h)
                    higher = jnp.maximum(top, jnp.max(s, 0, keepdims=True))
                    shrink = jnp.exp(top - higher)
                    p = jnp.exp(s - higher)
                    total = total * shrink + jnp.sum(p, 0, keepdims=True)
                    fresh += [higher, total, acc * shrink + values_by(j, count, h, p)]
                return tuple(fresh)

            pairs = i // 2
            state = lax.fori_loop(0, pairs, lambda j, s: key_blocks(2 * j, 2, s), tuple(state))
            state = lax.fori_loop(2 * pairs, i, lambda j, s: key_blocks(j, 1, s), state)
            out = jnp.concatenate(
                [state[3 * h + 2] * (1.0 / state[3 * h + 1]) for h in range(heads)], 0
            )
            out_ref[m, 0, rows_at(i, block), :] = jnp.transpose(out).astype(bf16)
            lse_ref[m, i] = jnp.concatenate(
                [state[3 * h] + jnp.log(state[3 * h + 1]) for h in range(heads)], 0
            )
            for sub in range(block // place_rows):
                place = i * (block // place_rows) + sub
                send_home(out_ref, back, send_out, take_out, m, place)
            return carry

        lax.fori_loop(0, blocks, query_block, 0)
        return carry

    lax.fori_loop(0, micro, one_micro, 0)

    def finish(m, carry):
        for step in range(1, seq):
            to_peer(cut, qkv_ref, send_in, take_in, m, step).wait_send()
        take_home(out_ref, back, send_out, take_out, m)
        join_heads(back, m, 1, attended_ref)
        return carry

    lax.fori_loop(0, micro, finish, 0)
    gather[-1]()


def self_forward(projected, bias, seq, shards, kinds, groups, y_size):
    micro, rows, width = projected.shape
    part = width // 3 // seq
    heads = part // HD
    length = rows * seq
    blocks = length // BLOCK
    whole = pl.BlockSpec(memory_space=pltpu.VMEM)
    sems = pltpu.SemaphoreType.DMA((micro, seq))
    count = len(shards)
    any_place = [pl.BlockSpec(memory_space=pl.ANY)] * count
    plan = gather_parts(shards, kinds, groups)
    return pl.pallas_call(
        functools.partial(self_forward_kernel, heads, BLOCK, plan, count),
        in_specs=[whole, whole] + any_place,
        out_specs=[whole] * 4 + any_place,
        out_shape=[
            jax.ShapeDtypeStruct((micro, 3, length, part), bf16),
            jax.ShapeDtypeStruct((micro, 1, length, part), bf16),
            jax.ShapeDtypeStruct((micro, blocks, heads, BLOCK), f32),
            jax.ShapeDtypeStruct((micro, rows, width // 3), bf16),
        ]
        + [gather_out(s, k, seq // 2, y_size) for s, k in zip(shards, kinds)],
        scratch_shapes=[
            pltpu.VMEM((micro, 3, seq, rows, part), bf16),
            pltpu.VMEM((micro, 1, seq, rows, part), bf16),
            pltpu.VMEM((heads, length, part), bf16),
            pltpu.VMEM((blocks, part, BLOCK), bf16),
            sems,
            sems,
            sems,
            sems,
        ]
        + gather_sems(plan, seq // 2, y_size),
        compiler_params=pltpu.CompilerParams(
            vmem_limit_bytes=50 << 20, collective_id=1, has_side_effects=True
        ),
        name="self_forward",
    )(projected, bias, *shards)


def self_backward_kernel(heads, block, kinds, *refs):
    count = len(kinds)
    rows_ref, qkv_ref, bias_ref, out_ref, lse_ref = refs[:5]
    sources, refs = refs[5 : 5 + count], refs[5 + count :]
    grad_ref, owned, refs = refs[0], refs[1 : 1 + count], refs[1 + count :]
    cut, gout, grads, back, queries, keys_h, gouts, delta, grad_q = refs[:9]
    send_in, take_in, send_out, take_out = refs[9:13]
    buffers, refs = scatter_buffers(kinds, refs[13:])
    scatter = scatter_steps(kinds, sources, owned, buffers, refs)
    micro, _, length, width = qkv_ref.shape
    seq = lax.axis_size("seq")
    blocks = length // block
    per = block // TILE
    place_rows = length // seq
    masks = head_masks((block, width), heads)
    lane = lax.broadcasted_iota(jnp.int32, (8, width), 1)
    first_lane = lax.broadcasted_iota(jnp.int32, (8, width), 0) * HD
    pick = jnp.where((lane >= first_lane) & (lane < first_lane + HD), 1.0, 0.0)
    placed = spread(scatter[1:-1], 1, SCATTER_END * micro * blocks // 100)
    greet(both_peers())

    def launch(m, carry):
        cut_heads(rows_ref, m, 1, cut)
        send_blocks(cut, gout, send_in, take_in, m)
        return carry

    lax.fori_loop(0, micro, launch, 0)
    scatter[0]()
    key_place = lax.broadcasted_iota(jnp.int32, (block, block), 0)
    query_place = lax.broadcasted_iota(jnp.int32, (block, block), 1)
    causal = key_place <= query_place

    def one_micro(m, carry):
        take_blocks(cut, gout, send_in, take_in, m)

        def prepare(i, carry):
            rows = rows_at(i, block)
            q = qkv_ref[m, 0, rows, :].astype(f32) * scale_factor
            k = qkv_ref[m, 1, rows, :].astype(f32)
            g = gout[m, 0, rows, :].astype(f32)
            for h in range(heads):
                queries[h, rows, :] = keep_head(q, masks[h], heads).astype(bf16)
                keys_h[h, rows, :] = keep_head(k, masks[h], heads).astype(bf16)
                gouts[h, rows, :] = keep_head(g, masks[h], heads).astype(bf16)
            delta[i] = lax.dot_general(
                pick,
                g * out_ref[m, 0, rows, :].astype(f32),
                (((1,), (1,)), ((), ())),
                precision=lax.Precision.HIGHEST,
                preferred_element_type=f32,
            )
            grad_q[rows, :] = jnp.zeros((block, width), f32)
            return carry

        lax.fori_loop(0, blocks, prepare, 0)

        def key_block(j, carry):
            run_slot(placed, m * blocks + j)
            krows = rows_at(j, block)

            def pair(i, grad_k, grad_v, diagonal):
                rows = rows_at(i, block)
                bias = bias_ref[m, j, i]
                gq = grad_q[rows, :]
                for h in range(heads):
                    raw = dot_nt(qkv_ref[m, 1, krows, :], queries[h, rows, :])
                    shift = bias - lse_ref[m, i, h : h + 1, :]
                    s = (raw.reshape(per, TILE, block) + shift[:, None, :]).reshape(block, block)
                    if diagonal:
                        s = jnp.where(causal, s, masked_score)
                    p = jnp.exp(s)
                    gp = dot_nt(qkv_ref[m, 2, krows, :], gouts[h, rows, :])
                    gs = (p * (gp - delta[i, h : h + 1, :])).astype(bf16)
                    grad_v = grad_v + dot_nn(p.astype(bf16), gouts[h, rows, :])
                    grad_k = grad_k + dot_nn(gs, queries[h, rows, :])
                    gq = gq + dot_tn(gs, keys_h[h, krows, :])
                grad_q[rows, :] = gq
                return grad_k, grad_v

            zero = jnp.zeros((block, width), f32)
            state = pair(j, zero, zero, True)
            state = lax.fori_loop(
                j + 1, blocks, lambda i, s: pair(i, s[0], s[1], False), state
            )
            grads[m, 0, krows, :] = (grad_q[krows, :] * scale_factor).astype(bf16)
            grads[m, 1, krows, :] = state[0].astype(bf16)
            grads[m, 2, krows, :] = state[1].astype(bf16)
            for sub in range(block // place_rows):
                place = j * (block // place_rows) + sub
                send_home(grads, back, send_out, take_out, m, place)
            return carry

        lax.fori_loop(0, blocks, key_block, 0)
        return carry

    lax.fori_loop(0, micro, one_micro, 0)

    def finish(m, carry):
        for step in range(1, seq):
            to_peer(cut, gout, send_in, take_in, m, step).wait_send()
        take_home(grads, back, send_out, take_out, m)
        join_heads(back, m, 3, grad_ref)
        return carry

    scatter[-1]()
    lax.fori_loop(0, micro, finish, 0)


def self_backward(grad_attended, qkv, bias, out, lse, seq, arrays, kinds, y_size):
    micro, rows, width = grad_attended.shape
    length, part = qkv.shape[2:]
    heads = part // HD
    blocks = length // BLOCK
    whole = pl.BlockSpec(memory_space=pltpu.VMEM)
    sems = pltpu.SemaphoreType.DMA((micro, seq))
    sources = scatter_blocks(arrays, kinds, seq // 2, y_size)
    count = len(arrays)
    scratch = []
    for source, kind in zip(sources, kinds):
        scratch += scatter_shapes(source, kind)
    return pl.pallas_call(
        functools.partial(self_backward_kernel, heads, BLOCK, kinds),
        in_specs=[whole] * 5 + [pl.BlockSpec(memory_space=pl.ANY)] * count,
        out_specs=[whole] * (1 + count),
        out_shape=[jax.ShapeDtypeStruct((micro, rows, 3 * width), bf16)]
        + [jax.ShapeDtypeStruct(b.shape[-2:], f32) for b in sources],
        scratch_shapes=[
            pltpu.VMEM((micro, 1, seq, rows, part), bf16),
            pltpu.VMEM((micro, 1, length, part), bf16),
            pltpu.VMEM((micro, 3, length, part), bf16),
            pltpu.VMEM((micro, 3, seq, rows, part), bf16),
            pltpu.VMEM((heads, length, part), bf16),
            pltpu.VMEM((heads, length, part), bf16),
            pltpu.VMEM((heads, length, part), bf16),
            pltpu.VMEM((blocks, 8, BLOCK), f32),
            pltpu.VMEM((length, part), f32),
            sems,
            sems,
            sems,
            sems,
        ]
        + scratch
        + scatter_sems(count, seq // 2, y_size),
        compiler_params=pltpu.CompilerParams(
            vmem_limit_bytes=60 << 20, collective_id=2, has_side_effects=True
        ),
        name="self_backward",
    )(grad_attended, qkv, bias, out, lse, *sources)


def cross_forward_kernel(lengths_ref, q_ref, pairs_ref, out_ref, lse_ref):
    count, width, rows = pairs_ref.shape[1], q_ref.shape[2], q_ref.shape[1]
    masks = head_masks((rows, 128), 2)
    valid = (
        lax.broadcasted_iota(jnp.int32, (count, rows), 0) < lengths_ref[pl.program_id(0)]
    )
    for g in range(width // 128):
        cut = slice(g * 128, g * 128 + 128)
        q = q_ref[0, :, cut].astype(f32) * scale_factor
        values = pairs_ref[0, :, width + g * 128 : width + g * 128 + 128]
        values_t = jnp.transpose(values.astype(f32)).astype(bf16)
        outs, lses = [], []
        for h in range(2):
            s = dot_nt(pairs_ref[0, :, cut], keep_head(q, masks[h], 2).astype(bf16))
            s = jnp.where(valid, s, masked_score)
            m = jnp.max(s, 0, keepdims=True)
            p = jnp.exp(s - m)
            total = jnp.sum(p, 0, keepdims=True)
            out = dot_nn(values_t[h * HD : (h + 1) * HD], p.astype(bf16))
            outs.append(out * (1.0 / total))
            lses.append(m + jnp.log(total))
        out_ref[0, :, cut] = jnp.transpose(jnp.concatenate(outs, 0)).astype(bf16)
        lse_ref[0, g] = jnp.concatenate(lses, 0)


def cross_forward(lengths, queries, pairs):
    micro, rows, width = queries.shape
    count = pairs.shape[1]
    groups = width // 128
    return pl.pallas_call(
        cross_forward_kernel,
        grid=(micro,),
        in_specs=[
            pl.BlockSpec(memory_space=pltpu.SMEM),
            pl.BlockSpec((1, rows, width), lambda m: (m, 0, 0)),
            pl.BlockSpec((1, count, 2 * width), lambda m: (m, 0, 0)),
        ],
        out_specs=[
            pl.BlockSpec((1, rows, width), lambda m: (m, 0, 0)),
            pl.BlockSpec((1, groups, 2, rows), lambda m: (m, 0, 0, 0)),
        ],
        out_shape=[
            jax.ShapeDtypeStruct((micro, rows, width), bf16),
            jax.ShapeDtypeStruct((micro, groups, 2, rows), f32),
        ],
        compiler_params=pltpu.CompilerParams(vmem_limit_bytes=32 << 20),
        name="cross_forward",
    )(lengths, queries, pairs)


def cross_backward_kernel(
    lengths_ref, q_ref, pairs_ref, out_ref, lse_ref, gout_ref, gq_ref, gpairs_ref
):
    count, width, rows = pairs_ref.shape[1], q_ref.shape[2], q_ref.shape[1]
    masks = head_masks((rows, 128), 2)
    key_masks = head_masks((count, 128), 2)
    valid = (
        lax.broadcasted_iota(jnp.int32, (count, rows), 0) < lengths_ref[pl.program_id(0)]
    )
    lane = lax.broadcasted_iota(jnp.int32, (8, 128), 1)
    row = lax.broadcasted_iota(jnp.int32, (8, 128), 0)
    pick = jnp.where((lane >= row * HD) & (lane < (row + 1) * HD), 1.0, 0.0)
    for group in range(width // 128):
        cut = slice(group * 128, group * 128 + 128)
        value_cut = slice(width + group * 128, width + group * 128 + 128)
        q = q_ref[0, :, cut].astype(f32) * scale_factor
        g = gout_ref[0, :, cut].astype(f32)
        k = pairs_ref[0, :, cut].astype(f32)
        delta = lax.dot_general(
            pick,
            g * out_ref[0, :, cut].astype(f32),
            (((1,), (1,)), ((), ())),
            precision=lax.Precision.HIGHEST,
            preferred_element_type=f32,
        )
        grad_q = jnp.zeros((rows, 128), f32)
        grad_k = jnp.zeros((count, 128), f32)
        grad_v = jnp.zeros((count, 128), f32)
        for h in range(2):
            qh = keep_head(q, masks[h], 2).astype(bf16)
            gh = keep_head(g, masks[h], 2).astype(bf16)
            kh = keep_head(k, key_masks[h], 2).astype(bf16)
            s = dot_nt(pairs_ref[0, :, cut], qh) - lse_ref[0, group, h : h + 1, :]
            p = jnp.exp(jnp.where(valid, s, masked_score))
            gp = dot_nt(pairs_ref[0, :, value_cut], gh)
            gs = (p * (gp - delta[h : h + 1, :])).astype(bf16)
            grad_v += dot_nn(p.astype(bf16), gh)
            grad_k += dot_nn(gs, qh)
            grad_q += dot_tn(gs, kh)
        gq_ref[0, :, cut] = (grad_q * scale_factor).astype(bf16)
        gpairs_ref[0, :, cut] = grad_k.astype(bf16)
        gpairs_ref[0, :, value_cut] = grad_v.astype(bf16)


def cross_backward(lengths, queries, pairs, out, lse, gout):
    micro, rows, width = queries.shape
    count = pairs.shape[1]
    groups = width // 128
    row_spec = pl.BlockSpec((1, rows, width), lambda m: (m, 0, 0))
    pair_spec = pl.BlockSpec((1, count, 2 * width), lambda m: (m, 0, 0))
    return pl.pallas_call(
        cross_backward_kernel,
        grid=(micro,),
        in_specs=[
            pl.BlockSpec(memory_space=pltpu.SMEM),
            row_spec,
            pair_spec,
            row_spec,
            pl.BlockSpec((1, groups, 2, rows), lambda m: (m, 0, 0, 0)),
            row_spec,
        ],
        out_specs=[row_spec, pair_spec],
        out_shape=[
            jax.ShapeDtypeStruct((micro, rows, width), bf16),
            jax.ShapeDtypeStruct((micro, count, 2 * width), bf16),
        ],
        compiler_params=pltpu.CompilerParams(vmem_limit_bytes=32 << 20),
        name="cross_backward",
    )(lengths, queries, pairs, out, lse, gout)


def ffn_backward_kernel(
    branch_ref, hidden_ref, active_ref, slope_ref, down_ref, up_ref,
    grad_down_ref, grad_up_ref, grad_hidden_ref, hidden_t,
):
    @pl.when(pl.program_id(0) == 0)
    def _():
        hidden_t[...] = jnp.transpose(hidden_ref[...].astype(f32)).astype(bf16)
        grad_hidden_ref[...] = jnp.zeros_like(grad_hidden_ref)

    branch = branch_ref[...]
    grad_active = dot_nt(branch, down_ref[...])
    grad_inner = (slope_ref[...].astype(f32) * grad_active).astype(bf16)
    grad_down_ref[...] = dot_tn(active_ref[...], branch).astype(bf16)
    grad_up_ref[...] = dot_nn(hidden_t[...], grad_inner).astype(bf16)
    grad_hidden_ref[...] += dot_nt(grad_inner, up_ref[...])


def ffn_backward(branch, hidden, active, slope, down_weight, upward_weight):
    rows, width = branch.shape
    inner = active.shape[1]
    piece = 512
    whole = pl.BlockSpec((rows, width), lambda i: (0, 0))
    across = pl.BlockSpec((rows, piece), lambda i: (0, i))
    down = pl.BlockSpec((piece, width), lambda i: (i, 0))
    up = pl.BlockSpec((width, piece), lambda i: (0, i))
    return pl.pallas_call(
        ffn_backward_kernel,
        grid=(inner // piece,),
        in_specs=[whole, whole, across, across, down, up],
        out_specs=[down, up, whole],
        out_shape=[
            jax.ShapeDtypeStruct((inner, width), bf16),
            jax.ShapeDtypeStruct((width, inner), bf16),
            jax.ShapeDtypeStruct((rows, width), f32),
        ],
        scratch_shapes=[pltpu.VMEM((width, rows), bf16)],
        compiler_params=pltpu.CompilerParams(vmem_limit_bytes=48 << 20),
        name="ffn_backward",
    )(branch, hidden, active, slope, down_weight, upward_weight)


def gelu_parts(v):
    inner = 0.7978845608028654 * (v + 0.044715 * (v * v * v))
    t = jnp.tanh(inner)
    value = 0.5 * v * (1.0 + t)
    slope = 0.5 * (1.0 + t) + 0.5 * v * (1.0 - t * t) * (
        0.7978845608028654 * (1.0 + 3.0 * 0.044715 * (v * v))
    )
    return value, slope


def per_device(
    tokens,
    memory,
    cotangent,
    tile_segment,
    parents,
    memory_lengths,
    self_qkv,
    self_out,
    cross_q,
    cross_kv,
    cross_out,
    ffn_in,
    ffn_out,
    norm_gain,
    norm_bias,
):
    micro, _, row_count, width = tokens.shape
    seq = lax.axis_size("seq")
    total_rows = micro * row_count
    memory_rows = memory.shape[2]

    devices = seq * lax.axis_size("fsdp")
    z_size, y_size = seq // 2, lax.axis_size("fsdp") // 2

    def flat(blocks):
        return blocks.reshape(-1, blocks.shape[-1])

    joint_weight = flat(gather_first([self_qkv], ("all",), ((0,),), z_size, y_size, 4)[0])

    x = tokens.reshape(total_rows, width)
    x32 = x.astype(f32)
    bias = jax.vmap(lambda t, p: tree_bias(t, p, BLOCK))(tile_segment[:, 0], parents[:, 0])
    lengths = memory_lengths[:, 0]

    projected = dot_nn(x, joint_weight).astype(bf16)
    gathered = self_forward(
        projected.reshape(micro, row_count, 3 * width),
        bias,
        seq,
        [
            self_out,
            jnp.concatenate([norm_gain, norm_bias], 0).astype(f32),
            cross_q,
            cross_kv,
            memory.reshape(micro * memory_rows, width),
            cross_out,
            ffn_in,
            ffn_out,
        ],
        ("all", "all", "all", "all", "seq", "all", "all", "all"),
        ((0, 1), (2, 4), (3,), (5,), (6,), (7,)),
        y_size,
    )
    qkv, attended_heads, self_lse, attended = gathered[:4]
    self_output, cross_weight, pair_weight = (flat(gathered[i]) for i in (4, 6, 7))
    cross_output, upward_weight, down_weight = (flat(gathered[i]) for i in (9, 10, 11))
    norms = gathered[5].reshape(devices, 6, width // devices).transpose(1, 0, 2).reshape(6, width)
    gain_rows, bias_rows = norms[:3], norms[3:]
    memory_full = gathered[8].reshape(seq, micro, memory_rows, width).transpose(1, 0, 2, 3)
    memory_full = memory_full.reshape(micro, seq * memory_rows, width)
    attended = attended.reshape(total_rows, width)

    mixed_first = residual_weight * x32 + dot_nn(attended, self_output)
    hidden_first = layer_norm(mixed_first, gain_rows[0], bias_rows[0])
    hidden_first_low = hidden_first.astype(bf16)
    cross_query = dot_nn(hidden_first_low, cross_weight).astype(bf16)
    cross_query = cross_query.reshape(micro, row_count, width)
    count = memory_full.shape[1]
    pairs = dot_nn(memory_full.reshape(micro * count, width), pair_weight).astype(bf16)
    pairs = pairs.reshape(micro, count, 2 * width)
    cross_heads, cross_lse = cross_forward(lengths, cross_query, pairs)
    cross_attended = cross_heads.reshape(total_rows, width)
    mixed_second = residual_weight * hidden_first + dot_nn(cross_attended, cross_output)
    hidden_second = layer_norm(mixed_second, gain_rows[1], bias_rows[1])
    hidden_second_low = hidden_second.astype(bf16)
    pre_active = dot_nn(hidden_second_low, upward_weight)
    active, slope = gelu_parts(pre_active)
    active, slope = lax.optimization_barrier((active.astype(bf16), slope.astype(bf16)))
    mixed_third = residual_weight * hidden_second + dot_nn(active, down_weight)
    output = layer_norm(mixed_third, gain_rows[2], bias_rows[2]).astype(bf16)

    upstream = cotangent.reshape(total_rows, width).astype(f32)
    grad_third, gain_third, bias_third = layer_norm_back(mixed_third, gain_rows[2], upstream)
    branch_third = grad_third.astype(bf16)
    grad_down, grad_upward, grad_hidden = ffn_backward(
        branch_third, hidden_second_low, active, slope, down_weight, upward_weight
    )
    grad_hidden_second = residual_weight * grad_third + grad_hidden
    grad_second, gain_second, bias_second = layer_norm_back(
        mixed_second, gain_rows[1], grad_hidden_second
    )
    branch_second = grad_second.astype(bf16)
    grad_cross_output = dot_tn(cross_attended, branch_second).astype(bf16)
    grad_cross_attended = dot_nt(branch_second, cross_output).astype(bf16)
    grad_cross_low, memory_partial = cross_backward(
        lengths,
        cross_query,
        pairs,
        cross_heads,
        cross_lse,
        grad_cross_attended.reshape(micro, row_count, width),
    )
    memory_partial = memory_partial.reshape(micro * count, 2 * width)
    memory_share = dot_nt(memory_partial, pair_weight).astype(bf16)
    memory_share = memory_share.reshape(micro, seq, memory_rows, width).transpose(1, 0, 2, 3)
    grad_pair_weight = dot_tn(memory_full.reshape(micro * count, width), memory_partial)
    grad_cross_low = grad_cross_low.reshape(total_rows, width)
    grad_cross_weight = dot_tn(hidden_first_low, grad_cross_low).astype(bf16)
    grad_hidden_first = residual_weight * grad_second + dot_nt(grad_cross_low, cross_weight)
    grad_first, gain_first, bias_first = layer_norm_back(
        mixed_first, gain_rows[0], grad_hidden_first
    )
    branch_first = grad_first.astype(bf16)
    grad_self_output = dot_tn(attended, branch_first).astype(bf16)
    grad_attended = dot_nt(branch_first, self_output).astype(bf16)
    grad_projected, own_upward, own_down, grad_memory = self_backward(
        grad_attended.reshape(micro, row_count, width),
        qkv,
        bias,
        attended_heads,
        self_lse,
        seq,
        [grad_upward, grad_down, memory_share.reshape(seq * micro * memory_rows, width)],
        (True, False, "seq"),
        y_size,
    )
    grad_projected = grad_projected.reshape(total_rows, 3 * width)
    grad_joint = dot_tn(x, grad_projected).astype(bf16)
    grad_tokens = (residual_weight * grad_first + dot_nt(grad_projected, joint_weight)).astype(bf16)
    norm_grads = jnp.stack(
        [gain_first, gain_second, gain_third, bias_first, bias_second, bias_third]
    )
    norm_blocks = norm_grads.reshape(6, devices, width // devices).transpose(1, 0, 2)
    owned = scatter_grads(
        [
            grad_joint,
            grad_self_output,
            grad_pair_weight.astype(bf16),
            grad_cross_weight,
            grad_cross_output,
            norm_blocks.reshape(6 * devices, width // devices),
        ],
        (True, True, False, False, False, False),
        z_size,
        y_size,
        3,
    )
    return (
        output.reshape(tokens.shape),
        grad_tokens.reshape(tokens.shape),
        grad_memory.astype(bf16).reshape(memory.shape),
        owned[0],
        owned[1],
        owned[3],
        owned[2],
        owned[4],
        own_upward,
        own_down,
        owned[5][:3],
        owned[5][3:],
    )


def solution(mesh):
    rows = P(None, "fsdp", "seq", None)
    weight = P(ALL, None)
    in_specs = (
        rows,
        rows,
        rows,
        P(None, "fsdp", None),
        P(None, "fsdp", None),
        P(None, "fsdp"),
    ) + (weight,) * 7 + (P(None, ALL),) * 2
    out_specs = (rows, rows, rows) + (weight,) * 7 + (P(None, ALL),) * 2
    return jax.shard_map(
        per_device, mesh=mesh, in_specs=in_specs, out_specs=out_specs, check_vma=False
    )
```

```python
import functools

import jax
import jax.numpy as jnp
from jax import lax
from jax.experimental import pallas as pl
from jax.experimental.pallas import tpu as pltpu
from jax.sharding import PartitionSpec as P

H = 16
HD = 64
TILE = 128
BLOCK = 256
FIRST_SPLIT = 3
WINDOW = 4
GATHER_END = 85
SPLIT_ELEMENTS = 96 << 10
SCATTER_END = 95

scale_factor = 0.125
residual_weight = 36.0**0.25
norm_epsilon = 1e-05
masked_score = -1e30
ALL = ("seq", "fsdp")
f32 = jnp.float32
bf16 = jnp.bfloat16
MESH = pl.DeviceIdType.MESH


def dot_nn(a, b):
    return lax.dot_general(a, b, (((1,), (0,)), ((), ())), preferred_element_type=f32)


def dot_nt(a, b):
    return lax.dot_general(a, b, (((1,), (1,)), ((), ())), preferred_element_type=f32)


def dot_tn(a, b):
    return lax.dot_general(a, b, (((0,), (0,)), ((), ())), preferred_element_type=f32)


def norm_stats(incoming):
    row_mean = jnp.mean(incoming, -1, keepdims=True)
    centred = incoming - row_mean
    variance = jnp.mean(centred * centred, -1, keepdims=True)
    return centred, lax.rsqrt(variance + norm_epsilon)


def layer_norm(incoming, gain_row, bias_row):
    centred, inverse = norm_stats(incoming)
    return centred * inverse * gain_row + bias_row


def layer_norm_back(incoming, gain_row, upstream):
    centred, inverse = norm_stats(incoming)
    normal = centred * inverse
    grad_bias = jnp.sum(upstream, 0)
    grad_gain = jnp.sum(upstream * normal, 0)
    scaled = upstream * gain_row
    grad = inverse * (
        scaled
        - jnp.mean(scaled, -1, keepdims=True)
        - normal * jnp.mean(scaled * normal, -1, keepdims=True)
    )
    return grad, grad_gain, grad_bias


def ancestors(parent_ids):
    segment_ids = jnp.arange(parent_ids.shape[0], dtype=jnp.int32)
    hop = (parent_ids[:, None] == segment_ids[None, :]).astype(f32)
    reach = jnp.maximum(hop, (segment_ids[:, None] == segment_ids[None, :]).astype(f32))
    steps = 1
    while steps < parent_ids.shape[0]:
        reach = jnp.minimum(jnp.dot(reach, reach, precision=lax.Precision.HIGHEST), 1.0)
        steps *= 2
    return reach


def tree_bias(tile_segments, parent_ids, block):
    tiles = tile_segments.shape[0]
    onehot = (
        tile_segments[:, None] == jnp.arange(parent_ids.shape[0], dtype=jnp.int32)[None, :]
    ).astype(f32)
    high = lax.Precision.HIGHEST
    related = jnp.dot(
        jnp.dot(onehot, ancestors(parent_ids), precision=high), onehot.T, precision=high
    )
    bias = jnp.where(related > 0.5, 0.0, masked_score)
    per = block // TILE
    blocks = tiles // per
    bias = bias.reshape(blocks, per, blocks, per).transpose(2, 0, 3, 1)
    return jnp.repeat(bias, TILE, axis=3)


def head_masks(shape, heads):
    lane = lax.broadcasted_iota(jnp.int32, shape, 1)
    return [(lane >= h * HD) & (lane < (h + 1) * HD) for h in range(heads)]


def keep_head(value, mask, heads):
    return value if heads == 1 else jnp.where(mask, value, jnp.zeros_like(value))


def greet(peers):
    barrier = pltpu.get_barrier_semaphore()
    for peer in peers:
        pl.semaphore_signal(barrier, inc=1, device_id=peer, device_id_type=MESH)
    pl.semaphore_wait(barrier, len(peers))


def peer_at(step):
    count = lax.axis_size("seq")
    return lax.rem(lax.axis_index("seq") + step, count)


def rows_at(i, count):
    return pl.ds(pl.multiple_of(i * count, count), count)


def cut_heads(rows_ref, m, parts, blocks_ref):
    seq, part = blocks_ref.shape[2], blocks_ref.shape[4]
    for p in range(parts):
        for s in range(seq):
            first = (p * seq + s) * part
            blocks_ref[m, p, s] = rows_ref[m, :, first : first + part]


def join_heads(blocks_ref, m, parts, rows_ref):
    seq, part = blocks_ref.shape[2], blocks_ref.shape[4]
    for p in range(parts):
        for s in range(seq):
            first = (p * seq + s) * part
            rows_ref[m, :, first : first + part] = blocks_ref[m, p, s]


def to_peer(source_ref, target_ref, send, receive, m, step):
    rows = source_ref.shape[3]
    return pltpu.make_async_remote_copy(
        src_ref=source_ref.at[m, :, peer_at(step)],
        dst_ref=target_ref.at[m, :, rows_at(lax.axis_index("seq"), rows)],
        send_sem=send.at[m, step],
        recv_sem=receive.at[m, step],
        device_id={"seq": peer_at(step)},
        device_id_type=MESH,
    )


def to_self(source_ref, target_ref, sem, m):
    rows = source_ref.shape[3]
    me = lax.axis_index("seq")
    return pltpu.make_async_copy(
        source_ref.at[m, :, me], target_ref.at[m, :, rows_at(me, rows)], sem.at[m, 0]
    )


def send_blocks(source_ref, target_ref, send, receive, m):
    for step in range(1, lax.axis_size("seq")):
        to_peer(source_ref, target_ref, send, receive, m, step).start()
    to_self(source_ref, target_ref, send, m).start()


def take_blocks(source_ref, target_ref, send, receive, m, between=None):
    for step in range(1, lax.axis_size("seq")):
        to_peer(source_ref, target_ref, send, receive, m, step).wait_recv()
        if between is not None:
            between(step)
    to_self(source_ref, target_ref, send, m).wait()


def home_copy(source_ref, target_ref, send, receive, m, place):
    rows = target_ref.shape[3]
    me = lax.axis_index("seq")
    count = lax.axis_size("seq")
    step = lax.rem(place - me + count, count)
    return pltpu.make_async_remote_copy(
        src_ref=source_ref.at[m, :, rows_at(place, rows)],
        dst_ref=target_ref.at[m, :, me],
        send_sem=send.at[m, step],
        recv_sem=receive.at[m, step],
        device_id={"seq": place},
        device_id_type=MESH,
    )


def home_self(source_ref, target_ref, sem, m):
    rows = target_ref.shape[3]
    me = lax.axis_index("seq")
    return pltpu.make_async_copy(
        source_ref.at[m, :, rows_at(me, rows)], target_ref.at[m, :, me], sem.at[m, 0]
    )


def send_home(source_ref, target_ref, send, receive, m, place):
    me = lax.axis_index("seq")

    @pl.when(place != me)
    def _():
        home_copy(source_ref, target_ref, send, receive, m, place).start()

    @pl.when(place == me)
    def _():
        home_self(source_ref, target_ref, send, m).start()


def take_home(source_ref, target_ref, send, receive, m):
    for step in range(1, lax.axis_size("seq")):
        home_copy(source_ref, target_ref, send, receive, m, peer_at(step)).wait()
    home_self(source_ref, target_ref, send, m).wait()


def scatter_places():
    s, f = lax.axis_index("seq"), lax.axis_index("fsdp")
    z, y = s // 2, f // 2
    return z, s - 2 * z, y, f - 2 * y, lax.axis_size("seq") // 2, lax.axis_size("fsdp") // 2


def scatter_peers():
    z, x, y, c, z_size, y_size = scatter_places()
    peers = [{"fsdp": 2 * y + 1 - c}, {"seq": 2 * z + 1 - x}]
    peers += [{"fsdp": 2 * lax.rem(y + k, y_size) + c} for k in range(1, y_size)]
    peers += [{"seq": 2 * lax.rem(z + k, z_size) + x} for k in range(1, z_size)]
    return peers


def scatter_shapes(blocks, x_first):
    if x_first == "seq":
        z_size, _, rows, columns = blocks.shape
        shape = (z_size, rows, columns)
        return [pltpu.VMEM(shape, blocks.dtype)] * 2 + [
            pltpu.VMEM((z_size - 1, rows, columns), blocks.dtype)
        ]
    z_size, _, y_size, _, rows, columns = blocks.shape
    if x_first:
        first, second = (1, y_size), (y_size - 1,)
    else:
        first, second = (y_size - 1, 2), (1,)
    kind = blocks.dtype
    return [
        pltpu.VMEM((z_size, 2, y_size, rows, columns), kind),
        pltpu.VMEM((z_size, 2, y_size, rows, columns), kind),
        pltpu.VMEM((z_size,) + first + (rows, columns), kind),
        pltpu.VMEM((z_size,) + second + (rows, columns), kind),
        pltpu.VMEM((z_size - 1, rows, columns), kind),
    ]


def scatter_sems(count, z_size, y_size):
    pair = pltpu.SemaphoreType.DMA((count, z_size))
    triple = pltpu.SemaphoreType.DMA((count, z_size, max(1, y_size - 1)))
    return [pair, pair, pair, triple, triple, triple, triple, pair, pair]


def add_into(target, source):
    target[...] = target[...] + source[...]


def scatter_steps(kinds, sources, outs, buffers, sems):
    z, x, y, c, z_size, y_size = scatter_places()
    local, core_s, core_r, first_s, first_r, second_s, second_r, last_s, last_r = sems
    count = len(sources)

    def to_z(t):
        return lax.rem(z + 1 + t, z_size)

    def remote(source, target, send, receive, peer):
        return pltpu.make_async_remote_copy(
            src_ref=source,
            dst_ref=target,
            send_sem=send,
            recv_sem=receive,
            device_id=peer,
            device_id_type=MESH,
        )

    across = [a for a in range(count) if kinds[a] != "seq"]
    along = [a for a in range(count) if kinds[a] == "seq"]

    def own_copy(a, t):
        if kinds[a] == "seq":
            source = sources[a].at[to_z(t), x]
        else:
            source = sources[a].at[to_z(t), :, :, c]
        return pltpu.make_async_copy(source, buffers[a][0].at[t], local.at[a, t])

    def seq_first(a, t):
        return remote(
            sources[a].at[to_z(t), 1 - x],
            buffers[a][1].at[t],
            core_s.at[a, t],
            core_r.at[a, t],
            x_peer(),
        )

    def seq_last(a, t):
        return remote(
            buffers[a][0].at[t],
            buffers[a][2].at[t],
            last_s.at[a, t],
            last_r.at[a, t],
            {"seq": 2 * to_z(t) + x},
        )

    def core_copy(a, t):
        return remote(
            sources[a].at[to_z(t), :, :, 1 - c],
            buffers[a][1].at[t],
            core_s.at[a, t],
            core_r.at[a, t],
            {"fsdp": 2 * y + 1 - c},
        )

    def x_peer():
        return {"seq": 2 * z + 1 - x}

    def y_place(k):
        return lax.rem(y + k, y_size)

    def y_peer(k):
        return {"fsdp": 2 * y_place(k) + c}

    def first_copies(a, t):
        own, _, first, _, _ = buffers[a]
        if kinds[a]:
            sends = [(own.at[t, 1 - x], x_peer())]
        else:
            sends = [(own.at[t, :, y_place(k)], y_peer(k)) for k in range(1, y_size)]
        return [
            remote(source, first.at[t, k], first_s.at[a, t, k], first_r.at[a, t, k], peer)
            for k, (source, peer) in enumerate(sends)
        ]

    def second_copies(a, t):
        own, _, _, second, _ = buffers[a]
        if kinds[a]:
            sends = [(own.at[t, x, y_place(k)], y_peer(k)) for k in range(1, y_size)]
        else:
            sends = [(own.at[t, 1 - x, y], x_peer())]
        return [
            remote(source, second.at[t, k], second_s.at[a, t, k], second_r.at[a, t, k], peer)
            for k, (source, peer) in enumerate(sends)
        ]

    def last_copy(a, t):
        own, _, _, _, last = buffers[a]
        return remote(
            own.at[t, x, y],
            last.at[t],
            last_s.at[a, t],
            last_r.at[a, t],
            {"seq": 2 * to_z(t) + x},
        )

    def start_core(t):
        for a in range(count):
            (core_copy if a in across else seq_first)(a, t).start()
            own_copy(a, t).start()

    def core_step(t):
        for a in across:
            core_copy(a, t).wait_recv()
            own_copy(a, t).wait()
            own, core = buffers[a][:2]

            def add(i, carry, own=own, core=core):
                add_into(own.at[t, i // y_size, i % y_size], core.at[t, i // y_size, i % y_size])
                return carry

            lax.fori_loop(0, 2 * y_size, add, 0)
            for copy in first_copies(a, t):
                copy.start()
        if t + 2 < z_size:
            start_core(t + 2)

    def first_step(t):
        for a in across:
            own, _, first, _, _ = buffers[a]
            for k, copy in enumerate(first_copies(a, t)):
                copy.wait_recv()
                for i in range(y_size if kinds[a] else 2):
                    target = own.at[t, x, i] if kinds[a] else own.at[t, i, y]
                    add_into(target, first.at[t, k, i])
            for copy in second_copies(a, t):
                copy.start()

    def second_step(t):
        for a in along:
            seq_first(a, t).wait_recv()
            own_copy(a, t).wait()
            add_into(buffers[a][0].at[t], buffers[a][1].at[t])
            if t < z_size - 1:
                seq_last(a, t).start()
        for a in across:
            own, _, _, second, _ = buffers[a]
            for k, copy in enumerate(second_copies(a, t)):
                copy.wait_recv()
                add_into(own.at[t, x, y], second.at[t, k])
            if t < z_size - 1:
                last_copy(a, t).start()

    def final_step():
        for a in along:
            own, _, last = buffers[a]
            total = own[z_size - 1].astype(f32)
            for t in range(z_size - 1):
                seq_last(a, t).wait()
                total = total + last[t].astype(f32)
            outs[a][...] = total
            for t in range(z_size):
                seq_first(a, t).wait_send()
        for a in across:
            own, _, _, _, last = buffers[a]
            total = own[z_size - 1, x, y].astype(f32)
            for t in range(z_size - 1):
                last_copy(a, t).wait()
                total = total + last[t].astype(f32)
            outs[a][...] = total
            for t in range(z_size):
                core_copy(a, t).wait_send()
                for copy in first_copies(a, t) + second_copies(a, t):
                    copy.wait_send()

    def opening():
        start_core(0)
        if z_size > 1:
            start_core(1)

    steps = [opening]
    for t in range(z_size + 2):
        if t < z_size:
            steps.append(functools.partial(core_step, t))
        if 0 <= t - 1 < z_size:
            steps.append(functools.partial(first_step, t - 1))
        if 0 <= t - 2 < z_size:
            steps.append(functools.partial(second_step, t - 2))
    steps.append(final_step)
    return steps


def scatter_buffers(kinds, refs):
    buffers = []
    for kind in kinds:
        size = 3 if kind == "seq" else 5
        buffers.append(refs[:size])
        refs = refs[size:]
    return buffers, refs


def scatter_kernel(kinds, *refs):
    count = len(kinds)
    sources, outs, rest = refs[:count], refs[count : 2 * count], refs[2 * count :]
    buffers, rest = scatter_buffers(kinds, rest)
    greet(scatter_peers())
    for step in scatter_steps(kinds, sources, outs, buffers, rest):
        step()


def scatter_blocks(arrays, kinds, z_size, y_size):
    blocks = []
    for a, kind in zip(arrays, kinds):
        lead = (z_size, 2) if kind == "seq" else (z_size, 2, y_size, 2)
        blocks.append(a.reshape(lead + (-1, a.shape[1])))
    return blocks


def scatter_grads(arrays, kinds, z_size, y_size, collective_id):
    blocks = scatter_blocks(arrays, kinds, z_size, y_size)
    scratch = []
    for block, kind in zip(blocks, kinds):
        scratch += scatter_shapes(block, kind)
    return pl.pallas_call(
        functools.partial(scatter_kernel, kinds),
        in_specs=[pl.BlockSpec(memory_space=pl.ANY)] * len(arrays),
        out_specs=[pl.BlockSpec(memory_space=pltpu.VMEM)] * len(arrays),
        out_shape=[jax.ShapeDtypeStruct(b.shape[-2:], f32) for b in blocks],
        scratch_shapes=scratch + scatter_sems(len(arrays), z_size, y_size),
        compiler_params=pltpu.CompilerParams(
            vmem_limit_bytes=60 << 20, collective_id=collective_id, has_side_effects=True
        ),
        name="scatter_grads",
    )(*blocks)


def spread(steps, first, last):
    return [(first + k * (last - first) // max(1, len(steps) - 1), s) for k, s in enumerate(steps)]


def run_slot(placed, slot):
    for at, step in placed:
        pl.when(slot == at)(step)


def both_peers():
    _, _, y, c, _, y_size = scatter_places()
    peers = [{"seq": peer_at(step)} for step in range(1, lax.axis_size("seq"))]
    peers += [{"fsdp": 2 * y + 1 - c}]
    return peers + [{"fsdp": 2 * lax.rem(y + k, y_size) + c} for k in range(1, y_size)]


def gather_parts(shards, kinds, groups, most=2):
    parts, units = [], []
    for group in groups:
        pieces = []
        for a in group:
            rows, columns = shards[a].shape
            kind = kinds[a]
            split = most if rows % 32 == 0 and rows * columns >= SPLIT_ELEMENTS else 1
            for n in range(split):
                cut = (n * columns // split, columns // split)
                if kind == "seq" or rows % 32:
                    piece = [(a, 0, rows) + cut + ("x" if kind == "all" else kind,)]
                else:
                    half = rows // 2
                    piece = [(a, 0, half) + cut + ("x",), (a, half, half) + cut + ("y",)]
                if n == len(pieces):
                    pieces.append([])
                pieces[n] += piece
        for piece in pieces:
            units.append(range(len(parts), len(parts) + len(piece)))
            parts += piece
    return parts, units


def gather_sems(plan, z_size, y_size):
    count = len(plan[0])
    z_sem = pltpu.SemaphoreType.DMA((count, z_size))
    y_sem = pltpu.SemaphoreType.DMA((count, max(1, y_size - 1)))
    one = pltpu.SemaphoreType.DMA((count, 1))
    return [z_sem, z_sem, y_sem, y_sem, y_sem, y_sem, one, one]


def gather_steps(plan, shards, outs, sems):
    z, x, y, c, z_size, y_size = scatter_places()
    z_s, z_r, first_s, first_r, second_s, second_r, core_s, core_r = sems
    parts, units = plan

    def remote(view, peer, send, receive):
        return pltpu.make_async_remote_copy(
            src_ref=view,
            dst_ref=view,
            send_sem=send,
            recv_sem=receive,
            device_id=peer,
            device_id_type=MESH,
        )

    def shard_of(p):
        a, start, rows, left, columns, _ = parts[p]
        return shards[a].at[pl.ds(start, rows), pl.ds(left, columns)]

    def place(p, *lead):
        a, start, rows, left, columns, _ = parts[p]
        return outs[a].at[lead + (pl.ds(start, rows), pl.ds(left, columns))]

    def own(p):
        return place(p, z, x) if parts[p][-1] == "seq" else place(p, z, x, y, c)

    def own_copy(p):
        return pltpu.make_async_copy(shard_of(p), own(p), z_s.at[p, 0])

    def z_copies(p):
        return [
            pltpu.make_async_remote_copy(
                src_ref=shard_of(p),
                dst_ref=own(p),
                send_sem=z_s.at[p, k],
                recv_sem=z_r.at[p, k],
                device_id={"seq": 2 * lax.rem(z + k, z_size) + x},
                device_id_type=MESH,
            )
            for k in range(1, z_size)
        ]

    def x_peer():
        return {"seq": 2 * z + 1 - x}

    def y_peers():
        return [{"fsdp": 2 * lax.rem(y + k, y_size) + c} for k in range(1, y_size)]

    whole = slice(None)

    def first_copies(p):
        kind = parts[p][-1]
        view = place(p, whole, x) if kind == "seq" else place(p, whole, x, y, c)
        peers = y_peers() if kind == "y" else [x_peer()]
        return [
            remote(view, peer, first_s.at[p, k], first_r.at[p, k]) for k, peer in enumerate(peers)
        ]

    def second_copies(p):
        kind = parts[p][-1]
        if kind == "seq":
            return []
        view = place(p, whole, whole, y, c) if kind == "x" else place(p, whole, x, whole, c)
        peers = y_peers() if kind == "x" else [x_peer()]
        return [
            remote(view, peer, second_s.at[p, k], second_r.at[p, k]) for k, peer in enumerate(peers)
        ]

    def core_copies(p):
        if parts[p][-1] == "seq":
            return []
        view = place(p, whole, whole, whole, c)
        return [remote(view, {"fsdp": 2 * y + 1 - c}, core_s.at[p, 0], core_r.at[p, 0])]

    def step(t):
        def unit(at):
            return units[at] if 0 <= at < len(units) else ()

        for p in unit(t - 3):
            for copy in second_copies(p):
                copy.wait_recv()
            for copy in core_copies(p):
                copy.start()
        for p in unit(t - 2):
            for copy in first_copies(p):
                copy.wait_recv()
            for copy in second_copies(p):
                copy.start()
        for p in unit(t - 1):
            for copy in z_copies(p):
                copy.wait_recv()
            own_copy(p).wait()
            for copy in first_copies(p):
                copy.start()
        for p in unit(t):
            for copy in z_copies(p):
                copy.start()
            own_copy(p).start()

    def final_step():
        for p in range(len(parts)):
            for copy in core_copies(p):
                copy.wait()
            for copy in z_copies(p) + first_copies(p) + second_copies(p):
                copy.wait_send()

    return [functools.partial(step, t) for t in range(len(units) + 3)] + [final_step]


def gather_out(shard, kind, z_size, y_size):
    lead = (z_size, 2) if kind == "seq" else (z_size, 2, y_size, 2)
    return jax.ShapeDtypeStruct(lead + shard.shape, shard.dtype)


def gather_kernel(plan, count, *refs):
    shards, outs, sems = refs[:count], refs[count : 2 * count], refs[2 * count :]
    greet(scatter_peers())
    for step in gather_steps(plan, shards, outs, sems):
        step()


def gather_first(shards, kinds, groups, z_size, y_size, collective_id):
    plan = gather_parts(shards, kinds, groups, FIRST_SPLIT)
    return pl.pallas_call(
        functools.partial(gather_kernel, plan, len(shards)),
        in_specs=[pl.BlockSpec(memory_space=pl.ANY)] * len(shards),
        out_specs=[pl.BlockSpec(memory_space=pl.ANY)] * len(shards),
        out_shape=[gather_out(s, k, z_size, y_size) for s, k in zip(shards, kinds)],
        scratch_shapes=gather_sems(plan, z_size, y_size),
        compiler_params=pltpu.CompilerParams(collective_id=collective_id, has_side_effects=True),
        name="gather_first",
    )(*shards)


def self_forward_kernel(heads, block, plan, count, *refs):
    rows_ref, bias_ref = refs[:2]
    shards, refs = refs[2 : 2 + count], refs[2 + count :]
    qkv_ref, out_ref, lse_ref, attended_ref = refs[:4]
    whole, refs = refs[4 : 4 + count], refs[4 + count :]
    cut, back, queries, values_t, send_in, take_in, send_out, take_out = refs[:8]
    gather = gather_steps(plan, shards, whole, refs[8:])
    micro, _, length, width = qkv_ref.shape
    seq = lax.axis_size("seq")
    blocks = length // block
    per = block // TILE
    place_rows = length // seq
    masks = head_masks((block, width), heads)
    per_micro = blocks + seq - 1
    window = min(WINDOW, seq - 1)
    placed = spread(gather[1:-1], 0, GATHER_END * micro * per_micro // 100)
    greet(both_peers())

    def launch(m, carry):
        cut_heads(rows_ref, m, 3, cut)

        @pl.when(m < 1)
        def _():
            for step in range(1, window + 1):
                to_peer(cut, qkv_ref, send_in, take_in, m, step).start()

        to_self(cut, qkv_ref, send_in, m).start()
        return carry

    lax.fori_loop(0, micro, launch, 0)
    gather[0]()
    key_place = lax.broadcasted_iota(jnp.int32, (block, block), 0)
    query_place = lax.broadcasted_iota(jnp.int32, (block, block), 1)
    causal = key_place <= query_place

    def one_micro(m, carry):
        def between(step):
            run_slot(placed, m * per_micro + step - 1)
            if step + window < seq:
                to_peer(cut, qkv_ref, send_in, take_in, m, step + window).start()
            else:

                @pl.when(m + 1 < micro)
                def _():
                    following = step + window + 1 - seq
                    to_peer(cut, qkv_ref, send_in, take_in, m + 1, following).start()

        take_blocks(cut, qkv_ref, send_in, take_in, m, between)

        def prepare(i, carry):
            rows = rows_at(i, block)
            q = qkv_ref[m, 0, rows, :].astype(f32) * scale_factor
            for h in range(heads):
                queries[h, rows, :] = keep_head(q, masks[h], heads).astype(bf16)
            values_t[i] = jnp.transpose(qkv_ref[m, 2, rows, :].astype(f32)).astype(bf16)
            return carry

        lax.fori_loop(0, blocks, prepare, 0)

        def scores_of(i, j, count, h):
            keys = pl.ds(pl.multiple_of(j * block, block), count * block)
            raw = dot_nt(qkv_ref[m, 1, keys, :], queries[h, rows_at(i, block), :])
            bias = jnp.concatenate([bias_ref[m, j + k, i] for k in range(count)], 0)
            raw = raw.reshape(count * per, TILE, block) + bias[:, None, :]
            return raw.reshape(count * block, block)

        def values_by(j, count, h, p):
            p = p.astype(bf16)
            return sum(
                dot_nn(values_t[j + k][h * HD : (h + 1) * HD], p[k * block : (k + 1) * block])
                for k in range(count)
            )

        def query_block(i, carry):
            run_slot(placed, m * per_micro + seq - 1 + i)
            state = []
            for h in range(heads):
                s = jnp.where(causal, scores_of(i, i, 1, h), masked_score)
                top = jnp.max(s, 0, keepdims=True)
                p = jnp.exp(s - top)
                state += [top, jnp.sum(p, 0, keepdims=True), values_by(i, 1, h, p)]

            def key_blocks(j, count, state):
                fresh = []
                for h in range(heads):
                    top, total, acc = state[3 * h : 3 * h + 3]
                    s = scores_of(i, j, count, h)
                    higher = jnp.maximum(top, jnp.max(s, 0, keepdims=True))
                    shrink = jnp.exp(top - higher)
                    p = jnp.exp(s - higher)
                    total = total * shrink + jnp.sum(p, 0, keepdims=True)
                    fresh += [higher, total, acc * shrink + values_by(j, count, h, p)]
                return tuple(fresh)

            pairs = i // 2
            state = lax.fori_loop(0, pairs, lambda j, s: key_blocks(2 * j, 2, s), tuple(state))
            state = lax.fori_loop(2 * pairs, i, lambda j, s: key_blocks(j, 1, s), state)
            out = jnp.concatenate(
                [state[3 * h + 2] * (1.0 / state[3 * h + 1]) for h in range(heads)], 0
            )
            out_ref[m, 0, rows_at(i, block), :] = jnp.transpose(out).astype(bf16)
            lse_ref[m, i] = jnp.concatenate(
                [state[3 * h] + jnp.log(state[3 * h + 1]) for h in range(heads)], 0
            )
            for sub in range(block // place_rows):
                place = i * (block // place_rows) + sub
                send_home(out_ref, back, send_out, take_out, m, place)
            return carry

        lax.fori_loop(0, blocks, query_block, 0)
        return carry

    lax.fori_loop(0, micro, one_micro, 0)

    def finish(m, carry):
        for step in range(1, seq):
            to_peer(cut, qkv_ref, send_in, take_in, m, step).wait_send()
        take_home(out_ref, back, send_out, take_out, m)
        join_heads(back, m, 1, attended_ref)
        return carry

    lax.fori_loop(0, micro, finish, 0)
    gather[-1]()


def self_forward(projected, bias, seq, shards, kinds, groups, y_size):
    micro, rows, width = projected.shape
    part = width // 3 // seq
    heads = part // HD
    length = rows * seq
    blocks = length // BLOCK
    whole = pl.BlockSpec(memory_space=pltpu.VMEM)
    sems = pltpu.SemaphoreType.DMA((micro, seq))
    count = len(shards)
    any_place = [pl.BlockSpec(memory_space=pl.ANY)] * count
    plan = gather_parts(shards, kinds, groups)
    return pl.pallas_call(
        functools.partial(self_forward_kernel, heads, BLOCK, plan, count),
        in_specs=[whole, whole] + any_place,
        out_specs=[whole] * 4 + any_place,
        out_shape=[
            jax.ShapeDtypeStruct((micro, 3, length, part), bf16),
            jax.ShapeDtypeStruct((micro, 1, length, part), bf16),
            jax.ShapeDtypeStruct((micro, blocks, heads, BLOCK), f32),
            jax.ShapeDtypeStruct((micro, rows, width // 3), bf16),
        ]
        + [gather_out(s, k, seq // 2, y_size) for s, k in zip(shards, kinds)],
        scratch_shapes=[
            pltpu.VMEM((micro, 3, seq, rows, part), bf16),
            pltpu.VMEM((micro, 1, seq, rows, part), bf16),
            pltpu.VMEM((heads, length, part), bf16),
            pltpu.VMEM((blocks, part, BLOCK), bf16),
            sems,
            sems,
            sems,
            sems,
        ]
        + gather_sems(plan, seq // 2, y_size),
        compiler_params=pltpu.CompilerParams(
            vmem_limit_bytes=50 << 20, collective_id=1, has_side_effects=True
        ),
        name="self_forward",
    )(projected, bias, *shards)


def self_backward_kernel(heads, block, kinds, *refs):
    count = len(kinds)
    rows_ref, qkv_ref, bias_ref, out_ref, lse_ref = refs[:5]
    sources, refs = refs[5 : 5 + count], refs[5 + count :]
    grad_ref, owned, refs = refs[0], refs[1 : 1 + count], refs[1 + count :]
    cut, gout, grads, back, queries, keys_h, gouts, delta, grad_q = refs[:9]
    send_in, take_in, send_out, take_out = refs[9:13]
    buffers, refs = scatter_buffers(kinds, refs[13:])
    scatter = scatter_steps(kinds, sources, owned, buffers, refs)
    micro, _, length, width = qkv_ref.shape
    seq = lax.axis_size("seq")
    blocks = length // block
    per = block // TILE
    place_rows = length // seq
    masks = head_masks((block, width), heads)
    lane = lax.broadcasted_iota(jnp.int32, (8, width), 1)
    first_lane = lax.broadcasted_iota(jnp.int32, (8, width), 0) * HD
    pick = jnp.where((lane >= first_lane) & (lane < first_lane + HD), 1.0, 0.0)
    placed = spread(scatter[1:-1], 1, SCATTER_END * micro * blocks // 100)
    greet(both_peers())

    def launch(m, carry):
        cut_heads(rows_ref, m, 1, cut)

        @pl.when(m < 1)
        def _():
            send_blocks(cut, gout, send_in, take_in, m)

        return carry

    lax.fori_loop(0, micro, launch, 0)
    scatter[0]()
    key_place = lax.broadcasted_iota(jnp.int32, (block, block), 0)
    query_place = lax.broadcasted_iota(jnp.int32, (block, block), 1)
    causal = key_place <= query_place

    def one_micro(m, carry):
        take_blocks(cut, gout, send_in, take_in, m)

        @pl.when(m + 1 < micro)
        def _():
            send_blocks(cut, gout, send_in, take_in, m + 1)

        def prepare(i, carry):
            rows = rows_at(i, block)
            q = qkv_ref[m, 0, rows, :].astype(f32) * scale_factor
            k = qkv_ref[m, 1, rows, :].astype(f32)
            g = gout[m, 0, rows, :].astype(f32)
            for h in range(heads):
                queries[h, rows, :] = keep_head(q, masks[h], heads).astype(bf16)
                keys_h[h, rows, :] = keep_head(k, masks[h], heads).astype(bf16)
                gouts[h, rows, :] = keep_head(g, masks[h], heads).astype(bf16)
            delta[i] = lax.dot_general(
                pick,
                g * out_ref[m, 0, rows, :].astype(f32),
                (((1,), (1,)), ((), ())),
                precision=lax.Precision.HIGHEST,
                preferred_element_type=f32,
            )
            grad_q[rows, :] = jnp.zeros((block, width), f32)
            return carry

        lax.fori_loop(0, blocks, prepare, 0)

        def key_block(j, carry):
            run_slot(placed, m * blocks + j)
            krows = rows_at(j, block)

            def pair(i, grad_k, grad_v, diagonal):
                rows = rows_at(i, block)
                bias = bias_ref[m, j, i]
                gq = grad_q[rows, :]
                for h in range(heads):
                    raw = dot_nt(qkv_ref[m, 1, krows, :], queries[h, rows, :])
                    shift = bias - lse_ref[m, i, h : h + 1, :]
                    s = (raw.reshape(per, TILE, block) + shift[:, None, :]).reshape(block, block)
                    if diagonal:
                        s = jnp.where(causal, s, masked_score)
                    p = jnp.exp(s)
                    gp = dot_nt(qkv_ref[m, 2, krows, :], gouts[h, rows, :])
                    gs = (p * (gp - delta[i, h : h + 1, :])).astype(bf16)
                    grad_v = grad_v + dot_nn(p.astype(bf16), gouts[h, rows, :])
                    grad_k = grad_k + dot_nn(gs, queries[h, rows, :])
                    gq = gq + dot_tn(gs, keys_h[h, krows, :])
                grad_q[rows, :] = gq
                return grad_k, grad_v

            zero = jnp.zeros((block, width), f32)
            state = pair(j, zero, zero, True)
            state = lax.fori_loop(
                j + 1, blocks, lambda i, s: pair(i, s[0], s[1], False), state
            )
            grads[m, 0, krows, :] = (grad_q[krows, :] * scale_factor).astype(bf16)
            grads[m, 1, krows, :] = state[0].astype(bf16)
            grads[m, 2, krows, :] = state[1].astype(bf16)
            for sub in range(block // place_rows):
                place = j * (block // place_rows) + sub
                send_home(grads, back, send_out, take_out, m, place)
            return carry

        lax.fori_loop(0, blocks, key_block, 0)
        return carry

    lax.fori_loop(0, micro, one_micro, 0)

    def finish(m, carry):
        for step in range(1, seq):
            to_peer(cut, gout, send_in, take_in, m, step).wait_send()
        take_home(grads, back, send_out, take_out, m)
        join_heads(back, m, 3, grad_ref)
        return carry

    scatter[-1]()
    lax.fori_loop(0, micro, finish, 0)


def self_backward(grad_attended, qkv, bias, out, lse, seq, arrays, kinds, y_size):
    micro, rows, width = grad_attended.shape
    length, part = qkv.shape[2:]
    heads = part // HD
    blocks = length // BLOCK
    whole = pl.BlockSpec(memory_space=pltpu.VMEM)
    sems = pltpu.SemaphoreType.DMA((micro, seq))
    sources = scatter_blocks(arrays, kinds, seq // 2, y_size)
    count = len(arrays)
    scratch = []
    for source, kind in zip(sources, kinds):
        scratch += scatter_shapes(source, kind)
    return pl.pallas_call(
        functools.partial(self_backward_kernel, heads, BLOCK, kinds),
        in_specs=[whole] * 5 + [pl.BlockSpec(memory_space=pl.ANY)] * count,
        out_specs=[whole] * (1 + count),
        out_shape=[jax.ShapeDtypeStruct((micro, rows, 3 * width), bf16)]
        + [jax.ShapeDtypeStruct(b.shape[-2:], f32) for b in sources],
        scratch_shapes=[
            pltpu.VMEM((micro, 1, seq, rows, part), bf16),
            pltpu.VMEM((micro, 1, length, part), bf16),
            pltpu.VMEM((micro, 3, length, part), bf16),
            pltpu.VMEM((micro, 3, seq, rows, part), bf16),
            pltpu.VMEM((heads, length, part), bf16),
            pltpu.VMEM((heads, length, part), bf16),
            pltpu.VMEM((heads, length, part), bf16),
            pltpu.VMEM((blocks, 8, BLOCK), f32),
            pltpu.VMEM((length, part), f32),
            sems,
            sems,
            sems,
            sems,
        ]
        + scratch
        + scatter_sems(count, seq // 2, y_size),
        compiler_params=pltpu.CompilerParams(
            vmem_limit_bytes=60 << 20, collective_id=2, has_side_effects=True
        ),
        name="self_backward",
    )(grad_attended, qkv, bias, out, lse, *sources)


def cross_forward_kernel(lengths_ref, q_ref, pairs_ref, out_ref, lse_ref):
    count, width, rows = pairs_ref.shape[1], q_ref.shape[2], q_ref.shape[1]
    masks = head_masks((rows, 128), 2)
    valid = (
        lax.broadcasted_iota(jnp.int32, (count, rows), 0) < lengths_ref[pl.program_id(0)]
    )
    for g in range(width // 128):
        cut = slice(g * 128, g * 128 + 128)
        q = q_ref[0, :, cut].astype(f32) * scale_factor
        values = pairs_ref[0, :, width + g * 128 : width + g * 128 + 128]
        values_t = jnp.transpose(values.astype(f32)).astype(bf16)
        outs, lses = [], []
        for h in range(2):
            s = dot_nt(pairs_ref[0, :, cut], keep_head(q, masks[h], 2).astype(bf16))
            s = jnp.where(valid, s, masked_score)
            m = jnp.max(s, 0, keepdims=True)
            p = jnp.exp(s - m)
            total = jnp.sum(p, 0, keepdims=True)
            out = dot_nn(values_t[h * HD : (h + 1) * HD], p.astype(bf16))
            outs.append(out * (1.0 / total))
            lses.append(m + jnp.log(total))
        out_ref[0, :, cut] = jnp.transpose(jnp.concatenate(outs, 0)).astype(bf16)
        lse_ref[0, g] = jnp.concatenate(lses, 0)


def cross_forward(lengths, queries, pairs):
    micro, rows, width = queries.shape
    count = pairs.shape[1]
    groups = width // 128
    return pl.pallas_call(
        cross_forward_kernel,
        grid=(micro,),
        in_specs=[
            pl.BlockSpec(memory_space=pltpu.SMEM),
            pl.BlockSpec((1, rows, width), lambda m: (m, 0, 0)),
            pl.BlockSpec((1, count, 2 * width), lambda m: (m, 0, 0)),
        ],
        out_specs=[
            pl.BlockSpec((1, rows, width), lambda m: (m, 0, 0)),
            pl.BlockSpec((1, groups, 2, rows), lambda m: (m, 0, 0, 0)),
        ],
        out_shape=[
            jax.ShapeDtypeStruct((micro, rows, width), bf16),
            jax.ShapeDtypeStruct((micro, groups, 2, rows), f32),
        ],
        compiler_params=pltpu.CompilerParams(vmem_limit_bytes=32 << 20),
        name="cross_forward",
    )(lengths, queries, pairs)


def cross_backward_kernel(
    lengths_ref, q_ref, pairs_ref, out_ref, lse_ref, gout_ref, gq_ref, gpairs_ref
):
    count, width, rows = pairs_ref.shape[1], q_ref.shape[2], q_ref.shape[1]
    masks = head_masks((rows, 128), 2)
    key_masks = head_masks((count, 128), 2)
    valid = (
        lax.broadcasted_iota(jnp.int32, (count, rows), 0) < lengths_ref[pl.program_id(0)]
    )
    lane = lax.broadcasted_iota(jnp.int32, (8, 128), 1)
    row = lax.broadcasted_iota(jnp.int32, (8, 128), 0)
    pick = jnp.where((lane >= row * HD) & (lane < (row + 1) * HD), 1.0, 0.0)
    for group in range(width // 128):
        cut = slice(group * 128, group * 128 + 128)
        value_cut = slice(width + group * 128, width + group * 128 + 128)
        q = q_ref[0, :, cut].astype(f32) * scale_factor
        g = gout_ref[0, :, cut].astype(f32)
        k = pairs_ref[0, :, cut].astype(f32)
        delta = lax.dot_general(
            pick,
            g * out_ref[0, :, cut].astype(f32),
            (((1,), (1,)), ((), ())),
            precision=lax.Precision.HIGHEST,
            preferred_element_type=f32,
        )
        grad_q = jnp.zeros((rows, 128), f32)
        grad_k = jnp.zeros((count, 128), f32)
        grad_v = jnp.zeros((count, 128), f32)
        for h in range(2):
            qh = keep_head(q, masks[h], 2).astype(bf16)
            gh = keep_head(g, masks[h], 2).astype(bf16)
            kh = keep_head(k, key_masks[h], 2).astype(bf16)
            s = dot_nt(pairs_ref[0, :, cut], qh) - lse_ref[0, group, h : h + 1, :]
            p = jnp.exp(jnp.where(valid, s, masked_score))
            gp = dot_nt(pairs_ref[0, :, value_cut], gh)
            gs = (p * (gp - delta[h : h + 1, :])).astype(bf16)
            grad_v += dot_nn(p.astype(bf16), gh)
            grad_k += dot_nn(gs, qh)
            grad_q += dot_tn(gs, kh)
        gq_ref[0, :, cut] = (grad_q * scale_factor).astype(bf16)
        gpairs_ref[0, :, cut] = grad_k.astype(bf16)
        gpairs_ref[0, :, value_cut] = grad_v.astype(bf16)


def cross_backward(lengths, queries, pairs, out, lse, gout):
    micro, rows, width = queries.shape
    count = pairs.shape[1]
    groups = width // 128
    row_spec = pl.BlockSpec((1, rows, width), lambda m: (m, 0, 0))
    pair_spec = pl.BlockSpec((1, count, 2 * width), lambda m: (m, 0, 0))
    return pl.pallas_call(
        cross_backward_kernel,
        grid=(micro,),
        in_specs=[
            pl.BlockSpec(memory_space=pltpu.SMEM),
            row_spec,
            pair_spec,
            row_spec,
            pl.BlockSpec((1, groups, 2, rows), lambda m: (m, 0, 0, 0)),
            row_spec,
        ],
        out_specs=[row_spec, pair_spec],
        out_shape=[
            jax.ShapeDtypeStruct((micro, rows, width), bf16),
            jax.ShapeDtypeStruct((micro, count, 2 * width), bf16),
        ],
        compiler_params=pltpu.CompilerParams(vmem_limit_bytes=32 << 20),
        name="cross_backward",
    )(lengths, queries, pairs, out, lse, gout)


def ffn_backward_kernel(
    branch_ref, hidden_ref, active_ref, slope_ref, down_ref, up_ref,
    grad_down_ref, grad_up_ref, grad_hidden_ref, hidden_t,
):
    @pl.when(pl.program_id(0) == 0)
    def _():
        hidden_t[...] = jnp.transpose(hidden_ref[...].astype(f32)).astype(bf16)
        grad_hidden_ref[...] = jnp.zeros_like(grad_hidden_ref)

    branch = branch_ref[...]
    grad_active = dot_nt(branch, down_ref[...])
    grad_inner = (slope_ref[...].astype(f32) * grad_active).astype(bf16)
    grad_down_ref[...] = dot_tn(active_ref[...], branch).astype(bf16)
    grad_up_ref[...] = dot_nn(hidden_t[...], grad_inner).astype(bf16)
    grad_hidden_ref[...] += dot_nt(grad_inner, up_ref[...])


def ffn_backward(branch, hidden, active, slope, down_weight, upward_weight):
    rows, width = branch.shape
    inner = active.shape[1]
    piece = 512
    whole = pl.BlockSpec((rows, width), lambda i: (0, 0))
    across = pl.BlockSpec((rows, piece), lambda i: (0, i))
    down = pl.BlockSpec((piece, width), lambda i: (i, 0))
    up = pl.BlockSpec((width, piece), lambda i: (0, i))
    return pl.pallas_call(
        ffn_backward_kernel,
        grid=(inner // piece,),
        in_specs=[whole, whole, across, across, down, up],
        out_specs=[down, up, whole],
        out_shape=[
            jax.ShapeDtypeStruct((inner, width), bf16),
            jax.ShapeDtypeStruct((width, inner), bf16),
            jax.ShapeDtypeStruct((rows, width), f32),
        ],
        scratch_shapes=[pltpu.VMEM((width, rows), bf16)],
        compiler_params=pltpu.CompilerParams(vmem_limit_bytes=48 << 20),
        name="ffn_backward",
    )(branch, hidden, active, slope, down_weight, upward_weight)


def gelu_parts(v):
    inner = 0.7978845608028654 * (v + 0.044715 * (v * v * v))
    t = jnp.tanh(inner)
    value = 0.5 * v * (1.0 + t)
    slope = 0.5 * (1.0 + t) + 0.5 * v * (1.0 - t * t) * (
        0.7978845608028654 * (1.0 + 3.0 * 0.044715 * (v * v))
    )
    return value, slope


def per_device(
    tokens,
    memory,
    cotangent,
    tile_segment,
    parents,
    memory_lengths,
    self_qkv,
    self_out,
    cross_q,
    cross_kv,
    cross_out,
    ffn_in,
    ffn_out,
    norm_gain,
    norm_bias,
):
    micro, _, row_count, width = tokens.shape
    seq = lax.axis_size("seq")
    total_rows = micro * row_count
    memory_rows = memory.shape[2]

    devices = seq * lax.axis_size("fsdp")
    z_size, y_size = seq // 2, lax.axis_size("fsdp") // 2

    def flat(blocks):
        return blocks.reshape(-1, blocks.shape[-1])

    joint_weight = flat(gather_first([self_qkv], ("all",), ((0,),), z_size, y_size, 4)[0])

    x = tokens.reshape(total_rows, width)
    x32 = x.astype(f32)
    bias = jax.vmap(lambda t, p: tree_bias(t, p, BLOCK))(tile_segment[:, 0], parents[:, 0])
    lengths = memory_lengths[:, 0]

    projected = dot_nn(x, joint_weight).astype(bf16)
    gathered = self_forward(
        projected.reshape(micro, row_count, 3 * width),
        bias,
        seq,
        [
            self_out,
            jnp.concatenate([norm_gain, norm_bias], 0).astype(f32),
            cross_q,
            cross_kv,
            memory.reshape(micro * memory_rows, width),
            cross_out,
            ffn_in,
            ffn_out,
        ],
        ("all", "all", "all", "all", "seq", "all", "all", "all"),
        ((0, 1), (2, 4), (3,), (5,), (6,), (7,)),
        y_size,
    )
    qkv, attended_heads, self_lse, attended = gathered[:4]
    self_output, cross_weight, pair_weight = (flat(gathered[i]) for i in (4, 6, 7))
    cross_output, upward_weight, down_weight = (flat(gathered[i]) for i in (9, 10, 11))
    norms = gathered[5].reshape(devices, 6, width // devices).transpose(1, 0, 2).reshape(6, width)
    gain_rows, bias_rows = norms[:3], norms[3:]
    memory_full = gathered[8].reshape(seq, micro, memory_rows, width).transpose(1, 0, 2, 3)
    memory_full = memory_full.reshape(micro, seq * memory_rows, width)
    attended = attended.reshape(total_rows, width)

    mixed_first = residual_weight * x32 + dot_nn(attended, self_output)
    hidden_first = layer_norm(mixed_first, gain_rows[0], bias_rows[0])
    hidden_first_low = hidden_first.astype(bf16)
    cross_query = dot_nn(hidden_first_low, cross_weight).astype(bf16)
    cross_query = cross_query.reshape(micro, row_count, width)
    count = memory_full.shape[1]
    pairs = dot_nn(memory_full.reshape(micro * count, width), pair_weight).astype(bf16)
    pairs = pairs.reshape(micro, count, 2 * width)
    cross_heads, cross_lse = cross_forward(lengths, cross_query, pairs)
    cross_attended = cross_heads.reshape(total_rows, width)
    mixed_second = residual_weight * hidden_first + dot_nn(cross_attended, cross_output)
    hidden_second = layer_norm(mixed_second, gain_rows[1], bias_rows[1])
    hidden_second_low = hidden_second.astype(bf16)
    pre_active = dot_nn(hidden_second_low, upward_weight)
    active, slope = gelu_parts(pre_active)
    active, slope = lax.optimization_barrier((active.astype(bf16), slope.astype(bf16)))
    mixed_third = residual_weight * hidden_second + dot_nn(active, down_weight)
    output = layer_norm(mixed_third, gain_rows[2], bias_rows[2]).astype(bf16)

    upstream = cotangent.reshape(total_rows, width).astype(f32)
    grad_third, gain_third, bias_third = layer_norm_back(mixed_third, gain_rows[2], upstream)
    branch_third = grad_third.astype(bf16)
    grad_down, grad_upward, grad_hidden = ffn_backward(
        branch_third, hidden_second_low, active, slope, down_weight, upward_weight
    )
    grad_hidden_second = residual_weight * grad_third + grad_hidden
    grad_second, gain_second, bias_second = layer_norm_back(
        mixed_second, gain_rows[1], grad_hidden_second
    )
    branch_second = grad_second.astype(bf16)
    grad_cross_output = dot_tn(cross_attended, branch_second).astype(bf16)
    grad_cross_attended = dot_nt(branch_second, cross_output).astype(bf16)
    grad_cross_low, memory_partial = cross_backward(
        lengths,
        cross_query,
        pairs,
        cross_heads,
        cross_lse,
        grad_cross_attended.reshape(micro, row_count, width),
    )
    memory_partial = memory_partial.reshape(micro * count, 2 * width)
    memory_share = dot_nt(memory_partial, pair_weight).astype(bf16)
    memory_share = memory_share.reshape(micro, seq, memory_rows, width).transpose(1, 0, 2, 3)
    grad_pair_weight = dot_tn(memory_full.reshape(micro * count, width), memory_partial)
    grad_cross_low = grad_cross_low.reshape(total_rows, width)
    grad_cross_weight = dot_tn(hidden_first_low, grad_cross_low).astype(bf16)
    grad_hidden_first = residual_weight * grad_second + dot_nt(grad_cross_low, cross_weight)
    grad_first, gain_first, bias_first = layer_norm_back(
        mixed_first, gain_rows[0], grad_hidden_first
    )
    branch_first = grad_first.astype(bf16)
    grad_self_output = dot_tn(attended, branch_first).astype(bf16)
    grad_attended = dot_nt(branch_first, self_output).astype(bf16)
    grad_projected, own_upward, own_down, grad_memory = self_backward(
        grad_attended.reshape(micro, row_count, width),
        qkv,
        bias,
        attended_heads,
        self_lse,
        seq,
        [grad_upward, grad_down, memory_share.reshape(seq * micro * memory_rows, width)],
        (True, False, "seq"),
        y_size,
    )
    grad_projected = grad_projected.reshape(total_rows, 3 * width)
    grad_joint = dot_tn(x, grad_projected).astype(bf16)
    grad_tokens = (residual_weight * grad_first + dot_nt(grad_projected, joint_weight)).astype(bf16)
    norm_grads = jnp.stack(
        [gain_first, gain_second, gain_third, bias_first, bias_second, bias_third]
    )
    norm_blocks = norm_grads.reshape(6, devices, width // devices).transpose(1, 0, 2)
    owned = scatter_grads(
        [
            grad_joint,
            grad_self_output,
            grad_pair_weight.astype(bf16),
            grad_cross_weight,
            grad_cross_output,
            norm_blocks.reshape(6 * devices, width // devices),
        ],
        (True, True, False, False, False, False),
        z_size,
        y_size,
        3,
    )
    return (
        output.reshape(tokens.shape),
        grad_tokens.reshape(tokens.shape),
        grad_memory.astype(bf16).reshape(memory.shape),
        owned[0],
        owned[1],
        owned[3],
        owned[2],
        owned[4],
        own_upward,
        own_down,
        owned[5][:3],
        owned[5][3:],
    )


def solution(mesh):
    rows = P(None, "fsdp", "seq", None)
    weight = P(ALL, None)
    in_specs = (
        rows,
        rows,
        rows,
        P(None, "fsdp", None),
        P(None, "fsdp", None),
        P(None, "fsdp"),
    ) + (weight,) * 7 + (P(None, ALL),) * 2
    out_specs = (rows, rows, rows) + (weight,) * 7 + (P(None, ALL),) * 2
    return jax.shard_map(
        per_device, mesh=mesh, in_specs=in_specs, out_specs=out_specs, check_vma=False
    )
```
